512 devices in a mesh: region: 8 (over z_lo), sub: 64 (over x, y, z_hi, core).
Axes of the slice: x: 4, y: 4, z: 16 (z_hi: 2, z_lo: 8; z = z_hi * 8 + z_lo), core: 2. Of those that a mesh axis runs over, the one named last changes fastest.
Arguments:
- conn_x: int32 [2, 1048576], P(None, ('region', 'sub')), may hold values from 0 to 2175, as said below
- conn_y: int32 [2, 1048576], P(None, ('region', 'sub')), may hold values from 0 to 2559, as said below
- conn_z: int32 [2, 1048576], P(None, ('region', 'sub')), may hold values from 0 to 2111, as said below
- send_y: int32 [262144], P(('region', 'sub')), may hold values from 0 to 2047, as said below
- send_z: int32 [32768], P(('region', 'sub')), may hold values from 0 to 2047, as said below
- perm: float32 [2, 3, 1048576], P(None, None, ('region', 'sub')), may hold values from 0.1 to 10
- storage: float32 [2, 1048576], P(None, ('region', 'sub')), may hold values from 0.5 to 20
- sigma: float32 [1048576], P(('region', 'sub')), may hold values from 0.5 to 20
- source: float32 [2, 1048576], P(None, ('region', 'sub')), may hold values from -120 to 166
Outputs:
- trace: float32 [2, 3211264], P(None, ('region', 'sub'))
- pressure: float32 [2, 1048576], P(None, ('region', 'sub'))
- flux: float32 [2, 6, 1048576], P(None, None, ('region', 'sub'))
The draws below stay inside these ranges and needn't reach their ends.
Inputs may be any that keep to these rules, and one draw needn't show every extreme that they name: `conn_x`: each device's hexahedra form a block of 16 x 4 x 32, stored in a drawn order; its faces of each family are stored in a drawn order. Row 0 names the lower face along the first dimension, row 1 the upper. `conn_y`: values of 2048 and more name the block's lower-side faces, in the order of the lower device's send_y; the same owned face is named once as upper and at most once as lower. `conn_z`: values of 2048 and more name the block's lower-side faces, in the order of the lower device's send_z. `send_y`: distinct within a device: the block's upper-side faces along the second dimension. `send_z`: distinct within a device: the block's upper-side faces along the third dimension.
All inputs are finite; a program needn't handle non-finite values.
Results may differ from the reference program's by a relative error of at most 0.00013.
Values sent between devices are 32-bit elements; how exact they have to be, the bound alone decides.
A program may use at most 64 MiB of HBM per device.

```python
import math
import jax
import jax.numpy as jnp
from jax import lax

BX = 16
BY = 4
BZ = 32
ITERS = 3
E_DEV = 2048
NXF = 2176
NYF = 2048
NZF = 2048
GHOST_Y = 512
GHOST_Z = 64
NDEV = 512
ELEMENTS = 1048576
N_REGION = 8
N_SUB = 64


def layout(key):

    def one_device(device_key):
        cell_key, key_x, key_y, key_z = jax.random.split(device_key, 4)
        cell_of = jax.random.permutation(cell_key, E_DEV)
        place_x = jax.random.permutation(key_x, NXF)
        place_y = jax.random.permutation(key_y, NYF)
        place_z = jax.random.permutation(key_z, NZF)
        column = cell_of // (BY * BZ)
        row = cell_of // BZ % BY
        level = cell_of % BZ
        conn_x = jnp.stack([place_x[(column * BY + row) * BZ + level], place_x[((column + 1) * BY + row) * BZ + level]])
        lower_y = jnp.where(row == 0, NYF + column * BZ + level, place_y[(column * BY + jnp.maximum(row - 1, 0)) * BZ + level])
        upper_y = place_y[(column * BY + row) * BZ + level]
        lower_z = jnp.where(level == 0, NZF + column * BY + row, place_z[(column * BY + row) * BZ + jnp.maximum(level - 1, 0)])
        upper_z = place_z[(column * BY + row) * BZ + level]
        across_y = jnp.arange(BX * BZ)
        send_y = place_y[(across_y // BZ * BY + BY - 1) * BZ + across_y % BZ]
        across_z = jnp.arange(BX * BY)
        send_z = place_z[across_z * BZ + BZ - 1]
        return (conn_x, jnp.stack([lower_y, upper_y]), jnp.stack([lower_z, upper_z]), send_y, send_z)
    keys = jax.random.split(key, NDEV)
    conn_x, conn_y, conn_z, send_y, send_z = jax.vmap(one_device)(keys)

    def flat(array):
        return jnp.moveaxis(array, 0, 1).reshape(2, -1).astype(jnp.int32)
    return (flat(conn_x), flat(conn_y), flat(conn_z), send_y.reshape(-1).astype(jnp.int32), send_z.reshape(-1).astype(jnp.int32))


def draw_conn_x(key, part):
    shared = layout(key)
    return shared[0]


def draw_conn_y(key, part):
    shared = layout(key)
    return shared[1]


def draw_conn_z(key, part):
    shared = layout(key)
    return shared[2]


def draw_send_y(key, part):
    shared = layout(key)
    return shared[3]


def draw_send_z(key, part):
    shared = layout(key)
    return shared[4]


def draw_source(key, part):
    key = jax.random.fold_in(key, 7)
    column = lax.broadcasted_iota(jnp.int32, (2, ELEMENTS), 1)
    place = (column // E_DEV).astype(jnp.float32) / max(NDEV - 1, 1)
    rough = jnp.clip(jax.random.normal(key, (2, ELEMENTS), jnp.float32), -5.0, 5.0)
    return (8.0 * (1.0 + 2.0 * place) * rough).astype(jnp.float32)


def block_levels(stream_key, shape, cuts, low, top_value):
    gain, own = 1.0, jax.random.fold_in(stream_key, 6)
    for dim, blocks in cuts:
        heights = jnp.exp(jax.random.uniform(jax.random.fold_in(own, dim), (blocks,), jnp.float32, low / len(cuts), top_value / len(cuts)))
        gain = gain * jnp.repeat(heights, shape[dim] // blocks).reshape([-1 if axis == dim else 1 for axis in range(len(shape))])
    return gain


def setup_inputs(seed: int = 0) -> dict:
    key_of = jax.random.split(jax.random.key(seed), 10)
    return {
        "conn_x": draw_conn_x(jax.random.fold_in(key_of[9], 71), 0),
        "conn_y": draw_conn_y(jax.random.fold_in(key_of[9], 71), 0),
        "conn_z": draw_conn_z(jax.random.fold_in(key_of[9], 71), 0),
        "send_y": draw_send_y(jax.random.fold_in(key_of[9], 71), 0),
        "send_z": draw_send_z(jax.random.fold_in(key_of[9], 71), 0),
        "perm": jnp.clip(jnp.exp(math.log(10.0) - 4.6051702 * jax.random.uniform(key_of[5], (2, 3, ELEMENTS), jnp.float32) ** block_levels(key_of[5], (2, 3, ELEMENTS), ((2, 512),), -0.2, 0.2)), 0.1, 10.0),
        "storage": jnp.clip(jnp.exp(math.log(20.0) - 3.6888795 * jax.random.uniform(key_of[6], (2, ELEMENTS), jnp.float32) ** block_levels(key_of[6], (2, ELEMENTS), ((1, 512),), -0.2, 0.2)), 0.5, 20.0),
        "sigma": jnp.clip(jnp.exp(math.log(20.0) - 3.6888795 * jax.random.uniform(key_of[7], (ELEMENTS,), jnp.float32) ** block_levels(key_of[7], (ELEMENTS,), ((0, 512),), -0.2, 0.2)), 0.5, 20.0),
        "source": draw_source(jax.random.fold_in(key_of[9], 71), 0),
    }


def element_terms(perm, storage, sigma):
    trans = 2.0 * perm
    total = 2.0 * jnp.sum(trans, axis=1)
    diag_a = total[0] + storage[0] + sigma
    diag_b = total[1] + storage[1] + sigma
    return trans, diag_a, diag_b, diag_a * diag_b - sigma * sigma


def solve_pair(load, sigma, diag_a, diag_b, determ):
    first = (diag_b * load[0] + sigma * load[1]) / determ
    second = (sigma * load[0] + diag_a * load[1]) / determ
    return jnp.stack([first, second])


def face_load(values, trans):
    return sum(trans[:, side] * (values[side][:, 0] + values[side][:, 1]) for side in range(3))


def reference(conn_x, conn_y, conn_z, send_y, send_z, perm, storage, sigma, source):
    def split(array):
        return array.reshape(array.shape[:-1] + (NDEV, -1))

    conns = (split(conn_x), split(conn_y), split(conn_z))
    lists = (split(send_y), split(send_z))
    trans, diag_a, diag_b, determ = element_terms(split(perm), split(storage), split(sigma))
    sigma_dev = split(sigma)
    anchor = split(source)
    counts = (NXF, NYF + GHOST_Y, NZF + GHOST_Z)

    gather_faces = jax.vmap(lambda vector, index: jnp.take(vector, index, axis=1), in_axes=(1, 1), out_axes=2)
    pick_rows = jax.vmap(lambda vector, index: vector[:, index], in_axes=(1, 0), out_axes=1)
    add_rows = jax.vmap(lambda vector, index, extra: vector.at[:, index].add(extra), in_axes=(1, 0, 1), out_axes=1)

    def deposit(values, index, count):
        return jax.vmap(lambda part, where: jnp.zeros((2, count), jnp.float32).at[:, where].add(part), in_axes=(2, 1), out_axes=1)(values, index)

    def shifted(values, axis, upward):
        grid = values.reshape(2, N_REGION, N_SUB, values.shape[-1])
        length = grid.shape[axis]
        padding = [(0, 0), (0, 0), (0, 0), (0, 0)]
        if upward:
            padding[axis] = (1, 0)
            grid = lax.slice_in_dim(jnp.pad(grid, padding), 0, length, axis=axis)
        else:
            padding[axis] = (0, 1)
            grid = lax.slice_in_dim(jnp.pad(grid, padding), 1, length + 1, axis=axis)
        return grid.reshape(values.shape)

    def extend(vector):
        face_x, face_y, face_z = vector
        under_y = shifted(pick_rows(face_y, lists[0]), 2, True)
        under_z = shifted(pick_rows(face_z, lists[1]), 1, True)
        return face_x, jnp.concatenate([face_y, under_y], axis=2), jnp.concatenate([face_z, under_z], axis=2)

    def settle(parts):
        part_x, part_y, part_z = parts
        total_y = add_rows(part_y[:, :, :NYF], lists[0], shifted(part_y[:, :, NYF:], 2, False))
        total_z = add_rows(part_z[:, :, :NZF], lists[1], shifted(part_z[:, :, NZF:], 1, False))
        return part_x, total_y, total_z

    def pairs(load):
        return solve_pair(load, sigma_dev, diag_a, diag_b, determ)

    def faces(extended):
        return tuple(gather_faces(extended[side], conns[side]) for side in range(3))

    def operate(vector):
        values = faces(extend(vector))
        solved = pairs(face_load(values, trans))
        return settle(tuple(deposit(trans[:, side][:, None] * (values[side] - solved[:, None]), conns[side], counts[side]) for side in range(3)))

    def inner(first, second):
        return sum(jnp.sum(first[side] * second[side]) for side in range(3))

    def blend(first, factor, second):
        return tuple(a + factor * b for a, b in zip(first, second))

    base = pairs(anchor)
    shape = (2, 2) + base.shape[1:]
    rhs = settle(tuple(deposit(jnp.broadcast_to((trans[:, side] * base)[:, None], shape), conns[side], counts[side]) for side in range(3)))
    trace = tuple(jnp.zeros_like(part) for part in rhs)
    resid = rhs
    direction = rhs
    norm_now = inner(resid, resid)
    for step in range(ITERS):
        image = operate(direction)
        alpha = norm_now / inner(direction, image)
        trace = blend(trace, alpha, direction)
        resid = blend(resid, -alpha, image)
        norm_next = inner(resid, resid)
        direction = blend(resid, norm_next / norm_now, direction)
        norm_now = norm_next
    values = faces(extend(trace))
    pressure = pairs(anchor + face_load(values, trans))
    flux = jnp.concatenate([trans[:, side][:, None] * (pressure[:, None] - values[side]) for side in range(3)], axis=1)
    trace_out = jnp.concatenate([trace[0], trace[1], trace[2]], axis=2).reshape(2, -1)
    return trace_out, pressure.reshape(2, -1), flux.reshape(2, 6, -1)
```

```python
import functools

import jax
import jax.numpy as jnp
from jax import lax
from jax.experimental import pallas as pl
from jax.experimental.pallas import tpu as pltpu
from jax.sharding import PartitionSpec as P

MESH = pl.DeviceIdType.MESH
F32 = jnp.float32
I32 = jnp.int32
ROWS = 16
LANES = 128
E_DEV = ROWS * LANES
NXF = 2176
ROUNDS = 3


def iota(shape, dim):
    return lax.broadcasted_iota(I32, shape, dim)


def inverse(pieces):
    total = None
    for ref, row, columns, first in pieces:
        step = min(256, columns)
        for start in range(0, columns, step):
            face = ref[row : row + 1, start : start + step]
            cell = iota((1, step), 1) + (first + start)
            spot = jnp.where(iota((LANES, step), 0) == (face & 127), 1.0, 0.0).astype(jnp.bfloat16)
            hit = iota((24, step), 0) == (face >> 7)
            low = jnp.where(hit, (cell & 127).astype(F32), 0.0)
            high = jnp.where(hit, ((cell >> 7) + 1).astype(F32), 0.0)
            left = jnp.concatenate([low, high], axis=0).astype(jnp.bfloat16)
            part = lax.dot_general(left, spot, (((1,), (1,)), ((), ())), preferred_element_type=F32)
            total = part if total is None else total + part
    whole = total.astype(I32)
    return (whole[24:] - 1) * 128 + whole[:24]


def lane_gather(rows, lane):
    numbers = lax.GatherDimensionNumbers(
        offset_dims=(),
        collapsed_slice_dims=(1,),
        start_index_map=(1,),
        operand_batching_dims=(0,),
        start_indices_batching_dims=(0,),
    )
    return lax.gather(
        rows, lane[..., None], numbers, (1, 1), mode=lax.GatherScatterMode.PROMISE_IN_BOUNDS
    )


def lookup(rows, index, start=None):
    lane, high = index & 127, index >> 7
    out = start
    for number, row in rows:
        wide = jnp.broadcast_to(row, index.shape)
        found = lane_gather(wide, lane)
        out = jnp.where(high == number, found, jnp.zeros_like(found) if out is None else out)
    return out


def table(ref, count=ROWS, first=0):
    return [(first + h, ref[h : h + 1, :]) for h in range(count)]


def total_row(parts):
    lane = iota((1, LANES), 1)
    row = jnp.zeros((1, LANES), F32)
    for number, part in enumerate(parts):
        flat = jnp.sum(part, axis=0, keepdims=True)
        row = jnp.where(lane == number, jnp.sum(flat, axis=1, keepdims=True), row)
    return row


def pick(row, number):
    return jnp.sum(jnp.where(iota((1, LANES), 1) == number, row, 0.0), axis=1, keepdims=True)


def kernel(
    n_region, n_sub,
    conn_x, conn_y, conn_z, send_y, send_z, perm, storage, sigma_ref, source,
    trace_out, pressure_out, flux_out,
    stage, istage, zlist, itable, tables,
    y_send, y_recv, z_send, z_recv, halo_send_sem, halo_recv_sem,
    a_send, a_recv, b_send, b_recv, a_send_sem, a_recv_sem, b_send_sem, b_recv_sem,
):
    region, sub = lax.axis_index("region"), lax.axis_index("sub")
    n_flat, n_deep = n_sub // 2, 2 * n_region
    core, deep = lax.rem(sub, 2), lax.rem(lax.div(sub, 2), 2)
    flat_me = lax.div(sub, 4) * 2 + core
    deep_me = deep * n_region + region
    sub_up, sub_down = lax.rem(sub + 1, n_sub), lax.rem(sub + n_sub - 1, n_sub)
    region_up, region_down = lax.rem(region + 1, n_region), lax.rem(region + n_region - 1, n_region)

    def flat_peer(offset):
        peer = lax.rem(flat_me + offset, n_flat)
        return (region, lax.div(peer, 2) * 4 + deep * 2 + lax.rem(peer, 2))

    def deep_peer(offset):
        peer = lax.rem(deep_me + offset, n_deep)
        return (lax.rem(peer, n_region), sub - deep * 2 + lax.div(peer, n_region) * 2)

    barrier = pltpu.get_barrier_semaphore()

    def greet(device):
        pl.semaphore_signal(barrier, inc=1, device_id=device, device_id_type=MESH)

    greet((region, sub_up))
    greet((region, sub_down))
    lax.fori_loop(1, n_flat, lambda j, c: (greet(flat_peer(j)), c)[1], 0)
    lax.fori_loop(1, n_deep, lambda j, c: (greet(deep_peer(j)), c)[1], 0)

    def unpack(ref, count, base):
        for i in range(ROWS):
            base[count * i : count * (i + 1), :] = ref(i)
        return [base[pl.ds(k, ROWS, stride=count), :] for k in range(count)]

    def lanes(i):
        return slice(LANES * i, LANES * (i + 1))

    faces_x = unpack(lambda i: conn_x[:, lanes(i)], 2, istage.at[0])
    faces_y = unpack(lambda i: conn_y[:, lanes(i)], 2, istage.at[1])
    faces_z = unpack(lambda i: conn_z[:, lanes(i)], 2, istage.at[2])
    trans = []
    for c in range(2):
        trans.append([2.0 * t for t in unpack(lambda i: perm[c, :, lanes(i)], 3, stage.at[c])])
    store = unpack(lambda i: storage[:, lanes(i)], 2, stage.at[2])
    origin = unpack(lambda i: source[:, lanes(i)], 2, stage.at[3])
    sigma = sigma_ref[...]

    zlist[0:1, :] = jnp.full((1, LANES), -1, I32)
    zlist[0:1, 0:64] = send_z[...]
    itable[0] = inverse([(conn_x, 0, E_DEV, 0)])
    itable[1] = inverse([(conn_x, 1, E_DEV, 0)])
    itable[2] = inverse([(conn_y, 0, E_DEV, 0), (send_y, 0, 512, E_DEV)])
    itable[3] = inverse([(conn_y, 1, E_DEV, 0)])
    itable[4] = inverse([(conn_z, 0, E_DEV, 0), (zlist, 0, LANES, E_DEV)])
    itable[5] = inverse([(conn_z, 1, E_DEV, 0)])

    def at_face(which, face, count=ROWS):
        return lookup(table(itable.at[which], count), face, jnp.full(face.shape, -1, I32))

    def own(which, face):
        return jnp.where(face >= E_DEV, face, at_face(which, face))

    up = [at_face(0, faces_x[1], 17), at_face(2, faces_y[1]), at_face(4, faces_z[1])]
    down = [at_face(1, faces_x[0], 17), own(3, faces_y[0]), own(5, faces_z[0])]
    last_y, last_z = sub == n_sub - 1, region == n_region - 1
    up[1] = jnp.where(jnp.logical_and(up[1] >= E_DEV, last_y), -1, up[1])
    up[2] = jnp.where(jnp.logical_and(up[2] >= E_DEV, last_z), -1, up[2])
    first_y = jnp.logical_and(down[1] >= E_DEV, sub == 0)
    first_z = jnp.logical_and(down[2] >= E_DEV, region == 0)
    lone_x = down[0] < 0
    for i in range(4):
        istage[3, i : i + 1, :] = send_y[:, lanes(i)]
    up_y_cells = at_face(3, istage[3, 0:4, :])
    down_y_cells = itable[2, ROWS : ROWS + 4, :]
    up_z_cells = at_face(5, zlist[0:1, :])
    down_z_cells = itable[4, ROWS : ROWS + 1, :]

    diag = [2.0 * (trans[c][0] + trans[c][1] + trans[c][2]) + store[c] + sigma for c in range(2)]
    determ = diag[0] * diag[1] - sigma * sigma
    solve_00, solve_01, solve_11 = diag[1] / determ, sigma / determ, diag[0] / determ

    def solve(load):
        return (solve_00 * load[0] + solve_01 * load[1], solve_01 * load[0] + solve_11 * load[1])

    def face_load(v):
        return [
            sum(trans[c][d] * (v[c][d][0] + v[c][d][1]) for d in range(3)) for c in range(2)
        ]

    def contributions(v, inner):
        return [
            [[trans[c][d] * (v[c][d][s] - inner[c]) for s in range(2)] for d in range(3)]
            for c in range(2)
        ]

    def copies(step):
        def one(kind, send, recv, device):
            return pltpu.make_async_remote_copy(
                src_ref=send,
                dst_ref=recv,
                send_sem=halo_send_sem.at[step, kind],
                recv_sem=halo_recv_sem.at[step, kind],
                device_id=device,
                device_id_type=MESH,
            )

        return [
            one(0, y_send.at[step, 0], y_recv.at[step, 0], (region, sub_up)),
            one(1, y_send.at[step, 1], y_recv.at[step, 1], (region, sub_down)),
            one(2, z_send.at[step, 0], z_recv.at[step, 0], (region_up, sub)),
            one(3, z_send.at[step, 1], z_recv.at[step, 1], (region_down, sub)),
        ]

    def publish(step, g, wait_first=None):
        for c in range(2):
            for d in range(3):
                for s in range(2):
                    tables[c * 6 + d * 2 + s] = g[c][d][s]
        for c in range(2):
            here = 4 * c
            y_send[step, 0, here : here + 4, :] = lookup(table(tables.at[c * 6 + 3]), up_y_cells)
            y_send[step, 1, here : here + 4, :] = lookup(table(tables.at[c * 6 + 2]), down_y_cells)
            z_send[step, 0, c : c + 1, :] = lookup(table(tables.at[c * 6 + 5]), up_z_cells)
            z_send[step, 1, c : c + 1, :] = lookup(table(tables.at[c * 6 + 4]), down_z_cells)
        if wait_first is not None:
            wait_first()
        for copy in copies(step):
            copy.start()

    def assemble(step, g):
        out = [[[None, None] for _ in range(3)] for _ in range(2)]
        for c in range(2):
            for d in range(3):
                base = c * 6 + d * 2
                out[c][d][1] = g[c][d][1] + lookup(table(tables.at[base]), up[d])
                out[c][d][0] = g[c][d][0] + lookup(table(tables.at[base + 1]), down[d])
        for copy in copies(step):
            copy.wait_recv()
        for c in range(2):
            from_below_y = table(y_recv.at[step, 0, pl.ds(4 * c, 4)], 4, ROWS)
            from_above_y = table(y_recv.at[step, 1, pl.ds(4 * c, 4)], 4, ROWS)
            from_below_z = table(z_recv.at[step, 0, pl.ds(c, 1)], 1, ROWS)
            from_above_z = table(z_recv.at[step, 1, pl.ds(c, 1)], 1, ROWS)
            out[c][1][1] = out[c][1][1] + lookup(from_above_y, up[1])
            out[c][2][1] = out[c][2][1] + lookup(from_above_z, up[2])
            out[c][1][0] = jnp.where(first_y, 0.0, out[c][1][0] + lookup(from_below_y, down[1]))
            out[c][2][0] = jnp.where(first_z, 0.0, out[c][2][0] + lookup(from_below_z, down[2]))
        return out

    def inner(u, v):
        total = sum(u[c][d][1] * v[c][d][1] for c in range(2) for d in range(3))
        edge = sum(u[c][0][0] * v[c][0][0] for c in range(2))
        return total + jnp.where(lone_x, edge, 0.0)

    def energy(v, load, solved):
        total = sum(
            trans[c][d] * (v[c][d][0] * v[c][d][0] + v[c][d][1] * v[c][d][1])
            for c in range(2)
            for d in range(3)
        )
        return total - (load[0] * solved[0] + load[1] * solved[1])

    def scatter(send, recv, send_sem, recv_sem, peer, count, row):
        send[0:1, :] = row
        recv[count - 1 : count, :] = row

        def one(j, carry):
            pltpu.make_async_remote_copy(
                src_ref=send.at[pl.ds(0, 1)],
                dst_ref=recv.at[pl.ds(j - 1, 1)],
                send_sem=send_sem,
                recv_sem=recv_sem,
                device_id=peer(j),
                device_id_type=MESH,
            ).start()
            return carry

        lax.fori_loop(1, count, one, 0)

    def drain(buffer, sem, count):
        rows = buffer.at[pl.ds(0, count - 1)]
        pltpu.make_async_copy(rows, rows, sem).wait()

    def flat_start(k, row):
        scatter(a_send.at[k], a_recv.at[k], a_send_sem.at[k], a_recv_sem.at[k], flat_peer, n_flat, row)

    def flat_done(k):
        drain(a_recv.at[k], a_recv_sem.at[k], n_flat)
        return jnp.sum(a_recv[k], axis=0, keepdims=True)

    def deep_start(k, row):
        scatter(b_send.at[k], b_recv.at[k], b_send_sem.at[k], b_recv_sem.at[k], deep_peer, n_deep, row)

    def deep_done(k):
        drain(b_recv.at[k], b_recv_sem.at[k], n_deep)
        return jnp.sum(b_recv[k], axis=0, keepdims=True)

    base = solve(origin)
    g = [[[trans[c][d] * base[c]] * 2 for d in range(3)] for c in range(2)]
    greetings = 2 + (n_flat - 1) + (n_deep - 1)
    publish(0, g, lambda: pl.semaphore_wait(barrier, greetings))
    b = assemble(0, g)

    load = face_load(b)
    solved = solve(load)
    g = contributions(b, solved)
    publish(1, g)
    flat_start(0, total_row([inner(b, b), energy(b, load, solved)]))
    w = assemble(1, g)

    g = contributions(w, solve(face_load(w)))
    publish(2, g)
    deep_start(0, flat_done(0))
    ww = assemble(2, g)

    first = deep_done(0)
    norm_0 = pick(first, 0)
    alpha_0 = norm_0 / pick(first, 1)

    def blend(u, factor, v):
        return [
            [[u[c][d][s] - factor * v[c][d][s] for s in range(2)] for d in range(3)]
            for c in range(2)
        ]

    r = blend(b, alpha_0, w)
    s = blend(w, alpha_0, ww)
    load = face_load(s)
    flat_start(1, total_row([inner(r, r), inner(r, s), inner(s, s), energy(s, load, solve(load))]))
    deep_start(1, flat_done(1))
    sums = deep_done(1)
    rr, rs, ss, sas = (pick(sums, k) for k in range(4))

    beta_0 = rr / norm_0
    alpha_1 = rr / (rs - beta_0 * rr / alpha_0)
    ws = -(rr / alpha_0 + rs) / alpha_0
    norm_2 = -alpha_1 * (rs - alpha_1 * ss - alpha_1 * beta_0 * ws)
    beta_1 = norm_2 / rr
    ratio = alpha_1 * beta_0 / alpha_0
    along = ss - alpha_1 * sas - ratio * (ws - ss)
    energy_2 = -norm_2 / alpha_1 * (1.0 + ratio) - alpha_1 * along
    alpha_2 = norm_2 / (energy_2 - beta_1 * norm_2 / alpha_1)
    on_b = alpha_0 + alpha_1 * beta_0 + alpha_2 * beta_1 * beta_0
    on_r = alpha_1 + alpha_2 * (1.0 + beta_1)
    on_s = -alpha_2 * alpha_1
    on_w = -alpha_2 * alpha_1 * beta_0
    trace = [
        [
            [
                on_b * b[c][d][k] + on_r * r[c][d][k] + on_s * s[c][d][k] + on_w * w[c][d][k]
                for k in range(2)
            ]
            for d in range(3)
        ]
        for c in range(2)
    ]

    load = face_load(trace)
    pressure = solve([origin[c] + load[c] for c in range(2)])
    for c in range(2):
        stage[0, pl.ds(c, ROWS, stride=2), :] = pressure[c]
    for i in range(ROWS):
        pressure_out[:, lanes(i)] = stage[0, 2 * i : 2 * i + 2, :]
    for c in range(2):
        for d in range(3):
            for k in range(2):
                flux = trans[c][d] * (pressure[c] - trace[c][d][k])
                stage[1 + c, pl.ds(2 * d + k, ROWS, stride=8), :] = flux
        for i in range(ROWS):
            flux_out[c, :, lanes(i)] = stage[1 + c, 8 * i : 8 * i + 6, :]

    for c in range(2):
        for d in range(3):
            for k in range(2):
                tables[c * 6 + d * 2 + k] = trace[c][d][k]
        by_x = lookup(table(tables.at[c * 6 + 1]), itable[1])
        by_x = jnp.where(itable[1] < 0, lookup(table(tables.at[c * 6]), itable[0]), by_x)
        by_y = lookup(table(tables.at[c * 6 + 3]), itable[3, 0:ROWS, :])
        by_z = lookup(table(tables.at[c * 6 + 5]), itable[5, 0:ROWS, :])
        stage[3, pl.ds(c, 17, stride=2), :] = by_x[0:17]
        stage[3, pl.ds(34 + c, ROWS, stride=2), :] = by_y
        stage[3, pl.ds(66 + c, ROWS, stride=2), :] = by_z
    for i in range(49):
        trace_out[:, lanes(i)] = stage[3, 2 * i : 2 * i + 2, :]

    for step in range(ROUNDS):
        for copy in copies(step):
            copy.wait_send()
    for k in range(2):
        drain(a_recv.at[k], a_send_sem.at[k], n_flat)
        drain(b_recv.at[k], b_send_sem.at[k], n_deep)


def solution(mesh):
    n_region, n_sub = mesh.shape["region"], mesh.shape["sub"]
    n_flat, n_deep = n_sub // 2, 2 * n_region

    def local(conn_x, conn_y, conn_z, send_y, send_z, perm, storage, sigma, source):
        vmem = pl.BlockSpec(memory_space=pltpu.VMEM)
        dma = pltpu.SemaphoreType.DMA
        return pl.pallas_call(
            functools.partial(kernel, n_region, n_sub),
            out_shape=(
                jax.ShapeDtypeStruct((2, NXF + 2 * E_DEV), F32),
                jax.ShapeDtypeStruct((2, E_DEV), F32),
                jax.ShapeDtypeStruct((2, 6, E_DEV), F32),
            ),
            in_specs=[vmem] * 9,
            out_specs=(vmem,) * 3,
            scratch_shapes=[
                pltpu.VMEM((4, LANES + 8, LANES), F32),
                pltpu.VMEM((4, 40, LANES), I32),
                pltpu.VMEM((8, LANES), I32),
                pltpu.VMEM((6, 24, LANES), I32),
                pltpu.VMEM((12, ROWS, LANES), F32),
                pltpu.VMEM((ROUNDS, 2, 8, LANES), F32),
                pltpu.VMEM((ROUNDS, 2, 8, LANES), F32),
                pltpu.VMEM((ROUNDS, 2, 2, LANES), F32),
                pltpu.VMEM((ROUNDS, 2, 2, LANES), F32),
                dma((ROUNDS, 4)),
                dma((ROUNDS, 4)),
                pltpu.VMEM((2, 8, LANES), F32),
                pltpu.VMEM((2, n_flat, LANES), F32),
                pltpu.VMEM((2, 8, LANES), F32),
                pltpu.VMEM((2, n_deep, LANES), F32),
                dma((2,)),
                dma((2,)),
                dma((2,)),
                dma((2,)),
            ],
            compiler_params=pltpu.CompilerParams(
                collective_id=0, has_side_effects=True, vmem_limit_bytes=32 * 1024 * 1024
            ),
        )(
            conn_x, conn_y, conn_z, send_y.reshape(1, 512), send_z.reshape(1, 64),
            perm, storage, sigma.reshape(ROWS, LANES), source,
        )

    both = ("region", "sub")
    return jax.shard_map(
        local,
        mesh=mesh,
        in_specs=(
            P(None, both), P(None, both), P(None, both), P(both), P(both),
            P(None, None, both), P(None, both), P(both), P(None, both),
        ),
        out_specs=(P(None, both), P(None, both), P(None, None, both)),
        check_vma=False,
    )
```

```python
import functools

import jax
import jax.numpy as jnp
from jax import lax
from jax.experimental import pallas as pl
from jax.experimental.pallas import tpu as pltpu
from jax.sharding import PartitionSpec as P

MESH = pl.DeviceIdType.MESH
F32 = jnp.float32
I32 = jnp.int32
ROWS = 16
LANES = 128
E_DEV = ROWS * LANES
NXF = 2176
ROUNDS = 3


def iota(shape, dim):
    return lax.broadcasted_iota(I32, shape, dim)


def inverse(pieces):
    total = None
    for ref, row, stride, count, first in pieces:
        for start in range(0, count, 2):
            spots, hits = [], []
            for i in range(start, min(start + 2, count)):
                face = ref[row + stride * i : row + stride * i + 1, :]
                cell = iota((1, LANES), 1) + (first + LANES * i)
                spots.append(jnp.where(iota((LANES, LANES), 0) == (face & 127), 1.0, 0.0))
                hit = iota((24, LANES), 0) == (face >> 7)
                low = jnp.where(hit, (cell & 127).astype(F32), 0.0)
                high = jnp.where(hit, ((cell >> 7) + 1).astype(F32), 0.0)
                hits.append(jnp.concatenate([low, high], axis=0))
            left = jnp.concatenate(hits, axis=1).astype(jnp.bfloat16)
            spot = jnp.concatenate(spots, axis=1).astype(jnp.bfloat16)
            part = lax.dot_general(left, spot, (((1,), (1,)), ((), ())), preferred_element_type=F32)
            total = part if total is None else total + part
    whole = total.astype(I32)
    return (whole[24:] - 1) * 128 + whole[:24]


def lane_gather(rows, lane):
    numbers = lax.GatherDimensionNumbers(
        offset_dims=(),
        collapsed_slice_dims=(1,),
        start_index_map=(1,),
        operand_batching_dims=(0,),
        start_indices_batching_dims=(0,),
    )
    return lax.gather(
        rows, lane[..., None], numbers, (1, 1), mode=lax.GatherScatterMode.PROMISE_IN_BOUNDS
    )


def lookup(rows, index, start=None):
    lane, high = index & 127, index >> 7
    out = start
    for number, row in rows:
        wide = jnp.broadcast_to(row, index.shape)
        found = lane_gather(wide, lane)
        out = jnp.where(high == number, found, jnp.zeros_like(found) if out is None else out)
    return out


def table(ref, count=ROWS, first=0):
    return [(first + h, ref[h : h + 1, :]) for h in range(count)]


def total_row(parts):
    lane = iota((1, LANES), 1)
    row = jnp.zeros((1, LANES), F32)
    for number, part in enumerate(parts):
        flat = jnp.sum(part, axis=0, keepdims=True)
        row = jnp.where(lane == number, jnp.sum(flat, axis=1, keepdims=True), row)
    return row


def pick(row, number):
    return jnp.sum(jnp.where(iota((1, LANES), 1) == number, row, 0.0), axis=1, keepdims=True)


def kernel(
    n_region, n_sub,
    conn_x, conn_y, conn_z, send_y, send_z, perm, storage, sigma_ref, source,
    trace_out, pressure_out, flux_out,
    zlist, itable, tables, vtables, by_face,
    y_send, y_recv, z_send, z_recv, halo_send_sem, halo_recv_sem,
    a_send, a_recv, b_send, b_recv, a_send_sem, a_recv_sem, b_send_sem, b_recv_sem,
):
    region, sub = lax.axis_index("region"), lax.axis_index("sub")
    n_flat, n_deep = n_sub // 2, 2 * n_region
    core, deep = lax.rem(sub, 2), lax.rem(lax.div(sub, 2), 2)
    flat_me = lax.div(sub, 4) * 2 + core
    deep_me = deep * n_region + region
    sub_up, sub_down = lax.rem(sub + 1, n_sub), lax.rem(sub + n_sub - 1, n_sub)
    region_up, region_down = lax.rem(region + 1, n_region), lax.rem(region + n_region - 1, n_region)

    def flat_peer(offset):
        peer = lax.rem(flat_me + offset, n_flat)
        return (region, lax.div(peer, 2) * 4 + deep * 2 + lax.rem(peer, 2))

    def deep_peer(offset):
        peer = lax.rem(deep_me + offset, n_deep)
        return (lax.rem(peer, n_region), sub - deep * 2 + lax.div(peer, n_region) * 2)

    barrier = pltpu.get_barrier_semaphore()

    def greet(device):
        pl.semaphore_signal(barrier, inc=1, device_id=device, device_id_type=MESH)

    greet((region, sub_up))
    greet((region, sub_down))
    for j in range(1, n_flat):
        greet(flat_peer(j))
    for j in range(1, n_deep):
        greet(deep_peer(j))

    def pair(ref, first=0):
        return [ref[pl.ds(first + k, ROWS, stride=2), :] for k in range(2)]

    by_side = [pair(perm, 32 * d) for d in range(3)]
    trans = [[2.0 * by_side[d][c] for d in range(3)] for c in range(2)]
    store, origin, sigma = pair(storage), pair(source), sigma_ref[...]

    diag = [2.0 * (trans[c][0] + trans[c][1] + trans[c][2]) + store[c] + sigma for c in range(2)]
    determ = diag[0] * diag[1] - sigma * sigma
    solve_00, solve_01, solve_11 = diag[1] / determ, sigma / determ, diag[0] / determ

    def solve(load):
        return (solve_00 * load[0] + solve_01 * load[1], solve_01 * load[0] + solve_11 * load[1])

    def face_load(v):
        return [
            sum(trans[c][d] * (v[c][d][0] + v[c][d][1]) for d in range(3)) for c in range(2)
        ]

    def contributions(v, inner):
        return [
            [[trans[c][d] * (v[c][d][s] - inner[c]) for s in range(2)] for d in range(3)]
            for c in range(2)
        ]

    base = solve(origin)
    rhs_g = [[[trans[c][d] * base[c]] * 2 for d in range(3)] for c in range(2)]

    def at_face(which, face, count=ROWS):
        return lookup(table(itable.at[which], count), face, jnp.full(face.shape, -1, I32))

    def own(which, face):
        return jnp.where(face >= E_DEV, face, at_face(which, face))

    zlist[0:1, :] = jnp.full((1, LANES), -1, I32)
    zlist[0:1, 0:64] = send_z[...]
    itable[2] = inverse([(conn_y, 0, 2, ROWS, 0), (send_y, 0, 1, 4, E_DEV)])
    itable[3] = inverse([(conn_y, 1, 2, ROWS, 0)])
    itable[4] = inverse([(conn_z, 0, 2, ROWS, 0), (zlist, 0, 1, 1, E_DEV)])
    itable[5] = inverse([(conn_z, 1, 2, ROWS, 0)])
    up_y_cells = at_face(3, send_y[...])
    down_y_cells = itable[2, ROWS : ROWS + 4, :]
    up_z_cells = at_face(5, zlist[0:1, :])
    down_z_cells = itable[4, ROWS : ROWS + 1, :]

    def copies(step):
        def one(kind, send, recv, device):
            return pltpu.make_async_remote_copy(
                src_ref=send,
                dst_ref=recv,
                send_sem=halo_send_sem.at[step, kind],
                recv_sem=halo_recv_sem.at[step, kind],
                device_id=device,
                device_id_type=MESH,
            )

        return [
            one(0, y_send.at[step, 0], y_recv.at[step, 0], (region, sub_up)),
            one(1, y_send.at[step, 1], y_recv.at[step, 1], (region, sub_down)),
            one(2, z_send.at[step, 0], z_recv.at[step, 0], (region_up, sub)),
            one(3, z_send.at[step, 1], z_recv.at[step, 1], (region_down, sub)),
        ]

    def publish(step, g, wait_first=None):
        for d in (1, 2, 0):
            for c in range(2):
                for s in range(2):
                    tables[c * 6 + d * 2 + s] = g[c][d][s]
        for c in range(2):
            here = 4 * c
            y_send[step, 0, here : here + 4, :] = lookup(table(tables.at[c * 6 + 3]), up_y_cells)
            y_send[step, 1, here : here + 4, :] = lookup(table(tables.at[c * 6 + 2]), down_y_cells)
            z_send[step, 0, c : c + 1, :] = lookup(table(tables.at[c * 6 + 5]), up_z_cells)
            z_send[step, 1, c : c + 1, :] = lookup(table(tables.at[c * 6 + 4]), down_z_cells)
        if wait_first is not None:
            wait_first()
        for copy in copies(step):
            copy.start()

    greetings = 2 + (n_flat - 1) + (n_deep - 1)
    publish(0, rhs_g, lambda: pl.semaphore_wait(barrier, greetings))

    itable[0] = inverse([(conn_x, 0, 2, ROWS, 0)])
    itable[1] = inverse([(conn_x, 1, 2, ROWS, 0)])
    faces_x, faces_y, faces_z = pair(conn_x), pair(conn_y), pair(conn_z)
    up = [at_face(0, faces_x[1], 17), at_face(2, faces_y[1]), at_face(4, faces_z[1])]
    down = [at_face(1, faces_x[0], 17), own(3, faces_y[0]), own(5, faces_z[0])]
    last_y, last_z = sub == n_sub - 1, region == n_region - 1
    up[1] = jnp.where(jnp.logical_and(up[1] >= E_DEV, last_y), -1, up[1])
    up[2] = jnp.where(jnp.logical_and(up[2] >= E_DEV, last_z), -1, up[2])
    first_y = jnp.logical_and(down[1] >= E_DEV, sub == 0)
    first_z = jnp.logical_and(down[2] >= E_DEV, region == 0)
    lone_x = down[0] < 0

    def assemble(step, g):
        out = [[[None, None] for _ in range(3)] for _ in range(2)]
        for c in range(2):
            for d in range(3):
                at = c * 6 + d * 2
                out[c][d][1] = g[c][d][1] + lookup(table(tables.at[at]), up[d])
                out[c][d][0] = g[c][d][0] + lookup(table(tables.at[at + 1]), down[d])
        for copy in copies(step):
            copy.wait_recv()
        for c in range(2):
            from_below_y = table(y_recv.at[step, 0, pl.ds(4 * c, 4)], 4, ROWS)
            from_above_y = table(y_recv.at[step, 1, pl.ds(4 * c, 4)], 4, ROWS)
            from_below_z = table(z_recv.at[step, 0, pl.ds(c, 1)], 1, ROWS)
            from_above_z = table(z_recv.at[step, 1, pl.ds(c, 1)], 1, ROWS)
            out[c][1][1] = out[c][1][1] + lookup(from_above_y, up[1])
            out[c][2][1] = out[c][2][1] + lookup(from_above_z, up[2])
            out[c][1][0] = jnp.where(first_y, 0.0, out[c][1][0] + lookup(from_below_y, down[1]))
            out[c][2][0] = jnp.where(first_z, 0.0, out[c][2][0] + lookup(from_below_z, down[2]))
        return out

    def by_faces(number, v):
        for c in range(2):
            parts = (v[c][0][0], v[c][0][1], v[c][1][1], v[c][2][1])
            for k, part in enumerate(parts):
                vtables[number, c * 4 + k] = part
            x_low, x_up, y_up, z_up = (table(vtables.at[number, c * 4 + k]) for k in range(4))
            by_x = jnp.where(itable[1] < 0, lookup(x_low, itable[0]), lookup(x_up, itable[1]))
            by_face[number, pl.ds(c, 17, stride=2), :] = by_x[0:17]
            by_face[number, pl.ds(34 + c, ROWS, stride=2), :] = lookup(y_up, itable[3, 0:ROWS, :])
            by_face[number, pl.ds(66 + c, ROWS, stride=2), :] = lookup(z_up, itable[5, 0:ROWS, :])

    def inner(u, v):
        total = sum(u[c][d][1] * v[c][d][1] for c in range(2) for d in range(3))
        edge = sum(u[c][0][0] * v[c][0][0] for c in range(2))
        return total + jnp.where(lone_x, edge, 0.0)

    def energy(v, load, solved):
        total = sum(
            trans[c][d] * (v[c][d][0] * v[c][d][0] + v[c][d][1] * v[c][d][1])
            for c in range(2)
            for d in range(3)
        )
        return total - (load[0] * solved[0] + load[1] * solved[1])

    def scatter(send, recv, send_sem, recv_sem, peer, count, row):
        send[0:1, :] = row
        recv[count - 1 : count, :] = row
        for j in range(1, count):
            pltpu.make_async_remote_copy(
                src_ref=send.at[pl.ds(0, 1)],
                dst_ref=recv.at[pl.ds(j - 1, 1)],
                send_sem=send_sem,
                recv_sem=recv_sem,
                device_id=peer(j),
                device_id_type=MESH,
            ).start()

    def drain(buffer, sem, count):
        rows = buffer.at[pl.ds(0, count - 1)]
        pltpu.make_async_copy(rows, rows, sem).wait()

    def flat_start(k, row):
        scatter(a_send.at[k], a_recv.at[k], a_send_sem.at[k], a_recv_sem.at[k], flat_peer, n_flat, row)

    def flat_done(k):
        drain(a_recv.at[k], a_recv_sem.at[k], n_flat)
        return jnp.sum(a_recv[k], axis=0, keepdims=True)

    def deep_start(k, row):
        scatter(b_send.at[k], b_recv.at[k], b_send_sem.at[k], b_recv_sem.at[k], deep_peer, n_deep, row)

    def deep_done(k):
        drain(b_recv.at[k], b_recv_sem.at[k], n_deep)
        return jnp.sum(b_recv[k], axis=0, keepdims=True)

    b = assemble(0, rhs_g)

    load_b = face_load(b)
    inside_b = solve(load_b)
    g_b = contributions(b, inside_b)
    publish(1, g_b)
    flat_start(0, total_row([inner(b, b), energy(b, load_b, inside_b)]))
    by_faces(0, b)
    w = assemble(1, g_b)

    load_w = face_load(w)
    inside_w = solve(load_w)
    g_w = contributions(w, inside_w)
    publish(2, g_w)
    deep_start(0, flat_done(0))
    by_faces(1, w)
    ww = assemble(2, g_w)

    first = deep_done(0)
    norm_0 = pick(first, 0)
    alpha_0 = norm_0 / pick(first, 1)

    def blend(u, factor, v):
        return [
            [[u[c][d][s] - factor * v[c][d][s] for s in range(2)] for d in range(3)]
            for c in range(2)
        ]

    r = blend(b, alpha_0, w)
    s = blend(w, alpha_0, ww)
    load = face_load(s)
    flat_start(1, total_row([inner(r, r), inner(r, s), inner(s, s), energy(s, load, solve(load))]))
    load_ww = face_load(ww)
    inside_ww = solve(load_ww)
    g_ww = contributions(ww, inside_ww)
    by_faces(2, ww)
    deep_start(1, flat_done(1))
    for step in range(ROUNDS):
        for copy in copies(step):
            copy.wait_send()
    drain(a_recv.at[0], a_send_sem.at[0], n_flat)
    drain(b_recv.at[0], b_send_sem.at[0], n_deep)
    drain(a_recv.at[1], a_send_sem.at[1], n_flat)
    sums = deep_done(1)
    rr, rs, ss, sas = (pick(sums, k) for k in range(4))

    beta_0 = rr / norm_0
    alpha_1 = rr / (rs - beta_0 * rr / alpha_0)
    ws = -(rr / alpha_0 + rs) / alpha_0
    norm_2 = -alpha_1 * (rs - alpha_1 * ss - alpha_1 * beta_0 * ws)
    beta_1 = norm_2 / rr
    ratio = alpha_1 * beta_0 / alpha_0
    along = ss - alpha_1 * sas - ratio * (ws - ss)
    energy_2 = -norm_2 / alpha_1 * (1.0 + ratio) - alpha_1 * along
    alpha_2 = norm_2 / (energy_2 - beta_1 * norm_2 / alpha_1)
    on_r = alpha_1 + alpha_2 * (1.0 + beta_1)
    on_s = -alpha_2 * alpha_1
    on_b = alpha_0 + alpha_1 * beta_0 + alpha_2 * beta_1 * beta_0 + on_r
    on_w = -alpha_2 * alpha_1 * beta_0 - alpha_0 * on_r + on_s
    on_ww = -alpha_0 * on_s

    for c in range(2):
        pressure_out[pl.ds(c, ROWS, stride=2), :] = base[c] + (
            on_b * inside_b[c] + on_w * inside_w[c] + on_ww * inside_ww[c]
        )
        for d in range(3):
            for k in range(2):
                flux = on_b * g_b[c][d][k] + on_w * g_w[c][d][k] + on_ww * g_ww[c][d][k]
                flux_out[pl.ds(32 * (2 * d + k) + c, ROWS, stride=2), :] = rhs_g[c][d][k] - flux
    by_face[0] = on_b * by_face[0] + on_w * by_face[1] + on_ww * by_face[2]
    for i in range(49):
        trace_out[:, LANES * i : LANES * (i + 1)] = by_face[0, 2 * i : 2 * i + 2, :]
    drain(b_recv.at[1], b_send_sem.at[1], n_deep)


def pair_rows(array):
    return array.reshape(2, ROWS, LANES).transpose(1, 0, 2).reshape(2 * ROWS, LANES)


def solution(mesh):
    n_region, n_sub = mesh.shape["region"], mesh.shape["sub"]
    n_flat, n_deep = n_sub // 2, 2 * n_region

    def local(conn_x, conn_y, conn_z, send_y, send_z, perm, storage, sigma, source):
        vmem = pl.BlockSpec(memory_space=pltpu.VMEM)
        dma = pltpu.SemaphoreType.DMA
        sides = perm.transpose(1, 0, 2).reshape(3, 2, ROWS, LANES).transpose(0, 2, 1, 3)
        trace, pressure, flux = pl.pallas_call(
            functools.partial(kernel, n_region, n_sub),
            out_shape=(
                jax.ShapeDtypeStruct((2, NXF + 2 * E_DEV), F32),
                jax.ShapeDtypeStruct((2 * ROWS, LANES), F32),
                jax.ShapeDtypeStruct((12 * ROWS, LANES), F32),
            ),
            in_specs=[vmem] * 9,
            out_specs=(vmem,) * 3,
            scratch_shapes=[
                pltpu.VMEM((8, LANES), I32),
                pltpu.VMEM((6, 24, LANES), I32),
                pltpu.VMEM((12, ROWS, LANES), F32),
                pltpu.VMEM((3, 8, ROWS, LANES), F32),
                pltpu.VMEM((3, 104, LANES), F32),
                pltpu.VMEM((ROUNDS, 2, 8, LANES), F32),
                pltpu.VMEM((ROUNDS, 2, 8, LANES), F32),
                pltpu.VMEM((ROUNDS, 2, 2, LANES), F32),
                pltpu.VMEM((ROUNDS, 2, 2, LANES), F32),
                dma((ROUNDS, 4)),
                dma((ROUNDS, 4)),
                pltpu.VMEM((2, 8, LANES), F32),
                pltpu.VMEM((2, n_flat, LANES), F32),
                pltpu.VMEM((2, 8, LANES), F32),
                pltpu.VMEM((2, n_deep, LANES), F32),
                dma((2,)),
                dma((2,)),
                dma((2,)),
                dma((2,)),
            ],
            compiler_params=pltpu.CompilerParams(
                collective_id=0, has_side_effects=True, vmem_limit_bytes=32 * 1024 * 1024
            ),
        )(
            pair_rows(conn_x), pair_rows(conn_y), pair_rows(conn_z),
            send_y.reshape(4, LANES), send_z.reshape(1, 64),
            sides.reshape(6 * ROWS, LANES), pair_rows(storage), sigma.reshape(ROWS, LANES),
            pair_rows(source),
        )
        pressure = pressure.reshape(ROWS, 2, LANES).transpose(1, 0, 2).reshape(2, E_DEV)
        flux = flux.reshape(6, ROWS, 2, LANES).transpose(2, 0, 1, 3).reshape(2, 6, E_DEV)
        return trace, pressure, flux

    both = ("region", "sub")
    return jax.shard_map(
        local,
        mesh=mesh,
        in_specs=(
            P(None, both), P(None, both), P(None, both), P(both), P(both),
            P(None, None, both), P(None, both), P(both), P(None, both),
        ),
        out_specs=(P(None, both), P(None, both), P(None, None, both)),
        check_vma=False,
    )
```

```python
import functools

import jax
import jax.numpy as jnp
from jax import lax
from jax.experimental import pallas as pl
from jax.experimental.pallas import tpu as pltpu
from jax.sharding import PartitionSpec as P

MESH = pl.DeviceIdType.MESH
F32 = jnp.float32
I32 = jnp.int32
ROWS = 16
LANES = 128
E_DEV = ROWS * LANES
NXF = 2176
ROUNDS = 3


def iota(shape, dim):
    return lax.broadcasted_iota(I32, shape, dim)


def lane_gather(rows, lane):
    numbers = lax.GatherDimensionNumbers(
        offset_dims=(),
        collapsed_slice_dims=(1,),
        start_index_map=(1,),
        operand_batching_dims=(0,),
        start_indices_batching_dims=(0,),
    )
    return lax.gather(
        rows, lane[..., None], numbers, (1, 1), mode=lax.GatherScatterMode.PROMISE_IN_BOUNDS
    )


def lookup(rows, index, start=None):
    lane, high = index & 127, index >> 7
    out = start
    for number, row in rows:
        wide = jnp.broadcast_to(row, index.shape)
        found = lane_gather(wide, lane)
        out = jnp.where(high == number, found, jnp.zeros_like(found) if out is None else out)
    return out


def table(ref, count=ROWS, first=0):
    return [(first + h, ref[h : h + 1, :]) for h in range(count)]


def total_row(parts):
    lane = iota((1, LANES), 1)
    row = jnp.zeros((1, LANES), F32)
    for number, part in enumerate(parts):
        flat = jnp.sum(part, axis=0, keepdims=True)
        row = jnp.where(lane == number, jnp.sum(flat, axis=1, keepdims=True), row)
    return row


def pick(row, number):
    return jnp.sum(jnp.where(iota((1, LANES), 1) == number, row, 0.0), axis=1, keepdims=True)


def spots(place):
    return jnp.where(iota((LANES, LANES), 0) == (place & 127), 1.0, 0.0).astype(jnp.bfloat16)


def by_row(hit, *values):
    blocks = [jnp.where(hit, value, 0.0) for value in values]
    return jnp.concatenate(blocks, axis=0).astype(jnp.bfloat16)


def product(left, right):
    return lax.dot_general(left, right, (((1,), (1,)), ((), ())), preferred_element_type=F32)


def cut(value):
    scaled = value * 65537.0
    high = scaled - (scaled - value)
    rest = value - high
    scaled = rest * 65537.0
    middle = scaled - (scaled - rest)
    return high, middle, rest - middle


def kernel(
    n_region, n_sub,
    conn_x_in, conn_y_in, conn_z_in, send_y_in, send_z_in, perm_in, storage_in, sigma_in, source_in,
    trace_out, pressure_out, flux_out,
    conn_x, conn_y, conn_z, send_y, send_z, perm, storage, sigma_ref, source, in_sem,
    zlist, tables, place, ilist, cuts, left, spot, moved, by_face,
    y_send, y_recv, z_send, z_recv, halo_send_sem, halo_recv_sem,
    a_send, a_recv, b_send, b_recv, a_send_sem, a_recv_sem, b_send_sem, b_recv_sem,
):
    loads = [
        pltpu.make_async_copy(there, here, in_sem.at[k])
        for k, (there, here) in enumerate(
            (
                (conn_y_in, conn_y), (conn_z_in, conn_z), (conn_x_in, conn_x),
                (send_y_in, send_y), (send_z_in, send_z),
                (perm_in, perm), (storage_in, storage), (sigma_in, sigma_ref), (source_in, source),
            )
        )
    ]
    for load in loads:
        load.start()

    region, sub = lax.axis_index("region"), lax.axis_index("sub")
    n_flat, n_deep = n_sub // 2, 2 * n_region
    core, deep = lax.rem(sub, 2), lax.rem(lax.div(sub, 2), 2)
    flat_me = lax.div(sub, 4) * 2 + core
    deep_me = deep * n_region + region
    sub_up, sub_down = lax.rem(sub + 1, n_sub), lax.rem(sub + n_sub - 1, n_sub)
    region_up, region_down = lax.rem(region + 1, n_region), lax.rem(region + n_region - 1, n_region)

    def flat_peer(offset):
        peer = lax.rem(flat_me + offset, n_flat)
        return (region, lax.div(peer, 2) * 4 + deep * 2 + lax.rem(peer, 2))

    def deep_peer(offset):
        peer = lax.rem(deep_me + offset, n_deep)
        return (lax.rem(peer, n_region), sub - deep * 2 + lax.div(peer, n_region) * 2)

    barrier = pltpu.get_barrier_semaphore()

    def greet(device):
        pl.semaphore_signal(barrier, inc=1, device_id=device, device_id_type=MESH)

    greet((region, sub_up))
    greet((region, sub_down))
    for j in range(1, n_flat):
        greet(flat_peer(j))
    for j in range(1, n_deep):
        greet(deep_peer(j))
    for load in loads:
        load.wait()

    def pair(ref, first=0):
        return [ref[pl.ds(first + k, ROWS, stride=2), :] for k in range(2)]

    def chunk(i):
        return pl.ds(pl.multiple_of(i * LANES, LANES), LANES)

    def element_terms(trans, store, sigma):
        diag = [
            2.0 * (trans[c][0] + trans[c][1] + trans[c][2]) + store[c] + sigma for c in range(2)
        ]
        determ = diag[0] * diag[1] - sigma * sigma
        return diag[1] / determ, sigma / determ, diag[0] / determ

    def solve(terms, load):
        return (terms[0] * load[0] + terms[1] * load[1], terms[1] * load[0] + terms[2] * load[1])

    def faces_step(i, carry):
        lane, row = iota((1, LANES), 1).astype(F32), (i + 1).astype(F32)
        for k, (ref, side, count, first, at) in enumerate(
            (
                (conn_y, 1, 16, 0, 0), (conn_z, 1, 16, 0, 32), (conn_y, 0, 8, 16, 64),
                (conn_z, 0, 8, 16, 80), (conn_x, 1, 24, 0, 96),
            )
        ):
            face = ref[pl.ds(2 * i + side, 1), :]
            hit = iota((count, LANES), 0) == (face >> 7) - first
            left[at : at + 2 * count, chunk(i)] = by_row(hit, lane, row)
            spot[k, :, chunk(i)] = spots(face)
        return carry

    lax.fori_loop(0, ROWS, faces_step, 0)

    def cells(k, at, count):
        found = product(left[at : at + 2 * count, :], spot[k]).astype(I32)
        return (found[count:] - 1) * LANES + found[:count]

    cell_y, cell_z = cells(0, 0, 16), cells(1, 32, 16)
    side_y, side_z = cells(2, 64, 8), cells(3, 80, 8)
    cell_x = cells(4, 96, 24)
    place[0, 0:ROWS, :] = cell_y
    place[1, 0:ROWS, :] = cell_z
    place[2, 0:24, :] = cell_x
    zlist[0:1, :] = jnp.full((1, LANES), -1, I32)
    zlist[0:1, 0:64] = send_z[...]

    def find(ref, index, missing, count=ROWS):
        return lookup(table(ref, count), index, jnp.full(index.shape, missing, I32))

    up_y = find(place.at[0], send_y[...], -1)
    up_z = find(place.at[1], zlist[0:1, :], -1)
    down_y, down_z = side_y[0:4], side_z[0:1]

    def copies(step):
        def one(kind, send, recv, device):
            return pltpu.make_async_remote_copy(
                src_ref=send,
                dst_ref=recv,
                send_sem=halo_send_sem.at[step, kind],
                recv_sem=halo_recv_sem.at[step, kind],
                device_id=device,
                device_id_type=MESH,
            )

        return [
            one(0, y_send.at[step, 0], y_recv.at[step, 0], (region, sub_up)),
            one(1, y_send.at[step, 1], y_recv.at[step, 1], (region, sub_down)),
            one(2, z_send.at[step, 0], z_recv.at[step, 0], (region_up, sub)),
            one(3, z_send.at[step, 1], z_recv.at[step, 1], (region_down, sub)),
        ]

    def keep_sides(at):
        for c in range(2):
            ilist[at, 4 * c : 4 * c + 4, :] = up_y
            ilist[at + 1, 4 * c : 4 * c + 4, :] = down_y
            ilist[at + 2, c : c + 1, :] = up_z
            ilist[at + 2, 2 + c : 3 + c, :] = down_z

    def publish(step, at, y_low, y_up, z_low, z_up, before=None):
        for k, part in enumerate((*y_up, *y_low)):
            tables[k, 0:ROWS, :] = part
        second = iota((8, LANES), 0) >= 4
        for k in range(2):
            rows = [
                (h, jnp.where(second, tables[2 * k + 1, h : h + 1, :], tables[2 * k, h : h + 1, :]))
                for h in range(ROWS)
            ]
            y_send[step, k] = lookup(rows, ilist[at + k])
        for k, part in enumerate((*z_up, *z_low)):
            tables[4, pl.ds(k, ROWS, stride=4), :] = part
        rows = [(h, tables[4, 4 * h : 4 * h + 4, :]) for h in range(ROWS)]
        z_rows = lookup(rows, ilist[at + 2, 0:4, :])
        z_send[step, 0] = z_rows[0:2]
        z_send[step, 1] = z_rows[2:4]
        if before is not None:
            before()
        for copy in copies(step):
            copy.start()

    keep_sides(0)
    by_side = [pair(perm, 32 * d) for d in range(3)]
    trans = [[2.0 * by_side[d][c] for d in range(3)] for c in range(2)]
    store, origin, sigma = pair(storage), pair(source), sigma_ref[...]
    base = solve(element_terms(trans, store, sigma), origin)
    first_y = [trans[c][1] * base[c] for c in range(2)]
    first_z = [trans[c][2] * base[c] for c in range(2)]
    greetings = 2 + (n_flat - 1) + (n_deep - 1)
    publish(0, 0, first_y, first_y, first_z, first_z, lambda: pl.semaphore_wait(barrier, greetings))

    faces = (pair(conn_x), pair(conn_y), pair(conn_z))
    below = (
        find(place.at[2], faces[0][0], -1, 17),
        find(place.at[0], faces[1][0], -1),
        find(place.at[1], faces[2][0], -1),
    )
    words = [jnp.where(cell >= 0, cell + 4097, 0) for cell in below]
    for level in range(5):
        for d, levels in enumerate((4, 2, 5)):
            if level < levels:
                place[3 + d, 0:ROWS, :] = words[d]
                ahead = find(place.at[3 + d], (words[d] & 4095) - 1, 0)
                words[d] = (words[d] & ~4095) + ahead
    steps = [word >> 12 for word in words]
    place[3, 0:ROWS, :] = steps[0] * LANES + steps[1] * 32 + steps[2]

    values = [*trans[0], *trans[1], *store, sigma, *origin]
    for k, value in enumerate(values):
        for j, part in enumerate(cut(value)):
            cuts[3 * k + j] = part
    lists = [faces[0][1], faces[1][1], faces[2][1], faces[0][0]]
    lists += [jnp.maximum(faces[d][0] - E_DEV, 0) for d in (1, 2)]
    for k, face in enumerate(lists):
        cuts[33 + 2 * k] = (face >> 7).astype(F32)
        cuts[34 + 2 * k] = (face & 127).astype(F32)

    def order_step(i, carry):
        at = place[3, pl.ds(i, 1), :]
        hit = iota((ROWS, LANES), 0) == (at >> 7)
        spot[0, :, chunk(i)] = spots(at)
        for k in range(45):
            left[ROWS * k : ROWS * (k + 1), chunk(i)] = by_row(hit, cuts[k, pl.ds(i, 1), :])
        lane, row = iota((1, LANES), 1).astype(F32), i.astype(F32)
        left[ROWS * 45 : ROWS * 47, chunk(i)] = by_row(hit, row, lane)
        return carry

    lax.fori_loop(0, ROWS, order_step, 0)
    moved[0 : ROWS * 47, :] = product(left[0 : ROWS * 47, :], spot[0])

    def part(k):
        return moved[ROWS * k : ROWS * (k + 1), :]

    values = [part(3 * k) + part(3 * k + 1) + part(3 * k + 2) for k in range(11)]
    trans, store = [values[0:3], values[3:6]], values[6:8]
    sigma, origin = values[8], values[9:11]
    for k in range(7):
        ilist[8 + 2 * k : 10 + 2 * k] = (
            (part(33 + 2 * k) * 128.0 + part(34 + 2 * k)).astype(I32).reshape(2, 8, LANES)
        )

    def listed(k):
        return ilist[8 + 2 * k : 10 + 2 * k].reshape(ROWS, LANES)

    terms = element_terms(trans, store, sigma)

    lane, row = iota((ROWS, LANES), 1), iota((ROWS, LANES), 0)
    level = lane & 31
    place[4, 0:ROWS, :] = place[3, 0:ROWS, :]
    up_y, down_y = find(place.at[3], up_y, -1), find(place.at[3], down_y, -1)
    up_z, down_z = find(place.at[3], up_z, -1), find(place.at[3], down_z, -1)
    keep_sides(3)
    entry = iota((1, LANES), 1).astype(F32)
    lefts, rights = [], []
    for h in range(4):
        at = ilist[3, h : h + 1, :]
        hit = iota((ROWS, LANES), 0) == (at >> 7)
        lefts.append(by_row(hit, entry, jnp.full((1, LANES), h + 1.0, F32)))
        rights.append(spots(at))
    found = product(jnp.concatenate(lefts, axis=1), jnp.concatenate(rights, axis=1)).astype(I32)
    above_y = (found[ROWS:] - 1) * LANES + found[:ROWS]
    at = ilist[5, 0:1, :]
    hit = iota((ROWS, LANES), 0) == (at >> 7)
    found = product(by_row(hit, entry, jnp.full((1, LANES), 1.0, F32)), spots(at)).astype(I32)
    above_z = (found[ROWS:] - 1) * LANES + found[:ROWS]
    above_y = jnp.where(sub == n_sub - 1, -1, above_y)
    above_z = jnp.where(region == n_region - 1, -1, above_z)
    low_y, low_z = lane < 32, level == 0
    below_y, below_z = jnp.where(low_y, listed(4), -1), jnp.where(low_z, listed(5), -1)
    zero_y = jnp.logical_and(low_y, sub == 0)
    zero_z = jnp.logical_and(low_z, region == 0)

    def face_load(v):
        return [
            sum(trans[c][d] * (v[c][d][0] + v[c][d][1]) for d in range(3)) for c in range(2)
        ]

    def contributions(v, inside):
        return [
            [[trans[c][d] * (v[c][d][s] - inside[c]) for s in range(2)] for d in range(3)]
            for c in range(2)
        ]

    def send(step, g):
        publish(step, 3, *([g[c][d][s] for c in range(2)] for d in (1, 2) for s in range(2)))

    def assemble(step, g):
        out = [[[None, None] for _ in range(3)] for _ in range(2)]
        for c in range(2):
            (x_low, x_up), (y_low, y_up), (z_low, z_up) = g[c]
            out[c][0][1] = x_up + jnp.where(row == 15, 0.0, pltpu.roll(x_low, 15, 0))
            out[c][0][0] = x_low + jnp.where(row == 0, 0.0, pltpu.roll(x_up, 1, 0))
            out[c][1][1] = jnp.where(lane >= 96, 0.0, pltpu.roll(y_low, 96, 1))
            out[c][1][0] = jnp.where(low_y, 0.0, pltpu.roll(y_up, 32, 1))
            out[c][2][1] = jnp.where(level == 31, 0.0, pltpu.roll(z_low, 127, 1))
            out[c][2][0] = jnp.where(low_z, 0.0, pltpu.roll(z_up, 1, 1))
        for copy in copies(step):
            copy.wait_recv()
        for c in range(2):
            from_below_y = lookup(table(y_recv.at[step, 0, pl.ds(4 * c, 4)], 4), below_y)
            from_above_y = lookup(table(y_recv.at[step, 1, pl.ds(4 * c, 4)], 4), above_y)
            from_below_z = lookup(table(z_recv.at[step, 0, pl.ds(c, 1)], 1), below_z)
            from_above_z = lookup(table(z_recv.at[step, 1, pl.ds(c, 1)], 1), above_z)
            out[c][1][1] = g[c][1][1] + (out[c][1][1] + from_above_y)
            out[c][2][1] = g[c][2][1] + (out[c][2][1] + from_above_z)
            out[c][1][0] = jnp.where(zero_y, 0.0, g[c][1][0] + (out[c][1][0] + from_below_y))
            out[c][2][0] = jnp.where(zero_z, 0.0, g[c][2][0] + (out[c][2][0] + from_below_z))
        return out

    def inner(u, v):
        total = sum(u[c][d][1] * v[c][d][1] for c in range(2) for d in range(3))
        edge = sum(u[c][0][0] * v[c][0][0] for c in range(2))
        return total + jnp.where(row == 0, edge, 0.0)

    def energy(v, load, solved):
        total = sum(
            trans[c][d] * (v[c][d][0] * v[c][d][0] + v[c][d][1] * v[c][d][1])
            for c in range(2)
            for d in range(3)
        )
        return total - (load[0] * solved[0] + load[1] * solved[1])

    def scatter(send, recv, send_sem, recv_sem, peer, count, row):
        send[0:1, :] = row
        recv[count - 1 : count, :] = row
        for j in sorted(range(1, count), key=lambda j: -min(j, count - j)):
            pltpu.make_async_remote_copy(
                src_ref=send.at[pl.ds(0, 1)],
                dst_ref=recv.at[pl.ds(j - 1, 1)],
                send_sem=send_sem,
                recv_sem=recv_sem,
                device_id=peer(j),
                device_id_type=MESH,
            ).start()

    def drain(buffer, sem, count):
        rows = buffer.at[pl.ds(0, count - 1)]
        pltpu.make_async_copy(rows, rows, sem).wait()

    def flat_start(k, row):
        scatter(a_send.at[k], a_recv.at[k], a_send_sem.at[k], a_recv_sem.at[k], flat_peer, n_flat, row)

    def flat_done(k):
        drain(a_recv.at[k], a_recv_sem.at[k], n_flat)
        return jnp.sum(a_recv[k], axis=0, keepdims=True)

    def deep_start(k, row):
        scatter(b_send.at[k], b_recv.at[k], b_send_sem.at[k], b_recv_sem.at[k], deep_peer, n_deep, row)

    def deep_done(k):
        drain(b_recv.at[k], b_recv_sem.at[k], n_deep)
        return jnp.sum(b_recv[k], axis=0, keepdims=True)

    base = solve(terms, origin)
    b = assemble(0, [[[trans[c][d] * base[c]] * 2 for d in range(3)] for c in range(2)])

    load = face_load(b)
    inside = solve(terms, load)
    g = contributions(b, inside)
    send(1, g)
    flat_start(0, total_row([inner(b, b), energy(b, load, inside)]))
    w = assemble(1, g)

    g = contributions(w, solve(terms, face_load(w)))
    send(2, g)
    deep_start(0, flat_done(0))
    ww = assemble(2, g)

    first = deep_done(0)
    norm_0 = pick(first, 0)
    alpha_0 = norm_0 / pick(first, 1)

    def blend(u, factor, v):
        return [
            [[u[c][d][s] - factor * v[c][d][s] for s in range(2)] for d in range(3)]
            for c in range(2)
        ]

    r = blend(b, alpha_0, w)
    s = blend(w, alpha_0, ww)
    load = face_load(s)
    flat_start(1, total_row([inner(r, r), inner(r, s), inner(s, s), energy(s, load, solve(terms, load))]))
    deep_start(1, flat_done(1))
    for step in range(ROUNDS):
        for copy in copies(step):
            copy.wait_send()
    drain(a_recv.at[0], a_send_sem.at[0], n_flat)
    drain(b_recv.at[0], b_send_sem.at[0], n_deep)
    drain(a_recv.at[1], a_send_sem.at[1], n_flat)
    sums = deep_done(1)
    rr, rs, ss, sas = (pick(sums, k) for k in range(4))

    beta_0 = rr / norm_0
    alpha_1 = rr / (rs - beta_0 * rr / alpha_0)
    ws = -(rr / alpha_0 + rs) / alpha_0
    norm_2 = -alpha_1 * (rs - alpha_1 * ss - alpha_1 * beta_0 * ws)
    beta_1 = norm_2 / rr
    ratio = alpha_1 * beta_0 / alpha_0
    along = ss - alpha_1 * sas - ratio * (ws - ss)
    energy_2 = -norm_2 / alpha_1 * (1.0 + ratio) - alpha_1 * along
    alpha_2 = norm_2 / (energy_2 - beta_1 * norm_2 / alpha_1)
    on_r = alpha_1 + alpha_2 * (1.0 + beta_1)
    on_s = -alpha_2 * alpha_1
    on_b = alpha_0 + alpha_1 * beta_0 + alpha_2 * beta_1 * beta_0 + on_r
    on_w = -alpha_2 * alpha_1 * beta_0 - alpha_0 * on_r + on_s
    on_ww = -alpha_0 * on_s

    trace = [
        [
            [on_b * b[c][d][k] + on_w * w[c][d][k] + on_ww * ww[c][d][k] for k in range(2)]
            for d in range(3)
        ]
        for c in range(2)
    ]
    load = face_load(trace)
    pressure = solve(terms, [origin[c] + load[c] for c in range(2)])
    flux = [
        [trans[c][d] * (pressure[c] - trace[c][d][k]) for d in range(3) for k in range(2)]
        for c in range(2)
    ]

    results = [*pressure, *flux[0], *flux[1]]
    results += [trace[c][d][1] for d in range(3) for c in range(2)]
    for k, value in enumerate(results):
        for j, piece in enumerate(cut(value)):
            cuts[3 * k + j] = piece
    for k in range(4):
        place[k, 0:ROWS, :] = listed((6, 1, 2, 0)[k])

    def back_step(i, carry):
        lanes = chunk(i)
        at = [place[k, pl.ds(i, 1), :] for k in range(4)]
        hit = [iota((ROWS, LANES), 0) == (at[k] >> 7) for k in range(3)]
        for k in range(4):
            spot[k, :, lanes] = spots(at[k])
        for k in range(42):
            left[ROWS * k : ROWS * (k + 1), lanes] = by_row(hit[0], cuts[k, pl.ds(i, 1), :])
        for k in range(6):
            here = ROWS * (42 + k)
            left[here : here + ROWS, lanes] = by_row(hit[1], cuts[48 + k, pl.ds(i, 1), :])
            here = ROWS * (48 + k)
            left[here : here + ROWS, lanes] = by_row(hit[2], cuts[54 + k, pl.ds(i, 1), :])
        hit_x = iota((24, LANES), 0) == (at[3] >> 7)
        for j in range(3):
            here = ROWS * 54 + 48 * j
            both = (cuts[42 + j, pl.ds(i, 1), :], cuts[45 + j, pl.ds(i, 1), :])
            left[here : here + 48, lanes] = by_row(hit_x, *both)
        return carry

    lax.fori_loop(0, ROWS, back_step, 0)
    moved[0 : ROWS * 42, :] = product(left[0 : ROWS * 42, :], spot[0])
    moved[ROWS * 42 : ROWS * 48, :] = product(left[ROWS * 42 : ROWS * 48, :], spot[1])
    moved[ROWS * 48 : ROWS * 54, :] = product(left[ROWS * 48 : ROWS * 54, :], spot[2])
    lowest = ilist[14, 0:1, :]
    hit_x = iota((24, LANES), 0) == (lowest >> 7)
    edges = [cut(trace[c][0][0][0:1, :]) for c in range(2)]
    edge = jnp.concatenate([by_row(hit_x, edges[0][j], edges[1][j]) for j in range(3)], axis=0)
    of_x = product(left[ROWS * 54 : ROWS * 63, :], spot[3]) + product(edge, spots(lowest))
    of_x = of_x[0:48] + of_x[48:96] + of_x[96:144]

    def whole(k):
        return part(k) + part(k + 1) + part(k + 2)

    for c in range(2):
        pressure_out[pl.ds(c, ROWS, stride=2), :] = whole(3 * c)
        for k in range(6):
            flux_out[pl.ds(32 * k + c, ROWS, stride=2), :] = whole(6 + 18 * c + 3 * k)
        by_face[pl.ds(c, 17, stride=2), :] = of_x[24 * c : 24 * c + 17]
        by_face[pl.ds(34 + c, ROWS, stride=2), :] = whole(42 + 3 * c)
        by_face[pl.ds(66 + c, ROWS, stride=2), :] = whole(48 + 3 * c)
    for i in range(49):
        trace_out[:, LANES * i : LANES * (i + 1)] = by_face[2 * i : 2 * i + 2, :]
    drain(b_recv.at[1], b_send_sem.at[1], n_deep)


def pair_rows(array):
    return array.reshape(2, ROWS, LANES).transpose(1, 0, 2).reshape(2 * ROWS, LANES)


def solution(mesh):
    n_region, n_sub = mesh.shape["region"], mesh.shape["sub"]
    n_flat, n_deep = n_sub // 2, 2 * n_region

    def local(conn_x, conn_y, conn_z, send_y, send_z, perm, storage, sigma, source):
        vmem = pl.BlockSpec(memory_space=pltpu.VMEM)
        dma = pltpu.SemaphoreType.DMA
        sides = perm.transpose(1, 0, 2).reshape(3, 2, ROWS, LANES).transpose(0, 2, 1, 3)
        trace, pressure, flux = pl.pallas_call(
            functools.partial(kernel, n_region, n_sub),
            out_shape=(
                jax.ShapeDtypeStruct((2, NXF + 2 * E_DEV), F32),
                jax.ShapeDtypeStruct((2 * ROWS, LANES), F32),
                jax.ShapeDtypeStruct((12 * ROWS, LANES), F32),
            ),
            in_specs=[pl.BlockSpec(memory_space=pltpu.HBM)] * 9,
            out_specs=(vmem,) * 3,
            scratch_shapes=[
                pltpu.VMEM((2 * ROWS, LANES), I32),
                pltpu.VMEM((2 * ROWS, LANES), I32),
                pltpu.VMEM((2 * ROWS, LANES), I32),
                pltpu.VMEM((4, LANES), I32),
                pltpu.VMEM((1, 64), I32),
                pltpu.VMEM((6 * ROWS, LANES), F32),
                pltpu.VMEM((2 * ROWS, LANES), F32),
                pltpu.VMEM((ROWS, LANES), F32),
                pltpu.VMEM((2 * ROWS, LANES), F32),
                dma((9,)),
                pltpu.VMEM((8, LANES), I32),
                pltpu.VMEM((5, 4 * ROWS, LANES), F32),
                pltpu.VMEM((6, 24, LANES), I32),
                pltpu.VMEM((22, 8, LANES), I32),
                pltpu.VMEM((60, ROWS, LANES), F32),
                pltpu.VMEM((63 * ROWS, E_DEV), jnp.bfloat16),
                pltpu.VMEM((5, LANES, E_DEV), jnp.bfloat16),
                pltpu.VMEM((54 * ROWS, LANES), F32),
                pltpu.VMEM((104, LANES), F32),
                pltpu.VMEM((ROUNDS, 2, 8, LANES), F32),
                pltpu.VMEM((ROUNDS, 2, 8, LANES), F32),
                pltpu.VMEM((ROUNDS, 2, 2, LANES), F32),
                pltpu.VMEM((ROUNDS, 2, 2, LANES), F32),
                dma((ROUNDS, 4)),
                dma((ROUNDS, 4)),
                pltpu.VMEM((2, 8, LANES), F32),
                pltpu.VMEM((2, n_flat, LANES), F32),
                pltpu.VMEM((2, 8, LANES), F32),
                pltpu.VMEM((2, n_deep, LANES), F32),
                dma((2,)),
                dma((2,)),
                dma((2,)),
                dma((2,)),
            ],
            compiler_params=pltpu.CompilerParams(
                collective_id=0, has_side_effects=True, vmem_limit_bytes=32 * 1024 * 1024
            ),
        )(
            pair_rows(conn_x), pair_rows(conn_y), pair_rows(conn_z),
            send_y.reshape(4, LANES), send_z.reshape(1, 64),
            sides.reshape(6 * ROWS, LANES), pair_rows(storage), sigma.reshape(ROWS, LANES),
            pair_rows(source),
        )
        pressure = pressure.reshape(ROWS, 2, LANES).transpose(1, 0, 2).reshape(2, E_DEV)
        flux = flux.reshape(6, ROWS, 2, LANES).transpose(2, 0, 1, 3).reshape(2, 6, E_DEV)
        return trace, pressure, flux

    both = ("region", "sub")
    return jax.shard_map(
        local,
        mesh=mesh,
        in_specs=(
            P(None, both), P(None, both), P(None, both), P(both), P(both),
            P(None, None, both), P(None, both), P(both), P(None, both),
        ),
        out_specs=(P(None, both), P(None, both), P(None, None, both)),
        check_vma=False,
    )
```

```python
import functools

import jax
import jax.numpy as jnp
from jax import lax
from jax.experimental import pallas as pl
from jax.experimental.pallas import tpu as pltpu
from jax.sharding import PartitionSpec as P

MESH = pl.DeviceIdType.MESH
F32 = jnp.float32
I32 = jnp.int32
ROWS = 16
LANES = 128
E_DEV = ROWS * LANES
NXF = 2176
ROUNDS = 3


def iota(shape, dim):
    return lax.broadcasted_iota(I32, shape, dim)


def inverse(pieces):
    total = None
    for ref, row, stride, count, first in pieces:
        for start in range(0, count, 2):
            spots, hits = [], []
            for i in range(start, min(start + 2, count)):
                face = ref[row + stride * i : row + stride * i + 1, :]
                cell = iota((1, LANES), 1) + (first + LANES * i)
                spots.append(jnp.where(iota((LANES, LANES), 0) == (face & 127), 1.0, 0.0))
                hit = iota((24, LANES), 0) == (face >> 7)
                low = jnp.where(hit, (cell & 127).astype(F32), 0.0)
                high = jnp.where(hit, ((cell >> 7) + 1).astype(F32), 0.0)
                hits.append(jnp.concatenate([low, high], axis=0))
            left = jnp.concatenate(hits, axis=1).astype(jnp.bfloat16)
            spot = jnp.concatenate(spots, axis=1).astype(jnp.bfloat16)
            part = lax.dot_general(left, spot, (((1,), (1,)), ((), ())), preferred_element_type=F32)
            total = part if total is None else total + part
    whole = total.astype(I32)
    return (whole[24:] - 1) * 128 + whole[:24]


def lane_gather(rows, lane):
    numbers = lax.GatherDimensionNumbers(
        offset_dims=(),
        collapsed_slice_dims=(1,),
        start_index_map=(1,),
        operand_batching_dims=(0,),
        start_indices_batching_dims=(0,),
    )
    return lax.gather(
        rows, lane[..., None], numbers, (1, 1), mode=lax.GatherScatterMode.PROMISE_IN_BOUNDS
    )


def lookup(rows, index, start=None):
    lane, high = index & 127, index >> 7
    out = start
    for number, row in rows:
        wide = jnp.broadcast_to(row, index.shape)
        found = lane_gather(wide, lane)
        out = jnp.where(high == number, found, jnp.zeros_like(found) if out is None else out)
    return out


def table(ref, count=ROWS, first=0):
    return [(first + h, ref[h : h + 1, :]) for h in range(count)]


def total_row(parts):
    lane = iota((1, LANES), 1)
    row = jnp.zeros((1, LANES), F32)
    for number, part in enumerate(parts):
        flat = jnp.sum(part, axis=0, keepdims=True)
        row = jnp.where(lane == number, jnp.sum(flat, axis=1, keepdims=True), row)
    return row


def pick(row, number):
    return jnp.sum(jnp.where(iota((1, LANES), 1) == number, row, 0.0), axis=1, keepdims=True)


def kernel(
    n_region, n_sub,
    conn_x_in, conn_y_in, conn_z_in, send_y_in, send_z_in, perm_in, storage_in, sigma_in, source_in,
    trace_out, pressure_out, flux_out,
    conn_x, conn_y, conn_z, send_y, send_z, perm, storage, sigma_ref, source, in_sem,
    zlist, itable, tables, vtables, by_face,
    y_send, y_recv, z_send, z_recv, halo_send_sem, halo_recv_sem,
    a_send, a_recv, b_send, b_recv, a_send_sem, a_recv_sem, b_send_sem, b_recv_sem,
):
    loads = [
        pltpu.make_async_copy(there, here, in_sem.at[k])
        for k, (there, here) in enumerate(
            (
                (conn_y_in, conn_y), (conn_z_in, conn_z), (send_y_in, send_y), (send_z_in, send_z),
                (perm_in, perm), (storage_in, storage), (sigma_in, sigma_ref), (source_in, source),
                (conn_x_in, conn_x),
            )
        )
    ]
    region, sub = lax.axis_index("region"), lax.axis_index("sub")
    n_flat, n_deep = n_sub // 2, 2 * n_region
    core, deep = lax.rem(sub, 2), lax.rem(lax.div(sub, 2), 2)
    flat_me = lax.div(sub, 4) * 2 + core
    deep_me = deep * n_region + region
    sub_up, sub_down = lax.rem(sub + 1, n_sub), lax.rem(sub + n_sub - 1, n_sub)
    region_up, region_down = lax.rem(region + 1, n_region), lax.rem(region + n_region - 1, n_region)

    def flat_peer(offset):
        peer = lax.rem(flat_me + offset, n_flat)
        return (region, lax.div(peer, 2) * 4 + deep * 2 + lax.rem(peer, 2))

    def deep_peer(offset):
        peer = lax.rem(deep_me + offset, n_deep)
        return (lax.rem(peer, n_region), sub - deep * 2 + lax.div(peer, n_region) * 2)

    barrier = pltpu.get_barrier_semaphore()

    def greet(device):
        pl.semaphore_signal(barrier, inc=1, device_id=device, device_id_type=MESH)

    greet((region, sub_up))
    greet((region, sub_down))
    for load in loads:
        load.start()
    for j in sorted(range(1, n_deep), key=lambda j: -min(j, n_deep - j)):
        greet(deep_peer(j))
    for j in range(1, n_flat):
        greet(flat_peer(j))
    for load in loads:
        load.wait()

    def pair(ref, first=0):
        return [ref[pl.ds(first + k, ROWS, stride=2), :] for k in range(2)]

    by_side = [pair(perm, 32 * d) for d in range(3)]
    trans = [[2.0 * by_side[d][c] for d in range(3)] for c in range(2)]
    store, origin, sigma = pair(storage), pair(source), sigma_ref[...]

    diag = [2.0 * (trans[c][0] + trans[c][1] + trans[c][2]) + store[c] + sigma for c in range(2)]
    determ = diag[0] * diag[1] - sigma * sigma
    solve_00, solve_01, solve_11 = diag[1] / determ, sigma / determ, diag[0] / determ

    def solve(load):
        return (solve_00 * load[0] + solve_01 * load[1], solve_01 * load[0] + solve_11 * load[1])

    def face_load(v):
        return [
            sum(trans[c][d] * (v[c][d][0] + v[c][d][1]) for d in range(3)) for c in range(2)
        ]

    def contributions(v, inner):
        return [
            [[trans[c][d] * (v[c][d][s] - inner[c]) for s in range(2)] for d in range(3)]
            for c in range(2)
        ]

    base = solve(origin)
    rhs_g = [[[trans[c][d] * base[c]] * 2 for d in range(3)] for c in range(2)]

    def at_face(which, face, count=ROWS):
        return lookup(table(itable.at[which], count), face, jnp.full(face.shape, -1, I32))

    def own(which, face):
        return jnp.where(face >= E_DEV, face, at_face(which, face))

    zlist[0:1, :] = jnp.full((1, LANES), -1, I32)
    zlist[0:1, 0:64] = send_z[...]
    itable[2] = inverse([(conn_y, 0, 2, ROWS, 0), (send_y, 0, 1, 4, E_DEV)])
    itable[3] = inverse([(conn_y, 1, 2, ROWS, 0)])
    itable[4] = inverse([(conn_z, 0, 2, ROWS, 0), (zlist, 0, 1, 1, E_DEV)])
    itable[5] = inverse([(conn_z, 1, 2, ROWS, 0)])
    up_y_cells = at_face(3, send_y[...])
    down_y_cells = itable[2, ROWS : ROWS + 4, :]
    up_z_cells = at_face(5, zlist[0:1, :])
    down_z_cells = itable[4, ROWS : ROWS + 1, :]

    def copies(step):
        def one(kind, send, recv, device):
            return pltpu.make_async_remote_copy(
                src_ref=send,
                dst_ref=recv,
                send_sem=halo_send_sem.at[step, kind],
                recv_sem=halo_recv_sem.at[step, kind],
                device_id=device,
                device_id_type=MESH,
            )

        return [
            one(0, y_send.at[step, 0], y_recv.at[step, 0], (region, sub_up)),
            one(1, y_send.at[step, 1], y_recv.at[step, 1], (region, sub_down)),
            one(2, z_send.at[step, 0], z_recv.at[step, 0], (region_up, sub)),
            one(3, z_send.at[step, 1], z_recv.at[step, 1], (region_down, sub)),
        ]

    def publish(step, g, wait_first=None):
        for d in (1, 2, 0):
            for c in range(2):
                for s in range(2):
                    tables[c * 6 + d * 2 + s] = g[c][d][s]
        for c in range(2):
            here = 4 * c
            y_send[step, 0, here : here + 4, :] = lookup(table(tables.at[c * 6 + 3]), up_y_cells)
            y_send[step, 1, here : here + 4, :] = lookup(table(tables.at[c * 6 + 2]), down_y_cells)
            z_send[step, 0, c : c + 1, :] = lookup(table(tables.at[c * 6 + 5]), up_z_cells)
            z_send[step, 1, c : c + 1, :] = lookup(table(tables.at[c * 6 + 4]), down_z_cells)
        if wait_first is not None:
            wait_first()
        for copy in copies(step):
            copy.start()

    greetings = 2 + (n_flat - 1) + (n_deep - 1)
    publish(0, rhs_g, lambda: pl.semaphore_wait(barrier, greetings))

    itable[0] = inverse([(conn_x, 0, 2, ROWS, 0)])
    itable[1] = inverse([(conn_x, 1, 2, ROWS, 0)])
    faces_x, faces_y, faces_z = pair(conn_x), pair(conn_y), pair(conn_z)
    up = [at_face(0, faces_x[1], 17), at_face(2, faces_y[1]), at_face(4, faces_z[1])]
    down = [at_face(1, faces_x[0], 17), own(3, faces_y[0]), own(5, faces_z[0])]
    last_y, last_z = sub == n_sub - 1, region == n_region - 1
    up[1] = jnp.where(jnp.logical_and(up[1] >= E_DEV, last_y), -1, up[1])
    up[2] = jnp.where(jnp.logical_and(up[2] >= E_DEV, last_z), -1, up[2])
    first_y = jnp.logical_and(down[1] >= E_DEV, sub == 0)
    first_z = jnp.logical_and(down[2] >= E_DEV, region == 0)
    lone_x = down[0] < 0

    def assemble(step, g):
        out = [[[None, None] for _ in range(3)] for _ in range(2)]
        for c in range(2):
            for d in range(3):
                at = c * 6 + d * 2
                out[c][d][1] = g[c][d][1] + lookup(table(tables.at[at]), up[d])
                out[c][d][0] = g[c][d][0] + lookup(table(tables.at[at + 1]), down[d])
        for copy in copies(step):
            copy.wait_recv()
        for c in range(2):
            from_below_y = table(y_recv.at[step, 0, pl.ds(4 * c, 4)], 4, ROWS)
            from_above_y = table(y_recv.at[step, 1, pl.ds(4 * c, 4)], 4, ROWS)
            from_below_z = table(z_recv.at[step, 0, pl.ds(c, 1)], 1, ROWS)
            from_above_z = table(z_recv.at[step, 1, pl.ds(c, 1)], 1, ROWS)
            out[c][1][1] = out[c][1][1] + lookup(from_above_y, up[1])
            out[c][2][1] = out[c][2][1] + lookup(from_above_z, up[2])
            out[c][1][0] = jnp.where(first_y, 0.0, out[c][1][0] + lookup(from_below_y, down[1]))
            out[c][2][0] = jnp.where(first_z, 0.0, out[c][2][0] + lookup(from_below_z, down[2]))
        return out

    def by_faces(number, v):
        for c in range(2):
            parts = (v[c][0][0], v[c][0][1], v[c][1][1], v[c][2][1])
            for k, part in enumerate(parts):
                vtables[number, c * 4 + k] = part
            x_low, x_up, y_up, z_up = (table(vtables.at[number, c * 4 + k]) for k in range(4))
            by_x = jnp.where(itable[1] < 0, lookup(x_low, itable[0]), lookup(x_up, itable[1]))
            by_face[number, pl.ds(c, 17, stride=2), :] = by_x[0:17]
            by_face[number, pl.ds(34 + c, ROWS, stride=2), :] = lookup(y_up, itable[3, 0:ROWS, :])
            by_face[number, pl.ds(66 + c, ROWS, stride=2), :] = lookup(z_up, itable[5, 0:ROWS, :])

    def inner(u, v):
        total = sum(u[c][d][1] * v[c][d][1] for c in range(2) for d in range(3))
        edge = sum(u[c][0][0] * v[c][0][0] for c in range(2))
        return total + jnp.where(lone_x, edge, 0.0)

    def energy(v, load, solved):
        total = sum(
            trans[c][d] * (v[c][d][0] * v[c][d][0] + v[c][d][1] * v[c][d][1])
            for c in range(2)
            for d in range(3)
        )
        return total - (load[0] * solved[0] + load[1] * solved[1])

    def scatter(send, recv, send_sem, recv_sem, peer, count, row):
        send[0:1, :] = row
        recv[count - 1 : count, :] = row
        for j in sorted(range(1, count), key=lambda j: -min(j, count - j)):
            pltpu.make_async_remote_copy(
                src_ref=send.at[pl.ds(0, 1)],
                dst_ref=recv.at[pl.ds(j - 1, 1)],
                send_sem=send_sem,
                recv_sem=recv_sem,
                device_id=peer(j),
                device_id_type=MESH,
            ).start()

    def drain(buffer, sem, count):
        rows = buffer.at[pl.ds(0, count - 1)]
        pltpu.make_async_copy(rows, rows, sem).wait()

    def flat_start(k, row):
        scatter(a_send.at[k], a_recv.at[k], a_send_sem.at[k], a_recv_sem.at[k], flat_peer, n_flat, row)

    def flat_done(k):
        drain(a_recv.at[k], a_recv_sem.at[k], n_flat)
        return jnp.sum(a_recv[k], axis=0, keepdims=True)

    def deep_start(k, row):
        scatter(b_send.at[k], b_recv.at[k], b_send_sem.at[k], b_recv_sem.at[k], deep_peer, n_deep, row)

    def deep_done(k):
        drain(b_recv.at[k], b_recv_sem.at[k], n_deep)
        return jnp.sum(b_recv[k], axis=0, keepdims=True)

    b = assemble(0, rhs_g)

    load_b = face_load(b)
    inside_b = solve(load_b)
    g_b = contributions(b, inside_b)
    publish(1, g_b)
    flat_start(0, total_row([inner(b, b), energy(b, load_b, inside_b)]))
    by_faces(0, b)
    w = assemble(1, g_b)

    load_w = face_load(w)
    inside_w = solve(load_w)
    g_w = contributions(w, inside_w)
    publish(2, g_w)
    deep_start(0, flat_done(0))
    by_faces(1, w)
    ww = assemble(2, g_w)

    first = deep_done(0)
    norm_0 = pick(first, 0)
    alpha_0 = norm_0 / pick(first, 1)

    def blend(u, factor, v):
        return [
            [[u[c][d][s] - factor * v[c][d][s] for s in range(2)] for d in range(3)]
            for c in range(2)
        ]

    r = blend(b, alpha_0, w)
    s = blend(w, alpha_0, ww)
    load = face_load(s)
    flat_start(1, total_row([inner(r, r), inner(r, s), inner(s, s), energy(s, load, solve(load))]))
    load_ww = face_load(ww)
    inside_ww = solve(load_ww)
    g_ww = contributions(ww, inside_ww)
    by_faces(2, ww)
    deep_start(1, flat_done(1))
    for step in range(ROUNDS):
        for copy in copies(step):
            copy.wait_send()
    drain(a_recv.at[0], a_send_sem.at[0], n_flat)
    drain(b_recv.at[0], b_send_sem.at[0], n_deep)
    drain(a_recv.at[1], a_send_sem.at[1], n_flat)
    sums = deep_done(1)
    rr, rs, ss, sas = (pick(sums, k) for k in range(4))

    beta_0 = rr / norm_0
    alpha_1 = rr / (rs - beta_0 * rr / alpha_0)
    ws = -(rr / alpha_0 + rs) / alpha_0
    norm_2 = -alpha_1 * (rs - alpha_1 * ss - alpha_1 * beta_0 * ws)
    beta_1 = norm_2 / rr
    ratio = alpha_1 * beta_0 / alpha_0
    along = ss - alpha_1 * sas - ratio * (ws - ss)
    energy_2 = -norm_2 / alpha_1 * (1.0 + ratio) - alpha_1 * along
    alpha_2 = norm_2 / (energy_2 - beta_1 * norm_2 / alpha_1)
    on_r = alpha_1 + alpha_2 * (1.0 + beta_1)
    on_s = -alpha_2 * alpha_1
    on_b = alpha_0 + alpha_1 * beta_0 + alpha_2 * beta_1 * beta_0 + on_r
    on_w = -alpha_2 * alpha_1 * beta_0 - alpha_0 * on_r + on_s
    on_ww = -alpha_0 * on_s

    for c in range(2):
        pressure_out[pl.ds(c, ROWS, stride=2), :] = base[c] + (
            on_b * inside_b[c] + on_w * inside_w[c] + on_ww * inside_ww[c]
        )
        for d in range(3):
            for k in range(2):
                flux = on_b * g_b[c][d][k] + on_w * g_w[c][d][k] + on_ww * g_ww[c][d][k]
                flux_out[pl.ds(32 * (2 * d + k) + c, ROWS, stride=2), :] = rhs_g[c][d][k] - flux
    by_face[0] = on_b * by_face[0] + on_w * by_face[1] + on_ww * by_face[2]
    for i in range(49):
        trace_out[:, LANES * i : LANES * (i + 1)] = by_face[0, 2 * i : 2 * i + 2, :]
    drain(b_recv.at[1], b_send_sem.at[1], n_deep)


def pair_rows(array):
    return array.reshape(2, ROWS, LANES).transpose(1, 0, 2).reshape(2 * ROWS, LANES)


def solution(mesh):
    n_region, n_sub = mesh.shape["region"], mesh.shape["sub"]
    n_flat, n_deep = n_sub // 2, 2 * n_region

    def local(conn_x, conn_y, conn_z, send_y, send_z, perm, storage, sigma, source):
        vmem = pl.BlockSpec(memory_space=pltpu.VMEM)
        dma = pltpu.SemaphoreType.DMA
        sides = perm.transpose(1, 0, 2).reshape(3, 2, ROWS, LANES).transpose(0, 2, 1, 3)
        trace, pressure, flux = pl.pallas_call(
            functools.partial(kernel, n_region, n_sub),
            out_shape=(
                jax.ShapeDtypeStruct((2, NXF + 2 * E_DEV), F32),
                jax.ShapeDtypeStruct((2 * ROWS, LANES), F32),
                jax.ShapeDtypeStruct((12 * ROWS, LANES), F32),
            ),
            in_specs=[pl.BlockSpec(memory_space=pltpu.HBM)] * 9,
            out_specs=(vmem,) * 3,
            scratch_shapes=[
                pltpu.VMEM((2 * ROWS, LANES), I32),
                pltpu.VMEM((2 * ROWS, LANES), I32),
                pltpu.VMEM((2 * ROWS, LANES), I32),
                pltpu.VMEM((4, LANES), I32),
                pltpu.VMEM((1, 64), I32),
                pltpu.VMEM((6 * ROWS, LANES), F32),
                pltpu.VMEM((2 * ROWS, LANES), F32),
                pltpu.VMEM((ROWS, LANES), F32),
                pltpu.VMEM((2 * ROWS, LANES), F32),
                dma((9,)),
                pltpu.VMEM((8, LANES), I32),
                pltpu.VMEM((6, 24, LANES), I32),
                pltpu.VMEM((12, ROWS, LANES), F32),
                pltpu.VMEM((3, 8, ROWS, LANES), F32),
                pltpu.VMEM((3, 104, LANES), F32),
                pltpu.VMEM((ROUNDS, 2, 8, LANES), F32),
                pltpu.VMEM((ROUNDS, 2, 8, LANES), F32),
                pltpu.VMEM((ROUNDS, 2, 2, LANES), F32),
                pltpu.VMEM((ROUNDS, 2, 2, LANES), F32),
                dma((ROUNDS, 4)),
                dma((ROUNDS, 4)),
                pltpu.VMEM((2, 8, LANES), F32),
                pltpu.VMEM((2, n_flat, LANES), F32),
                pltpu.VMEM((2, 8, LANES), F32),
                pltpu.VMEM((2, n_deep, LANES), F32),
                dma((2,)),
                dma((2,)),
                dma((2,)),
                dma((2,)),
            ],
            compiler_params=pltpu.CompilerParams(
                collective_id=0, has_side_effects=True, vmem_limit_bytes=60 * 1024 * 1024
            ),
        )(
            pair_rows(conn_x), pair_rows(conn_y), pair_rows(conn_z),
            send_y.reshape(4, LANES), send_z.reshape(1, 64),
            sides.reshape(6 * ROWS, LANES), pair_rows(storage), sigma.reshape(ROWS, LANES),
            pair_rows(source),
        )
        pressure = pressure.reshape(ROWS, 2, LANES).transpose(1, 0, 2).reshape(2, E_DEV)
        flux = flux.reshape(6, ROWS, 2, LANES).transpose(2, 0, 1, 3).reshape(2, 6, E_DEV)
        return trace, pressure, flux

    both = ("region", "sub")
    return jax.shard_map(
        local,
        mesh=mesh,
        in_specs=(
            P(None, both), P(None, both), P(None, both), P(both), P(both),
            P(None, None, both), P(None, both), P(both), P(None, both),
        ),
        out_specs=(P(None, both), P(None, both), P(None, None, both)),
        check_vma=False,
    )
```

```python
import functools

import jax
import jax.numpy as jnp
from jax import lax
from jax.experimental import pallas as pl
from jax.experimental.pallas import tpu as pltpu
from jax.sharding import PartitionSpec as P

MESH = pl.DeviceIdType.MESH
F32 = jnp.float32
I32 = jnp.int32
ROWS = 16
LANES = 128
E_DEV = ROWS * LANES
NXF = 2176
ROUNDS = 3


def iota(shape, dim):
    return lax.broadcasted_iota(I32, shape, dim)


def inverse(pieces):
    total = None
    for ref, row, stride, count, first in pieces:
        for start in range(0, count, 2):
            spots, hits = [], []
            for i in range(start, min(start + 2, count)):
                face = ref[row + stride * i : row + stride * i + 1, :]
                cell = iota((1, LANES), 1) + (first + LANES * i)
                spots.append(jnp.where(iota((LANES, LANES), 0) == (face & 127), 1.0, 0.0))
                hit = iota((24, LANES), 0) == (face >> 7)
                low = jnp.where(hit, (cell & 127).astype(F32), 0.0)
                high = jnp.where(hit, ((cell >> 7) + 1).astype(F32), 0.0)
                hits.append(jnp.concatenate([low, high], axis=0))
            left = jnp.concatenate(hits, axis=1).astype(jnp.bfloat16)
            spot = jnp.concatenate(spots, axis=1).astype(jnp.bfloat16)
            part = lax.dot_general(left, spot, (((1,), (1,)), ((), ())), preferred_element_type=F32)
            total = part if total is None else total + part
    whole = total.astype(I32)
    return (whole[24:] - 1) * 128 + whole[:24]


def lane_gather(rows, lane):
    numbers = lax.GatherDimensionNumbers(
        offset_dims=(),
        collapsed_slice_dims=(1,),
        start_index_map=(1,),
        operand_batching_dims=(0,),
        start_indices_batching_dims=(0,),
    )
    return lax.gather(
        rows, lane[..., None], numbers, (1, 1), mode=lax.GatherScatterMode.PROMISE_IN_BOUNDS
    )


def lookup(rows, index, start=None):
    lane, high = index & 127, index >> 7
    out = start
    for number, row in rows:
        wide = jnp.broadcast_to(row, index.shape)
        found = lane_gather(wide, lane)
        out = jnp.where(high == number, found, jnp.zeros_like(found) if out is None else out)
    return out


def table(ref, count=ROWS, first=0):
    return [(first + h, ref[h : h + 1, :]) for h in range(count)]


def total_row(parts):
    lane = iota((1, LANES), 1)
    row = jnp.zeros((1, LANES), F32)
    for number, part in enumerate(parts):
        flat = jnp.sum(part, axis=0, keepdims=True)
        row = jnp.where(lane == number, jnp.sum(flat, axis=1, keepdims=True), row)
    return row


def pick(row, number):
    return jnp.sum(jnp.where(iota((1, LANES), 1) == number, row, 0.0), axis=1, keepdims=True)


def kernel(
    n_region, n_sub,
    conn_x_in, conn_y_in, conn_z_in, send_y, send_z, perm_in, storage_in, sigma_ref, source_in,
    trace_out, pressure_out, flux_out,
    conn_x, conn_y, conn_z, perm, storage, source,
    zlist, itable, tables, sides, vtables, by_face, near_cells, far_cells, z_cells,
    near_send, near_recv, z_send, z_recv, far_send, far_recv, terms_send, terms_recv, far_next,
    near_sems, z_sems, far_sems,
    a_send, a_recv, b_send, b_recv, a_send_sem, a_recv_sem, b_send_sem, b_recv_sem,
):
    region, sub = lax.axis_index("region"), lax.axis_index("sub")
    n_flat, n_deep = n_sub // 2, 2 * n_region
    core, deep = lax.rem(sub, 2), lax.rem(lax.div(sub, 2), 2)
    flat_me = lax.div(sub, 4) * 2 + core
    deep_me = deep * n_region + region
    upper = core == 1
    far_peer, near_peer = lax.rem(sub + n_sub + 2 * core - 1, n_sub), sub + 1 - 2 * core
    region_up, region_down = lax.rem(region + 1, n_region), lax.rem(region + n_region - 1, n_region)

    def flat_peer(offset):
        peer = lax.rem(flat_me + offset, n_flat)
        return (region, lax.div(peer, 2) * 4 + deep * 2 + lax.rem(peer, 2))

    def deep_peer(offset):
        peer = lax.rem(deep_me + offset, n_deep)
        return (lax.rem(peer, n_region), sub - deep * 2 + lax.div(peer, n_region) * 2)

    barrier = pltpu.get_barrier_semaphore()

    def greet(device):
        pl.semaphore_signal(barrier, inc=1, device_id=device, device_id_type=MESH)

    greet((region, far_peer))
    for j in sorted(range(1, n_deep), key=lambda j: -min(j, n_deep - j)):
        greet(deep_peer(j))
    for j in range(1, n_flat):
        greet(flat_peer(j))

    def lanes(i):
        return slice(LANES * i, LANES * (i + 1))

    for there, here in (
        (conn_y_in, conn_y), (conn_z_in, conn_z), (conn_x_in, conn_x),
        (storage_in, storage), (source_in, source),
    ):
        for i in range(ROWS):
            here[2 * i : 2 * i + 2, :] = there[:, lanes(i)]
    for c in range(2):
        for i in range(ROWS):
            perm[pl.ds(2 * i + c, 3, stride=32), :] = perm_in[c, :, lanes(i)]

    def pair(ref, first=0):
        return [ref[pl.ds(first + k, ROWS, stride=2), :] for k in range(2)]

    by_side = [pair(perm, 32 * d) for d in range(3)]
    trans = [[2.0 * by_side[d][c] for d in range(3)] for c in range(2)]
    store, origin, sigma = pair(storage), pair(source), sigma_ref[...]

    diag = [2.0 * (trans[c][0] + trans[c][1] + trans[c][2]) + store[c] + sigma for c in range(2)]
    determ = diag[0] * diag[1] - sigma * sigma
    solve_00, solve_01, solve_11 = diag[1] / determ, sigma / determ, diag[0] / determ

    def solve(load):
        return (solve_00 * load[0] + solve_01 * load[1], solve_01 * load[0] + solve_11 * load[1])

    def face_load(v):
        return [
            sum(trans[c][d] * (v[c][d][0] + v[c][d][1]) for d in range(3)) for c in range(2)
        ]

    def contributions(v, inner):
        return [
            [[trans[c][d] * (v[c][d][s] - inner[c]) for s in range(2)] for d in range(3)]
            for c in range(2)
        ]

    base = solve(origin)
    rhs_g = [[[trans[c][d] * base[c]] * 2 for d in range(3)] for c in range(2)]

    def at_face(which, face, count=ROWS):
        return lookup(table(itable.at[which], count), face, jnp.full(face.shape, -1, I32))

    def own(which, face):
        return jnp.where(face >= E_DEV, face, at_face(which, face))

    zlist[0:1, :] = jnp.full((1, LANES), -1, I32)
    zlist[0:1, 0:64] = send_z[...]
    itable[2] = inverse([(conn_y, 0, 2, ROWS, 0), (send_y, 0, 1, 4, E_DEV)])
    itable[3] = inverse([(conn_y, 1, 2, ROWS, 0)])
    itable[4] = inverse([(conn_z, 0, 2, ROWS, 0), (zlist, 0, 1, 1, E_DEV)])
    itable[5] = inverse([(conn_z, 1, 2, ROWS, 0)])
    up_y_cells = at_face(3, send_y[...])
    down_y_cells = itable[2, ROWS : ROWS + 4, :]
    up_z_cells = at_face(5, zlist[0:1, :])
    down_z_cells = itable[4, ROWS : ROWS + 1, :]

    def by_core(if_upper, if_lower):
        return jnp.where(upper, if_upper, if_lower)

    for c in range(2):
        far_cells[4 * c : 4 * c + 4, :] = by_core(up_y_cells, down_y_cells)
        near_cells[4 * c : 4 * c + 4, :] = by_core(down_y_cells, up_y_cells)
        z_cells[c : c + 1, :] = up_z_cells
        z_cells[2 + c : 3 + c, :] = down_z_cells

    def remote(send, recv, sems, device):
        return pltpu.make_async_remote_copy(
            src_ref=send,
            dst_ref=recv,
            send_sem=sems.at[0],
            recv_sem=sems.at[1],
            device_id=device,
            device_id_type=MESH,
        )

    def copies(step):
        near, along = near_sems.at[step], z_sems.at[step]
        return [
            remote(near_send.at[step], near_recv.at[step], near, (region, near_peer)),
            remote(z_send.at[step, 0], z_recv.at[step, 0], along.at[0], (region_up, sub)),
            remote(z_send.at[step, 1], z_recv.at[step, 1], along.at[1], (region_down, sub)),
        ]

    far_first = remote(
        far_send.at[0, pl.ds(0, 8)], far_recv.at[0, pl.ds(0, 8)], far_sems.at[0], (region, far_peer)
    )
    far_second = remote(far_send.at[1], far_recv.at[1], far_sems.at[1], (region, far_peer))
    far_terms = remote(terms_send, terms_recv, far_sems.at[2], (region, far_peer))

    def side_values(at, cells, pair):
        for c in range(2):
            sides[at + c, 0:ROWS, :] = pair[c]
        second = iota((8, LANES), 0) >= 4
        rows = [
            (h, jnp.where(second, sides[at + 1, h : h + 1, :], sides[at, h : h + 1, :]))
            for h in range(ROWS)
        ]
        return lookup(rows, cells[...])

    def fill_far(step, g):
        pair = [by_core(g[c][1][1], g[c][1][0]) for c in range(2)]
        far_send[step, 0:8, :] = side_values(0, far_cells, pair)

    def fill_near(step, g):
        pair = [by_core(g[c][1][0], g[c][1][1]) for c in range(2)]
        near_send[step] = side_values(2, near_cells, pair)
        for s in range(2):
            for c in range(2):
                sides[4, pl.ds(2 - 2 * s + c, ROWS, stride=4), :] = g[c][2][s]
        rows = [(h, sides[4, 4 * h : 4 * h + 4, :]) for h in range(ROWS)]
        z_rows = lookup(rows, z_cells[0:4, :])
        z_send[step, 0] = z_rows[0:2]
        z_send[step, 1] = z_rows[2:4]

    def start(step):
        for copy in copies(step):
            copy.start()

    def keep(g):
        for d in (1, 2, 0):
            for c in range(2):
                for s in range(2):
                    tables[c * 6 + d * 2 + s] = g[c][d][s]

    greetings = 1 + (n_flat - 1) + (n_deep - 1)
    fill_far(0, rhs_g)
    fill_near(0, rhs_g)
    pl.semaphore_wait(barrier, greetings)
    far_first.start()
    start(0)
    keep(rhs_g)
    terms_send[0:8, :] = side_values(5, far_cells, [trans[c][1] for c in range(2)])
    terms_send[8:16, :] = side_values(7, far_cells, (solve_00, solve_01))
    terms_send[16:24, :] = side_values(9, far_cells, (solve_11, solve_11))
    far_terms.start()

    itable[0] = inverse([(conn_x, 0, 2, ROWS, 0)])
    itable[1] = inverse([(conn_x, 1, 2, ROWS, 0)])
    faces_x, faces_y, faces_z = pair(conn_x), pair(conn_y), pair(conn_z)
    up = [at_face(0, faces_x[1], 17), at_face(2, faces_y[1]), at_face(4, faces_z[1])]
    down = [at_face(1, faces_x[0], 17), own(3, faces_y[0]), own(5, faces_z[0])]
    last_z = region == n_region - 1
    up[2] = jnp.where(jnp.logical_and(up[2] >= E_DEV, last_z), -1, up[2])
    first_y = jnp.logical_and(down[1] >= E_DEV, sub == 0)
    first_z = jnp.logical_and(down[2] >= E_DEV, region == 0)
    lone_x = down[0] < 0
    far_index = by_core(up[1], down[1]) - E_DEV
    near_index = by_core(down[1], up[1]) - E_DEV
    at_far = far_index >= 0
    far_index = jnp.where(sub == n_sub - 1, -1, far_index)

    def assemble(step, g):
        out = [[[None, None] for _ in range(3)] for _ in range(2)]
        for c in range(2):
            for d in range(3):
                at = c * 6 + d * 2
                out[c][d][1] = g[c][d][1] + lookup(table(tables.at[at]), up[d])
                out[c][d][0] = g[c][d][0] + lookup(table(tables.at[at + 1]), down[d])
        for copy in copies(step):
            copy.wait_recv()
        for c in range(2):
            near = lookup(table(near_recv.at[step, pl.ds(4 * c, 4)], 4), near_index)
            out[c][1][1] = out[c][1][1] + by_core(0.0, near)
            out[c][1][0] = out[c][1][0] + by_core(near, 0.0)
            from_below_z = table(z_recv.at[step, 0, pl.ds(c, 1)], 1, ROWS)
            from_above_z = table(z_recv.at[step, 1, pl.ds(c, 1)], 1, ROWS)
            out[c][2][1] = out[c][2][1] + lookup(from_above_z, up[2])
            out[c][2][0] = jnp.where(first_z, 0.0, out[c][2][0] + lookup(from_below_z, down[2]))
        return out

    def add_far(out, rows):
        for c in range(2):
            far = lookup(table(rows.at[pl.ds(4 * c, 4)], 4), far_index)
            out[c][1][1] = out[c][1][1] + by_core(far, 0.0)
            out[c][1][0] = jnp.where(first_y, 0.0, out[c][1][0] + by_core(0.0, far))

    def by_faces(number, v):
        for c in range(2):
            parts = (v[c][0][0], v[c][0][1], v[c][1][1], v[c][2][1])
            for k, part in enumerate(parts):
                vtables[number, c * 4 + k] = part
            x_low, x_up, y_up, z_up = (table(vtables.at[number, c * 4 + k]) for k in range(4))
            by_x = jnp.where(itable[1] < 0, lookup(x_low, itable[0]), lookup(x_up, itable[1]))
            by_face[number, pl.ds(c, 17, stride=2), :] = by_x[0:17]
            by_face[number, pl.ds(34 + c, ROWS, stride=2), :] = lookup(y_up, itable[3, 0:ROWS, :])
            by_face[number, pl.ds(66 + c, ROWS, stride=2), :] = lookup(z_up, itable[5, 0:ROWS, :])

    def inner(u, v):
        total = sum(u[c][d][1] * v[c][d][1] for c in range(2) for d in range(3))
        edge = sum(u[c][0][0] * v[c][0][0] for c in range(2))
        return total + jnp.where(lone_x, edge, 0.0)

    def energy(v, load, solved):
        total = sum(
            trans[c][d] * (v[c][d][0] * v[c][d][0] + v[c][d][1] * v[c][d][1])
            for c in range(2)
            for d in range(3)
        )
        return total - (load[0] * solved[0] + load[1] * solved[1])

    def scatter(send, recv, send_sem, recv_sem, peer, count, row):
        send[0:1, :] = row
        recv[count - 1 : count, :] = row
        for j in range(1, count):
            pltpu.make_async_remote_copy(
                src_ref=send.at[pl.ds(0, 1)],
                dst_ref=recv.at[pl.ds(j - 1, 1)],
                send_sem=send_sem,
                recv_sem=recv_sem,
                device_id=peer(j),
                device_id_type=MESH,
            ).start()

    def drain(buffer, sem, count):
        rows = buffer.at[pl.ds(0, count - 1)]
        pltpu.make_async_copy(rows, rows, sem).wait()

    def flat_start(k, row):
        scatter(a_send.at[k], a_recv.at[k], a_send_sem.at[k], a_recv_sem.at[k], flat_peer, n_flat, row)

    def flat_done(k):
        drain(a_recv.at[k], a_recv_sem.at[k], n_flat)
        return jnp.sum(a_recv[k], axis=0, keepdims=True)

    def deep_start(k, row):
        scatter(b_send.at[k], b_recv.at[k], b_send_sem.at[k], b_recv_sem.at[k], deep_peer, n_deep, row)

    def deep_done(k):
        drain(b_recv.at[k], b_recv_sem.at[k], n_deep)
        return jnp.sum(b_recv[k], axis=0, keepdims=True)

    b = assemble(0, rhs_g)
    far_first.wait_recv()
    add_far(b, far_recv.at[0])

    load_b = face_load(b)
    inside_b = solve(load_b)
    g_b = contributions(b, inside_b)
    fill_near(1, g_b)
    start(1)
    keep(g_b)
    fill_far(1, g_b)
    flat_start(0, total_row([inner(b, b), energy(b, load_b, inside_b)]))
    w = assemble(1, g_b)

    def without_far(part, here):
        return jnp.where(jnp.logical_and(at_far, here), 0.0, part)

    apart = [
        [w[c][0], [without_far(w[c][1][0], core == 0), without_far(w[c][1][1], upper)], w[c][2]]
        for c in range(2)
    ]
    far_send[1, 8:16, :] = side_values(0, far_cells, face_load(apart))
    far_second.start()
    by_faces(0, b)
    deep_start(0, flat_done(0))
    far_terms.wait_recv()
    far_second.wait_recv()
    add_far(w, far_recv.at[1])

    far_w = far_send[1, 0:8, :] + far_recv[1, 0:8, :]
    far_trans = terms_recv[0:8, :]
    far_load = far_recv[1, 8:16, :] + far_trans * far_w
    load_0, load_1 = far_load[0:4], far_load[4:8]
    term_00, term_01, term_11 = (terms_recv[k : k + 4, :] for k in (8, 12, 16))
    far_next[0:4, :] = far_trans[0:4] * (far_w[0:4] - (term_00 * load_0 + term_01 * load_1))
    far_next[4:8, :] = far_trans[4:8] * (far_w[4:8] - (term_01 * load_0 + term_11 * load_1))

    load_w = face_load(w)
    inside_w = solve(load_w)
    g_w = contributions(w, inside_w)
    fill_near(2, g_w)
    start(2)
    keep(g_w)
    ww = assemble(2, g_w)
    add_far(ww, far_next)

    first = deep_done(0)
    norm_0 = pick(first, 0)
    alpha_0 = norm_0 / pick(first, 1)

    def blend(u, factor, v):
        return [
            [[u[c][d][s] - factor * v[c][d][s] for s in range(2)] for d in range(3)]
            for c in range(2)
        ]

    r = blend(b, alpha_0, w)
    s = blend(w, alpha_0, ww)
    load = face_load(s)
    flat_start(1, total_row([inner(r, r), inner(r, s), inner(s, s), energy(s, load, solve(load))]))
    load_ww = face_load(ww)
    inside_ww = solve(load_ww)
    g_ww = contributions(ww, inside_ww)
    by_faces(1, w)
    deep_start(1, flat_done(1))
    by_faces(2, ww)
    for step in range(ROUNDS):
        for copy in copies(step):
            copy.wait_send()
    for copy in (far_first, far_second, far_terms):
        copy.wait_send()
    drain(a_recv.at[0], a_send_sem.at[0], n_flat)
    drain(b_recv.at[0], b_send_sem.at[0], n_deep)
    drain(a_recv.at[1], a_send_sem.at[1], n_flat)
    sums = deep_done(1)
    rr, rs, ss, sas = (pick(sums, k) for k in range(4))

    beta_0 = rr / norm_0
    alpha_1 = rr / (rs - beta_0 * rr / alpha_0)
    ws = -(rr / alpha_0 + rs) / alpha_0
    norm_2 = -alpha_1 * (rs - alpha_1 * ss - alpha_1 * beta_0 * ws)
    beta_1 = norm_2 / rr
    ratio = alpha_1 * beta_0 / alpha_0
    along = ss - alpha_1 * sas - ratio * (ws - ss)
    energy_2 = -norm_2 / alpha_1 * (1.0 + ratio) - alpha_1 * along
    alpha_2 = norm_2 / (energy_2 - beta_1 * norm_2 / alpha_1)
    on_r = alpha_1 + alpha_2 * (1.0 + beta_1)
    on_s = -alpha_2 * alpha_1
    on_b = alpha_0 + alpha_1 * beta_0 + alpha_2 * beta_1 * beta_0 + on_r
    on_w = -alpha_2 * alpha_1 * beta_0 - alpha_0 * on_r + on_s
    on_ww = -alpha_0 * on_s

    for c in range(2):
        pressure_out[pl.ds(c, ROWS, stride=2), :] = base[c] + (
            on_b * inside_b[c] + on_w * inside_w[c] + on_ww * inside_ww[c]
        )
        for d in range(3):
            for k in range(2):
                flux = on_b * g_b[c][d][k] + on_w * g_w[c][d][k] + on_ww * g_ww[c][d][k]
                flux_out[pl.ds(32 * (2 * d + k) + c, ROWS, stride=2), :] = rhs_g[c][d][k] - flux
    by_face[0] = on_b * by_face[0] + on_w * by_face[1] + on_ww * by_face[2]
    for i in range(49):
        trace_out[:, LANES * i : LANES * (i + 1)] = by_face[0, 2 * i : 2 * i + 2, :]
    drain(b_recv.at[1], b_send_sem.at[1], n_deep)


def solution(mesh):
    n_region, n_sub = mesh.shape["region"], mesh.shape["sub"]
    n_flat, n_deep = n_sub // 2, 2 * n_region

    def local(conn_x, conn_y, conn_z, send_y, send_z, perm, storage, sigma, source):
        vmem = pl.BlockSpec(memory_space=pltpu.VMEM)
        dma = pltpu.SemaphoreType.DMA
        trace, pressure, flux = pl.pallas_call(
            functools.partial(kernel, n_region, n_sub),
            out_shape=(
                jax.ShapeDtypeStruct((2, NXF + 2 * E_DEV), F32),
                jax.ShapeDtypeStruct((2 * ROWS, LANES), F32),
                jax.ShapeDtypeStruct((12 * ROWS, LANES), F32),
            ),
            in_specs=[vmem] * 9,
            out_specs=(vmem,) * 3,
            scratch_shapes=[
                pltpu.VMEM((2 * ROWS, LANES), I32),
                pltpu.VMEM((2 * ROWS, LANES), I32),
                pltpu.VMEM((2 * ROWS, LANES), I32),
                pltpu.VMEM((6 * ROWS, LANES), F32),
                pltpu.VMEM((2 * ROWS, LANES), F32),
                pltpu.VMEM((2 * ROWS, LANES), F32),
                pltpu.VMEM((8, LANES), I32),
                pltpu.VMEM((6, 24, LANES), I32),
                pltpu.VMEM((12, ROWS, LANES), F32),
                pltpu.VMEM((11, 4 * ROWS, LANES), F32),
                pltpu.VMEM((3, 8, ROWS, LANES), F32),
                pltpu.VMEM((3, 104, LANES), F32),
                pltpu.VMEM((8, LANES), I32),
                pltpu.VMEM((8, LANES), I32),
                pltpu.VMEM((8, LANES), I32),
                pltpu.VMEM((ROUNDS, 8, LANES), F32),
                pltpu.VMEM((ROUNDS, 8, LANES), F32),
                pltpu.VMEM((ROUNDS, 2, 2, LANES), F32),
                pltpu.VMEM((ROUNDS, 2, 2, LANES), F32),
                pltpu.VMEM((2, 16, LANES), F32),
                pltpu.VMEM((2, 16, LANES), F32),
                pltpu.VMEM((24, LANES), F32),
                pltpu.VMEM((24, LANES), F32),
                pltpu.VMEM((8, LANES), F32),
                dma((ROUNDS, 2)),
                dma((ROUNDS, 2, 2)),
                dma((3, 2)),
                pltpu.VMEM((2, 8, LANES), F32),
                pltpu.VMEM((2, n_flat, LANES), F32),
                pltpu.VMEM((2, 8, LANES), F32),
                pltpu.VMEM((2, n_deep, LANES), F32),
                dma((2,)),
                dma((2,)),
                dma((2,)),
                dma((2,)),
            ],
            compiler_params=pltpu.CompilerParams(
                collective_id=0, has_side_effects=True, vmem_limit_bytes=32 * 1024 * 1024
            ),
        )(
            conn_x, conn_y, conn_z, send_y.reshape(4, LANES), send_z.reshape(1, 64),
            perm, storage, sigma.reshape(ROWS, LANES), source,
        )
        pressure = pressure.reshape(ROWS, 2, LANES).transpose(1, 0, 2).reshape(2, E_DEV)
        flux = flux.reshape(6, ROWS, 2, LANES).transpose(2, 0, 1, 3).reshape(2, 6, E_DEV)
        return trace, pressure, flux

    both = ("region", "sub")
    return jax.shard_map(
        local,
        mesh=mesh,
        in_specs=(
            P(None, both), P(None, both), P(None, both), P(both), P(both),
            P(None, None, both), P(None, both), P(both), P(None, both),
        ),
        out_specs=(P(None, both), P(None, both), P(None, None, both)),
        check_vma=False,
    )
```

```python
import functools

import jax
import jax.numpy as jnp
from jax import lax
from jax.experimental import pallas as pl
from jax.experimental.pallas import tpu as pltpu
from jax.sharding import PartitionSpec as P

MESH = pl.DeviceIdType.MESH
F32 = jnp.float32
I32 = jnp.int32
ROWS = 16
LANES = 128
E_DEV = ROWS * LANES
NXF = 2176
ROUNDS = 3


def iota(shape, dim):
    return lax.broadcasted_iota(I32, shape, dim)


def inverse(ref, side, more=()):
    def columns(face, number):
        spot = jnp.where(iota((LANES, LANES), 0) == (face & 127), 1.0, 0.0)
        hit = iota((24, LANES), 0) == (face >> 7)
        low = jnp.where(hit, iota((1, LANES), 1).astype(F32), 0.0)
        high = jnp.where(hit, (number + 1).astype(F32), 0.0)
        return jnp.concatenate([low, high], axis=0), spot

    def part(pairs):
        left = jnp.concatenate([pair[0] for pair in pairs], axis=1).astype(jnp.bfloat16)
        right = jnp.concatenate([pair[1] for pair in pairs], axis=1).astype(jnp.bfloat16)
        return lax.dot_general(left, right, (((1,), (1,)), ((), ())), preferred_element_type=F32)

    def step(i, total):
        rows = [4 * i + u for u in range(4)]
        return total + part([columns(ref[pl.ds(2 * r + side, 1), :], r) for r in rows])

    total = lax.fori_loop(0, ROWS // 4, step, jnp.zeros((48, LANES), F32))
    for other, count in more:
        total = total + part(
            [columns(other[h : h + 1, :], jnp.int32(ROWS + h)) for h in range(count)]
        )
    whole = total.astype(I32)
    return (whole[24:] - 1) * 128 + whole[:24]


def lane_gather(rows, lane):
    numbers = lax.GatherDimensionNumbers(
        offset_dims=(),
        collapsed_slice_dims=(1,),
        start_index_map=(1,),
        operand_batching_dims=(0,),
        start_indices_batching_dims=(0,),
    )
    return lax.gather(
        rows, lane[..., None], numbers, (1, 1), mode=lax.GatherScatterMode.PROMISE_IN_BOUNDS
    )


def lookup(rows, index, start=None):
    lane, high = index & 127, index >> 7
    out = start
    for number, row in rows:
        wide = jnp.broadcast_to(row, index.shape)
        found = lane_gather(wide, lane)
        out = jnp.where(high == number, found, jnp.zeros_like(found) if out is None else out)
    return out


def lookup_all(jobs, missing):
    lanes = [index & 127 for _, index in jobs]
    highs = [index >> 7 for _, index in jobs]

    def step(i, found):
        for u in range(4):
            row = 4 * i + u
            values = [
                lane_gather(jnp.broadcast_to(ref[pl.ds(row, 1), :], index.shape), lane)
                for (ref, index), lane in zip(jobs, lanes)
            ]
            found = [jnp.where(high == row, v, f) for high, v, f in zip(highs, values, found)]
        return found

    return lax.fori_loop(0, ROWS // 4, step, [jnp.full(i.shape, missing, r.dtype) for r, i in jobs])


def table(ref, count=ROWS, first=0):
    return [(first + h, ref[h : h + 1, :]) for h in range(count)]


def total_row(parts):
    lane = iota((1, LANES), 1)
    row = jnp.zeros((1, LANES), F32)
    for number, part in enumerate(parts):
        flat = jnp.sum(part, axis=0, keepdims=True)
        row = jnp.where(lane == number, jnp.sum(flat, axis=1, keepdims=True), row)
    return row


def pick(row, number):
    return jnp.sum(jnp.where(iota((1, LANES), 1) == number, row, 0.0), axis=1, keepdims=True)


def kernel(
    n_region, n_sub,
    conn_x_in, conn_y_in, conn_z_in, send_y, send_z, perm_in, storage_in, sigma_ref, source_in,
    trace_out, pressure_out, flux_out,
    conn_x, conn_y, conn_z, perm, storage, source,
    zlist, itable, tables, sides, vtables, by_face, near_cells, far_cells, z_cells,
    near_send, near_recv, z_send, z_recv, far_send, far_recv, terms_send, terms_recv, far_next,
    near_sems, z_sems, far_sems,
    a_send, a_recv, b_send, b_recv, a_send_sem, a_recv_sem, b_send_sem, b_recv_sem,
):
    region, sub = lax.axis_index("region"), lax.axis_index("sub")
    n_flat, n_deep = n_sub // 2, 2 * n_region
    core, deep = lax.rem(sub, 2), lax.rem(lax.div(sub, 2), 2)
    flat_me = lax.div(sub, 4) * 2 + core
    deep_me = deep * n_region + region
    upper = core == 1
    far_peer, near_peer = lax.rem(sub + n_sub + 2 * core - 1, n_sub), sub + 1 - 2 * core
    region_up, region_down = lax.rem(region + 1, n_region), lax.rem(region + n_region - 1, n_region)

    def flat_peer(offset):
        peer = lax.rem(flat_me + offset, n_flat)
        return (region, lax.div(peer, 2) * 4 + deep * 2 + lax.rem(peer, 2))

    def deep_peer(offset):
        peer = lax.rem(deep_me + offset, n_deep)
        return (lax.rem(peer, n_region), sub - deep * 2 + lax.div(peer, n_region) * 2)

    barrier = pltpu.get_barrier_semaphore()

    def greet(device):
        pl.semaphore_signal(barrier, inc=1, device_id=device, device_id_type=MESH)

    greet((region, far_peer))
    lax.fori_loop(1, n_deep, lambda j, c: (greet(deep_peer(j)), c)[1], 0)
    lax.fori_loop(1, n_flat, lambda j, c: (greet(flat_peer(j)), c)[1], 0)

    def lanes(i):
        return slice(LANES * i, LANES * (i + 1))

    for there, here in (
        (conn_y_in, conn_y), (conn_z_in, conn_z), (conn_x_in, conn_x),
        (storage_in, storage), (source_in, source),
    ):
        for i in range(ROWS):
            here[2 * i : 2 * i + 2, :] = there[:, lanes(i)]
    for c in range(2):
        for i in range(ROWS):
            perm[pl.ds(2 * i + c, 3, stride=32), :] = perm_in[c, :, lanes(i)]

    def pair(ref, first=0):
        return [ref[pl.ds(first + k, ROWS, stride=2), :] for k in range(2)]

    by_side = [pair(perm, 32 * d) for d in range(3)]
    trans = [[2.0 * by_side[d][c] for d in range(3)] for c in range(2)]
    store, origin, sigma = pair(storage), pair(source), sigma_ref[...]

    diag = [2.0 * (trans[c][0] + trans[c][1] + trans[c][2]) + store[c] + sigma for c in range(2)]
    determ = diag[0] * diag[1] - sigma * sigma
    solve_00, solve_01, solve_11 = diag[1] / determ, sigma / determ, diag[0] / determ

    def solve(load):
        return (solve_00 * load[0] + solve_01 * load[1], solve_01 * load[0] + solve_11 * load[1])

    def face_load(v):
        return [
            sum(trans[c][d] * (v[c][d][0] + v[c][d][1]) for d in range(3)) for c in range(2)
        ]

    def contributions(v, inner):
        return [
            [[trans[c][d] * (v[c][d][s] - inner[c]) for s in range(2)] for d in range(3)]
            for c in range(2)
        ]

    base = solve(origin)
    rhs_g = [[[trans[c][d] * base[c]] * 2 for d in range(3)] for c in range(2)]

    def at_face(which, face, count=ROWS):
        return lookup(table(itable.at[which], count), face, jnp.full(face.shape, -1, I32))

    zlist[0:1, :] = jnp.full((1, LANES), -1, I32)
    zlist[0:1, 0:64] = send_z[...]
    itable[2] = inverse(conn_y, 0, [(send_y, 4)])
    itable[3] = inverse(conn_y, 1)
    itable[4] = inverse(conn_z, 0, [(zlist, 1)])
    itable[5] = inverse(conn_z, 1)
    up_y_cells = at_face(3, send_y[...])
    down_y_cells = itable[2, ROWS : ROWS + 4, :]
    up_z_cells = at_face(5, zlist[0:1, :])
    down_z_cells = itable[4, ROWS : ROWS + 1, :]

    def by_core(if_upper, if_lower):
        return jnp.where(upper, if_upper, if_lower)

    for c in range(2):
        far_cells[4 * c : 4 * c + 4, :] = by_core(up_y_cells, down_y_cells)
        near_cells[4 * c : 4 * c + 4, :] = by_core(down_y_cells, up_y_cells)
        z_cells[c : c + 1, :] = up_z_cells
        z_cells[2 + c : 3 + c, :] = down_z_cells

    def remote(send, recv, sems, device):
        return pltpu.make_async_remote_copy(
            src_ref=send,
            dst_ref=recv,
            send_sem=sems.at[0],
            recv_sem=sems.at[1],
            device_id=device,
            device_id_type=MESH,
        )

    def copies(step):
        near, along = near_sems.at[step], z_sems.at[step]
        return [
            remote(near_send.at[step], near_recv.at[step], near, (region, near_peer)),
            remote(z_send.at[step, 0], z_recv.at[step, 0], along.at[0], (region_up, sub)),
            remote(z_send.at[step, 1], z_recv.at[step, 1], along.at[1], (region_down, sub)),
        ]

    far_first = remote(
        far_send.at[0, pl.ds(0, 8)], far_recv.at[0, pl.ds(0, 8)], far_sems.at[0], (region, far_peer)
    )
    far_second = remote(far_send.at[1], far_recv.at[1], far_sems.at[1], (region, far_peer))
    far_terms = remote(terms_send, terms_recv, far_sems.at[2], (region, far_peer))

    def side_values(at, cells, pair):
        for c in range(2):
            sides[at + c, 0:ROWS, :] = pair[c]
        second = iota((8, LANES), 0) >= 4
        rows = [
            (h, jnp.where(second, sides[at + 1, h : h + 1, :], sides[at, h : h + 1, :]))
            for h in range(ROWS)
        ]
        return lookup(rows, cells[...])

    def fill_far(step, g):
        pair = [by_core(g[c][1][1], g[c][1][0]) for c in range(2)]
        far_send[step, 0:8, :] = side_values(0, far_cells, pair)

    def fill_near(step, g):
        pair = [by_core(g[c][1][0], g[c][1][1]) for c in range(2)]
        near_send[step] = side_values(2, near_cells, pair)
        for s in range(2):
            for c in range(2):
                sides[4, pl.ds(2 - 2 * s + c, ROWS, stride=4), :] = g[c][2][s]
        rows = [(h, sides[4, 4 * h : 4 * h + 4, :]) for h in range(ROWS)]
        z_rows = lookup(rows, z_cells[0:4, :])
        z_send[step, 0] = z_rows[0:2]
        z_send[step, 1] = z_rows[2:4]

    def start(step):
        for copy in copies(step):
            copy.start()

    def keep(g):
        for d in (1, 2, 0):
            for c in range(2):
                for s in range(2):
                    tables[c * 6 + d * 2 + s] = g[c][d][s]

    greetings = 1 + (n_flat - 1) + (n_deep - 1)
    fill_far(0, rhs_g)
    fill_near(0, rhs_g)
    pl.semaphore_wait(barrier, greetings)
    far_first.start()
    start(0)
    keep(rhs_g)
    terms_send[0:8, :] = side_values(5, far_cells, [trans[c][1] for c in range(2)])
    terms_send[8:16, :] = side_values(7, far_cells, (solve_00, solve_01))
    terms_send[16:24, :] = side_values(9, far_cells, (solve_11, solve_11))
    far_terms.start()

    itable[0] = inverse(conn_x, 0)
    itable[1] = inverse(conn_x, 1)
    faces_x, faces_y, faces_z = pair(conn_x), pair(conn_y), pair(conn_z)
    asked = (faces_x[1], faces_y[1], faces_z[1], faces_x[0], faces_y[0], faces_z[0])
    found = lookup_all([(itable.at[k], face) for k, face in zip((0, 2, 4, 1, 3, 5), asked)], -1)
    up, down = list(found[:3]), list(found[3:])
    up[0] = lookup([(16, itable[0, 16:17, :])], asked[0], up[0])
    down[0] = lookup([(16, itable[1, 16:17, :])], asked[3], down[0])
    down[1] = jnp.where(asked[4] >= E_DEV, asked[4], down[1])
    down[2] = jnp.where(asked[5] >= E_DEV, asked[5], down[2])
    last_z = region == n_region - 1
    up[2] = jnp.where(jnp.logical_and(up[2] >= E_DEV, last_z), -1, up[2])
    first_y = jnp.logical_and(down[1] >= E_DEV, sub == 0)
    first_z = jnp.logical_and(down[2] >= E_DEV, region == 0)
    lone_x = down[0] < 0
    far_index = by_core(up[1], down[1]) - E_DEV
    near_index = by_core(down[1], up[1]) - E_DEV
    at_far = far_index >= 0
    far_index = jnp.where(sub == n_sub - 1, -1, far_index)

    def assemble(step, g):
        out = [[[None, None] for _ in range(3)] for _ in range(2)]
        across = lookup_all(
            [(tables.at[k], (up if k % 2 == 0 else down)[k % 6 // 2]) for k in range(12)], 0.0
        )
        for c in range(2):
            for d in range(3):
                at = c * 6 + d * 2
                out[c][d][1] = g[c][d][1] + across[at]
                out[c][d][0] = g[c][d][0] + across[at + 1]
        for copy in copies(step):
            copy.wait_recv()
        for c in range(2):
            near = lookup(table(near_recv.at[step, pl.ds(4 * c, 4)], 4), near_index)
            out[c][1][1] = out[c][1][1] + by_core(0.0, near)
            out[c][1][0] = out[c][1][0] + by_core(near, 0.0)
            from_below_z = table(z_recv.at[step, 0, pl.ds(c, 1)], 1, ROWS)
            from_above_z = table(z_recv.at[step, 1, pl.ds(c, 1)], 1, ROWS)
            out[c][2][1] = out[c][2][1] + lookup(from_above_z, up[2])
            out[c][2][0] = jnp.where(first_z, 0.0, out[c][2][0] + lookup(from_below_z, down[2]))
        return out

    def add_far(out, rows):
        for c in range(2):
            far = lookup(table(rows.at[pl.ds(4 * c, 4)], 4), far_index)
            out[c][1][1] = out[c][1][1] + by_core(far, 0.0)
            out[c][1][0] = jnp.where(first_y, 0.0, out[c][1][0] + by_core(0.0, far))

    def by_faces(number, v):
        jobs = []
        for c in range(2):
            parts = (v[c][0][0], v[c][0][1], v[c][1][1], v[c][2][1])
            for k, part in enumerate(parts):
                vtables[number, c * 4 + k] = part
                index = (itable[0], itable[1], itable[3, 0:ROWS, :], itable[5, 0:ROWS, :])[k]
                jobs.append((vtables.at[number, c * 4 + k], index))
        found = lookup_all(jobs, 0.0)
        for c in range(2):
            x_low, x_up, y_up, z_up = found[4 * c : 4 * c + 4]
            by_x = jnp.where(itable[1] < 0, x_low, x_up)
            by_face[number, pl.ds(c, 17, stride=2), :] = by_x[0:17]
            by_face[number, pl.ds(34 + c, ROWS, stride=2), :] = y_up
            by_face[number, pl.ds(66 + c, ROWS, stride=2), :] = z_up

    def inner(u, v):
        total = sum(u[c][d][1] * v[c][d][1] for c in range(2) for d in range(3))
        edge = sum(u[c][0][0] * v[c][0][0] for c in range(2))
        return total + jnp.where(lone_x, edge, 0.0)

    def energy(v, load, solved):
        total = sum(
            trans[c][d] * (v[c][d][0] * v[c][d][0] + v[c][d][1] * v[c][d][1])
            for c in range(2)
            for d in range(3)
        )
        return total - (load[0] * solved[0] + load[1] * solved[1])

    def scatter(send, recv, send_sem, recv_sem, peer, count, row):
        send[0:1, :] = row
        recv[count - 1 : count, :] = row

        def one(j, carry):
            pltpu.make_async_remote_copy(
                src_ref=send.at[pl.ds(0, 1)],
                dst_ref=recv.at[pl.ds(j - 1, 1)],
                send_sem=send_sem,
                recv_sem=recv_sem,
                device_id=peer(j),
                device_id_type=MESH,
            ).start()
            return carry

        lax.fori_loop(1, count, one, 0)

    def drain(buffer, sem, count):
        rows = buffer.at[pl.ds(0, count - 1)]
        pltpu.make_async_copy(rows, rows, sem).wait()

    def flat_start(k, row):
        scatter(a_send.at[k], a_recv.at[k], a_send_sem.at[k], a_recv_sem.at[k], flat_peer, n_flat, row)

    def flat_done(k):
        drain(a_recv.at[k], a_recv_sem.at[k], n_flat)
        return jnp.sum(a_recv[k], axis=0, keepdims=True)

    def deep_start(k, row):
        scatter(b_send.at[k], b_recv.at[k], b_send_sem.at[k], b_recv_sem.at[k], deep_peer, n_deep, row)

    def deep_done(k):
        drain(b_recv.at[k], b_recv_sem.at[k], n_deep)
        return jnp.sum(b_recv[k], axis=0, keepdims=True)

    b = assemble(0, rhs_g)
    far_first.wait_recv()
    add_far(b, far_recv.at[0])

    load_b = face_load(b)
    inside_b = solve(load_b)
    g_b = contributions(b, inside_b)
    fill_near(1, g_b)
    start(1)
    keep(g_b)
    fill_far(1, g_b)
    flat_start(0, total_row([inner(b, b), energy(b, load_b, inside_b)]))
    w = assemble(1, g_b)

    def without_far(part, here):
        return jnp.where(jnp.logical_and(at_far, here), 0.0, part)

    apart = [
        [w[c][0], [without_far(w[c][1][0], core == 0), without_far(w[c][1][1], upper)], w[c][2]]
        for c in range(2)
    ]
    far_send[1, 8:16, :] = side_values(0, far_cells, face_load(apart))
    far_second.start()
    by_faces(0, b)
    deep_start(0, flat_done(0))
    far_terms.wait_recv()
    far_second.wait_recv()
    add_far(w, far_recv.at[1])

    far_w = far_send[1, 0:8, :] + far_recv[1, 0:8, :]
    far_trans = terms_recv[0:8, :]
    far_load = far_recv[1, 8:16, :] + far_trans * far_w
    load_0, load_1 = far_load[0:4], far_load[4:8]
    term_00, term_01, term_11 = (terms_recv[k : k + 4, :] for k in (8, 12, 16))
    far_next[0:4, :] = far_trans[0:4] * (far_w[0:4] - (term_00 * load_0 + term_01 * load_1))
    far_next[4:8, :] = far_trans[4:8] * (far_w[4:8] - (term_01 * load_0 + term_11 * load_1))

    load_w = face_load(w)
    inside_w = solve(load_w)
    g_w = contributions(w, inside_w)
    fill_near(2, g_w)
    start(2)
    keep(g_w)
    ww = assemble(2, g_w)
    add_far(ww, far_next)

    first = deep_done(0)
    norm_0 = pick(first, 0)
    alpha_0 = norm_0 / pick(first, 1)

    def blend(u, factor, v):
        return [
            [[u[c][d][s] - factor * v[c][d][s] for s in range(2)] for d in range(3)]
            for c in range(2)
        ]

    r = blend(b, alpha_0, w)
    s = blend(w, alpha_0, ww)
    load = face_load(s)
    flat_start(1, total_row([inner(r, r), inner(r, s), inner(s, s), energy(s, load, solve(load))]))
    load_ww = face_load(ww)
    inside_ww = solve(load_ww)
    g_ww = contributions(ww, inside_ww)
    by_faces(1, w)
    deep_start(1, flat_done(1))
    by_faces(2, ww)
    for step in range(ROUNDS):
        for copy in copies(step):
            copy.wait_send()
    for copy in (far_first, far_second, far_terms):
        copy.wait_send()
    drain(a_recv.at[0], a_send_sem.at[0], n_flat)
    drain(b_recv.at[0], b_send_sem.at[0], n_deep)
    drain(a_recv.at[1], a_send_sem.at[1], n_flat)
    sums = deep_done(1)
    rr, rs, ss, sas = (pick(sums, k) for k in range(4))

    beta_0 = rr / norm_0
    alpha_1 = rr / (rs - beta_0 * rr / alpha_0)
    ws = -(rr / alpha_0 + rs) / alpha_0
    norm_2 = -alpha_1 * (rs - alpha_1 * ss - alpha_1 * beta_0 * ws)
    beta_1 = norm_2 / rr
    ratio = alpha_1 * beta_0 / alpha_0
    along = ss - alpha_1 * sas - ratio * (ws - ss)
    energy_2 = -norm_2 / alpha_1 * (1.0 + ratio) - alpha_1 * along
    alpha_2 = norm_2 / (energy_2 - beta_1 * norm_2 / alpha_1)
    on_r = alpha_1 + alpha_2 * (1.0 + beta_1)
    on_s = -alpha_2 * alpha_1
    on_b = alpha_0 + alpha_1 * beta_0 + alpha_2 * beta_1 * beta_0 + on_r
    on_w = -alpha_2 * alpha_1 * beta_0 - alpha_0 * on_r + on_s
    on_ww = -alpha_0 * on_s

    for c in range(2):
        pressure_out[pl.ds(c, ROWS, stride=2), :] = base[c] + (
            on_b * inside_b[c] + on_w * inside_w[c] + on_ww * inside_ww[c]
        )
        for d in range(3):
            for k in range(2):
                flux = on_b * g_b[c][d][k] + on_w * g_w[c][d][k] + on_ww * g_ww[c][d][k]
                flux_out[pl.ds(32 * (2 * d + k) + c, ROWS, stride=2), :] = rhs_g[c][d][k] - flux
    by_face[0] = on_b * by_face[0] + on_w * by_face[1] + on_ww * by_face[2]
    for i in range(49):
        trace_out[:, LANES * i : LANES * (i + 1)] = by_face[0, 2 * i : 2 * i + 2, :]
    drain(b_recv.at[1], b_send_sem.at[1], n_deep)


def solution(mesh):
    n_region, n_sub = mesh.shape["region"], mesh.shape["sub"]
    n_flat, n_deep = n_sub // 2, 2 * n_region

    def local(conn_x, conn_y, conn_z, send_y, send_z, perm, storage, sigma, source):
        vmem = pl.BlockSpec(memory_space=pltpu.VMEM)
        dma = pltpu.SemaphoreType.DMA
        trace, pressure, flux = pl.pallas_call(
            functools.partial(kernel, n_region, n_sub),
            out_shape=(
                jax.ShapeDtypeStruct((2, NXF + 2 * E_DEV), F32),
                jax.ShapeDtypeStruct((2 * ROWS, LANES), F32),
                jax.ShapeDtypeStruct((12 * ROWS, LANES), F32),
            ),
            in_specs=[vmem] * 9,
            out_specs=(vmem,) * 3,
            scratch_shapes=[
                pltpu.VMEM((2 * ROWS, LANES), I32),
                pltpu.VMEM((2 * ROWS, LANES), I32),
                pltpu.VMEM((2 * ROWS, LANES), I32),
                pltpu.VMEM((6 * ROWS, LANES), F32),
                pltpu.VMEM((2 * ROWS, LANES), F32),
                pltpu.VMEM((2 * ROWS, LANES), F32),
                pltpu.VMEM((8, LANES), I32),
                pltpu.VMEM((6, 24, LANES), I32),
                pltpu.VMEM((12, ROWS, LANES), F32),
                pltpu.VMEM((11, 4 * ROWS, LANES), F32),
                pltpu.VMEM((3, 8, ROWS, LANES), F32),
                pltpu.VMEM((3, 104, LANES), F32),
                pltpu.VMEM((8, LANES), I32),
                pltpu.VMEM((8, LANES), I32),
                pltpu.VMEM((8, LANES), I32),
                pltpu.VMEM((ROUNDS, 8, LANES), F32),
                pltpu.VMEM((ROUNDS, 8, LANES), F32),
                pltpu.VMEM((ROUNDS, 2, 2, LANES), F32),
                pltpu.VMEM((ROUNDS, 2, 2, LANES), F32),
                pltpu.VMEM((2, 16, LANES), F32),
                pltpu.VMEM((2, 16, LANES), F32),
                pltpu.VMEM((24, LANES), F32),
                pltpu.VMEM((24, LANES), F32),
                pltpu.VMEM((8, LANES), F32),
                dma((ROUNDS, 2)),
                dma((ROUNDS, 2, 2)),
                dma((3, 2)),
                pltpu.VMEM((2, 8, LANES), F32),
                pltpu.VMEM((2, n_flat, LANES), F32),
                pltpu.VMEM((2, 8, LANES), F32),
                pltpu.VMEM((2, n_deep, LANES), F32),
                dma((2,)),
                dma((2,)),
                dma((2,)),
                dma((2,)),
            ],
            compiler_params=pltpu.CompilerParams(
                collective_id=0, has_side_effects=True, vmem_limit_bytes=32 * 1024 * 1024
            ),
        )(
            conn_x, conn_y, conn_z, send_y.reshape(4, LANES), send_z.reshape(1, 64),
            perm, storage, sigma.reshape(ROWS, LANES), source,
        )
        pressure = pressure.reshape(ROWS, 2, LANES).transpose(1, 0, 2).reshape(2, E_DEV)
        flux = flux.reshape(6, ROWS, 2, LANES).transpose(2, 0, 1, 3).reshape(2, 6, E_DEV)
        return trace, pressure, flux

    both = ("region", "sub")
    return jax.shard_map(
        local,
        mesh=mesh,
        in_specs=(
            P(None, both), P(None, both), P(None, both), P(both), P(both),
            P(None, None, both), P(None, both), P(both), P(None, both),
        ),
        out_specs=(P(None, both), P(None, both), P(None, None, both)),
        check_vma=False,
    )
```

```python
import functools
import math

import jax
import jax.numpy as jnp
from jax import lax
from jax.experimental import pallas as pl
from jax.experimental.pallas import tpu as pltpu
from jax.sharding import PartitionSpec as P

MESH = pl.DeviceIdType.MESH
F32 = jnp.float32
I32 = jnp.int32
ROWS = 16
LANES = 128
E_DEV = ROWS * LANES
NXF = 2176
ROUNDS = 3


def iota(shape, dim):
    return lax.broadcasted_iota(I32, shape, dim)


def inverse(ref, side, more=()):
    def columns(face, number):
        spot = jnp.where(iota((LANES, LANES), 0) == (face & 127), 1.0, 0.0)
        hit = iota((24, LANES), 0) == (face >> 7)
        low = jnp.where(hit, iota((1, LANES), 1).astype(F32), 0.0)
        high = jnp.where(hit, (number + 1).astype(F32), 0.0)
        return jnp.concatenate([low, high], axis=0), spot

    def part(pairs):
        left = jnp.concatenate([pair[0] for pair in pairs], axis=1).astype(jnp.bfloat16)
        right = jnp.concatenate([pair[1] for pair in pairs], axis=1).astype(jnp.bfloat16)
        return lax.dot_general(left, right, (((1,), (1,)), ((), ())), preferred_element_type=F32)

    def step(i, total):
        rows = [4 * i + u for u in range(4)]
        return total + part([columns(ref[pl.ds(2 * r + side, 1), :], r) for r in rows])

    total = lax.fori_loop(0, ROWS // 4, step, jnp.zeros((48, LANES), F32))
    for other, count in more:
        total = total + part(
            [columns(other[h : h + 1, :], jnp.int32(ROWS + h)) for h in range(count)]
        )
    whole = total.astype(I32)
    return (whole[24:] - 1) * 128 + whole[:24]


def lane_gather(rows, lane):
    numbers = lax.GatherDimensionNumbers(
        offset_dims=(),
        collapsed_slice_dims=(1,),
        start_index_map=(1,),
        operand_batching_dims=(0,),
        start_indices_batching_dims=(0,),
    )
    return lax.gather(
        rows, lane[..., None], numbers, (1, 1), mode=lax.GatherScatterMode.PROMISE_IN_BOUNDS
    )


def lookup(rows, index, start=None):
    lane, high = index & 127, index >> 7
    out = start
    for number, row in rows:
        wide = jnp.broadcast_to(row, index.shape)
        found = lane_gather(wide, lane)
        out = jnp.where(high == number, found, jnp.zeros_like(found) if out is None else out)
    return out


def lookup_all(jobs, missing):
    lanes = [index & 127 for _, index in jobs]
    highs = [index >> 7 for _, index in jobs]

    def step(i, found):
        for u in range(4):
            row = 4 * i + u
            values = [
                lane_gather(jnp.broadcast_to(ref[pl.ds(row, 1), :], index.shape), lane)
                for (ref, index), lane in zip(jobs, lanes)
            ]
            found = [jnp.where(high == row, v, f) for high, v, f in zip(highs, values, found)]
        return found

    return lax.fori_loop(0, ROWS // 4, step, [jnp.full(i.shape, missing, r.dtype) for r, i in jobs])


def table(ref, count=ROWS, first=0):
    return [(first + h, ref[h : h + 1, :]) for h in range(count)]


def total_row(parts):
    lane = iota((1, LANES), 1)
    row = jnp.zeros((1, LANES), F32)
    for number, part in enumerate(parts):
        flat = jnp.sum(part, axis=0, keepdims=True)
        row = jnp.where(lane == number, jnp.sum(flat, axis=1, keepdims=True), row)
    return row


def pick(row, number):
    return jnp.sum(jnp.where(iota((1, LANES), 1) == number, row, 0.0), axis=1, keepdims=True)


def kernel(
    n_region, n_sub,
    conn_x_in, conn_y_in, conn_z_in, send_y, send_z, perm_in, storage_in, sigma_ref, source_in,
    trace_out, pressure_out, flux_out,
    conn_x, conn_y, conn_z, perm, storage, source,
    zlist, itable, tables, sides, vtables, by_face, near_cells, far_cells, z_cells,
    near_send, near_recv, z_send, z_recv, far_send, far_recv, terms_send, terms_recv, far_next,
    near_sems, z_sems, far_sems,
    row_send, flat_recv, side_recv, deep_recv, sum_sems,
):
    region, sub = lax.axis_index("region"), lax.axis_index("sub")
    n_side = math.isqrt(n_sub // 4)
    n_flat, n_deep = 2 * n_side, 2 * n_region
    core, deep = lax.rem(sub, 2), lax.rem(lax.div(sub, 2), 2)
    place_x, place_y = lax.div(sub, 4 * n_side), lax.rem(lax.div(sub, 4), n_side)
    flat_me = place_x * 2 + core
    deep_me = deep * n_region + region
    upper = core == 1
    far_peer, near_peer = lax.rem(sub + n_sub + 2 * core - 1, n_sub), sub + 1 - 2 * core
    region_up, region_down = lax.rem(region + 1, n_region), lax.rem(region + n_region - 1, n_region)

    def flat_peer(offset):
        peer = lax.rem(flat_me + offset, n_flat)
        column = lax.div(peer, 2) * n_side + place_y
        return (region, column * 4 + deep * 2 + lax.rem(peer, 2))

    def side_peer(offset):
        column = place_x * n_side + lax.rem(place_y + offset, n_side)
        return (region, column * 4 + deep * 2 + core)

    def deep_peer(offset):
        peer = lax.rem(deep_me + offset, n_deep)
        return (lax.rem(peer, n_region), sub - deep * 2 + lax.div(peer, n_region) * 2)

    barrier = pltpu.get_barrier_semaphore()

    def greet(device):
        pl.semaphore_signal(barrier, inc=1, device_id=device, device_id_type=MESH)

    greet((region, far_peer))
    for peer, count in ((deep_peer, n_deep), (flat_peer, n_flat), (side_peer, n_side)):
        for j in range(1, count):
            greet(peer(j))

    def lanes(i):
        return slice(LANES * i, LANES * (i + 1))

    for there, here in (
        (conn_y_in, conn_y), (conn_z_in, conn_z), (conn_x_in, conn_x),
        (storage_in, storage), (source_in, source),
    ):
        for i in range(ROWS):
            here[2 * i : 2 * i + 2, :] = there[:, lanes(i)]
    for c in range(2):
        for i in range(ROWS):
            perm[pl.ds(2 * i + c, 3, stride=32), :] = perm_in[c, :, lanes(i)]

    def pair(ref, first=0):
        return [ref[pl.ds(first + k, ROWS, stride=2), :] for k in range(2)]

    by_side = [pair(perm, 32 * d) for d in range(3)]
    trans = [[2.0 * by_side[d][c] for d in range(3)] for c in range(2)]
    store, origin, sigma = pair(storage), pair(source), sigma_ref[...]

    diag = [2.0 * (trans[c][0] + trans[c][1] + trans[c][2]) + store[c] + sigma for c in range(2)]
    determ = diag[0] * diag[1] - sigma * sigma
    solve_00, solve_01, solve_11 = diag[1] / determ, sigma / determ, diag[0] / determ

    def solve(load):
        return (solve_00 * load[0] + solve_01 * load[1], solve_01 * load[0] + solve_11 * load[1])

    def face_load(v):
        return [
            sum(trans[c][d] * (v[c][d][0] + v[c][d][1]) for d in range(3)) for c in range(2)
        ]

    def contributions(v, inner):
        return [
            [[trans[c][d] * (v[c][d][s] - inner[c]) for s in range(2)] for d in range(3)]
            for c in range(2)
        ]

    base = solve(origin)
    rhs_g = [[[trans[c][d] * base[c]] * 2 for d in range(3)] for c in range(2)]

    def at_face(which, face, count=ROWS):
        return lookup(table(itable.at[which], count), face, jnp.full(face.shape, -1, I32))

    zlist[0:1, :] = jnp.full((1, LANES), -1, I32)
    zlist[0:1, 0:64] = send_z[...]
    itable[2] = inverse(conn_y, 0, [(send_y, 4)])
    itable[3] = inverse(conn_y, 1)
    itable[4] = inverse(conn_z, 0, [(zlist, 1)])
    itable[5] = inverse(conn_z, 1)
    up_y_cells = at_face(3, send_y[...])
    down_y_cells = itable[2, ROWS : ROWS + 4, :]
    up_z_cells = at_face(5, zlist[0:1, :])
    down_z_cells = itable[4, ROWS : ROWS + 1, :]

    def by_core(if_upper, if_lower):
        return jnp.where(upper, if_upper, if_lower)

    for c in range(2):
        far_cells[4 * c : 4 * c + 4, :] = by_core(up_y_cells, down_y_cells)
        near_cells[4 * c : 4 * c + 4, :] = by_core(down_y_cells, up_y_cells)
        z_cells[c : c + 1, :] = up_z_cells
        z_cells[2 + c : 3 + c, :] = down_z_cells

    def remote(send, recv, sems, device):
        return pltpu.make_async_remote_copy(
            src_ref=send,
            dst_ref=recv,
            send_sem=sems.at[0],
            recv_sem=sems.at[1],
            device_id=device,
            device_id_type=MESH,
        )

    def copies(step):
        near, along = near_sems.at[step], z_sems.at[step]
        return [
            remote(near_send.at[step], near_recv.at[step], near, (region, near_peer)),
            remote(z_send.at[step, 0], z_recv.at[step, 0], along.at[0], (region_up, sub)),
            remote(z_send.at[step, 1], z_recv.at[step, 1], along.at[1], (region_down, sub)),
        ]

    far_first = remote(
        far_send.at[0, pl.ds(0, 8)], far_recv.at[0, pl.ds(0, 8)], far_sems.at[0], (region, far_peer)
    )
    far_second = remote(far_send.at[1], far_recv.at[1], far_sems.at[1], (region, far_peer))
    far_terms = remote(terms_send, terms_recv, far_sems.at[2], (region, far_peer))

    def side_values(at, cells, pair):
        for c in range(2):
            sides[at + c, 0:ROWS, :] = pair[c]
        second = iota((8, LANES), 0) >= 4
        rows = [
            (h, jnp.where(second, sides[at + 1, h : h + 1, :], sides[at, h : h + 1, :]))
            for h in range(ROWS)
        ]
        return lookup(rows, cells[...])

    def fill_far(step, g):
        pair = [by_core(g[c][1][1], g[c][1][0]) for c in range(2)]
        far_send[step, 0:8, :] = side_values(0, far_cells, pair)

    def fill_near(step, g):
        pair = [by_core(g[c][1][0], g[c][1][1]) for c in range(2)]
        near_send[step] = side_values(2, near_cells, pair)
        for s in range(2):
            for c in range(2):
                sides[4, pl.ds(2 - 2 * s + c, ROWS, stride=4), :] = g[c][2][s]
        rows = [(h, sides[4, 4 * h : 4 * h + 4, :]) for h in range(ROWS)]
        z_rows = lookup(rows, z_cells[0:4, :])
        z_send[step, 0] = z_rows[0:2]
        z_send[step, 1] = z_rows[2:4]

    def start(step):
        for copy in copies(step):
            copy.start()

    def keep(g):
        for d in (1, 2, 0):
            for c in range(2):
                for s in range(2):
                    tables[c * 6 + d * 2 + s] = g[c][d][s]

    greetings = 1 + (n_flat - 1) + (n_deep - 1) + (n_side - 1)
    fill_far(0, rhs_g)
    fill_near(0, rhs_g)
    pl.semaphore_wait(barrier, greetings)
    far_first.start()
    start(0)
    keep(rhs_g)
    terms_send[0:8, :] = side_values(5, far_cells, [trans[c][1] for c in range(2)])
    terms_send[8:16, :] = side_values(7, far_cells, (solve_00, solve_01))
    terms_send[16:24, :] = side_values(9, far_cells, (solve_11, solve_11))
    far_terms.start()

    itable[0] = inverse(conn_x, 0)
    itable[1] = inverse(conn_x, 1)
    faces_x, faces_y, faces_z = pair(conn_x), pair(conn_y), pair(conn_z)
    asked = (faces_x[1], faces_y[1], faces_z[1], faces_x[0], faces_y[0], faces_z[0])
    found = lookup_all([(itable.at[k], face) for k, face in zip((0, 2, 4, 1, 3, 5), asked)], -1)
    up, down = list(found[:3]), list(found[3:])
    up[0] = lookup([(16, itable[0, 16:17, :])], asked[0], up[0])
    down[0] = lookup([(16, itable[1, 16:17, :])], asked[3], down[0])
    down[1] = jnp.where(asked[4] >= E_DEV, asked[4], down[1])
    down[2] = jnp.where(asked[5] >= E_DEV, asked[5], down[2])
    last_z = region == n_region - 1
    up[2] = jnp.where(jnp.logical_and(up[2] >= E_DEV, last_z), -1, up[2])
    first_y = jnp.logical_and(down[1] >= E_DEV, sub == 0)
    first_z = jnp.logical_and(down[2] >= E_DEV, region == 0)
    lone_x = down[0] < 0
    far_index = by_core(up[1], down[1]) - E_DEV
    near_index = by_core(down[1], up[1]) - E_DEV
    at_far = far_index >= 0
    far_index = jnp.where(sub == n_sub - 1, -1, far_index)

    def assemble(step, g, meanwhile=None):
        out = [[[None, None] for _ in range(3)] for _ in range(2)]
        across = lookup_all(
            [(tables.at[k], (up if k % 2 == 0 else down)[k % 6 // 2]) for k in range(12)], 0.0
        )
        for c in range(2):
            for d in range(3):
                at = c * 6 + d * 2
                out[c][d][1] = g[c][d][1] + across[at]
                out[c][d][0] = g[c][d][0] + across[at + 1]
        if meanwhile is not None:
            meanwhile(out)
        for copy in copies(step):
            copy.wait_recv()
        for c in range(2):
            near = lookup(table(near_recv.at[step, pl.ds(4 * c, 4)], 4), near_index)
            out[c][1][1] = out[c][1][1] + by_core(0.0, near)
            out[c][1][0] = out[c][1][0] + by_core(near, 0.0)
            from_below_z = table(z_recv.at[step, 0, pl.ds(c, 1)], 1, ROWS)
            from_above_z = table(z_recv.at[step, 1, pl.ds(c, 1)], 1, ROWS)
            out[c][2][1] = out[c][2][1] + lookup(from_above_z, up[2])
            out[c][2][0] = jnp.where(first_z, 0.0, out[c][2][0] + lookup(from_below_z, down[2]))
        return out

    def add_far(out, rows):
        for c in range(2):
            far = lookup(table(rows.at[pl.ds(4 * c, 4)], 4), far_index)
            out[c][1][1] = out[c][1][1] + by_core(far, 0.0)
            out[c][1][0] = jnp.where(first_y, 0.0, out[c][1][0] + by_core(0.0, far))

    def by_faces(number, v):
        jobs = []
        for c in range(2):
            parts = (v[c][0][0], v[c][0][1], v[c][1][1], v[c][2][1])
            for k, part in enumerate(parts):
                vtables[number, c * 4 + k] = part
                index = (itable[0], itable[1], itable[3, 0:ROWS, :], itable[5, 0:ROWS, :])[k]
                jobs.append((vtables.at[number, c * 4 + k], index))
        found = lookup_all(jobs, 0.0)
        for c in range(2):
            x_low, x_up, y_up, z_up = found[4 * c : 4 * c + 4]
            by_x = jnp.where(itable[1] < 0, x_low, x_up)
            by_face[number, pl.ds(c, 17, stride=2), :] = by_x[0:17]
            by_face[number, pl.ds(34 + c, ROWS, stride=2), :] = y_up
            by_face[number, pl.ds(66 + c, ROWS, stride=2), :] = z_up

    def inner(u, v):
        total = sum(u[c][d][1] * v[c][d][1] for c in range(2) for d in range(3))
        edge = sum(u[c][0][0] * v[c][0][0] for c in range(2))
        return total + jnp.where(lone_x, edge, 0.0)

    def energy(v, load, solved):
        total = sum(
            trans[c][d] * (v[c][d][0] * v[c][d][0] + v[c][d][1] * v[c][d][1])
            for c in range(2)
            for d in range(3)
        )
        return total - (load[0] * solved[0] + load[1] * solved[1])

    stages = (
        (flat_recv, flat_peer, n_flat), (side_recv, side_peer, n_side), (deep_recv, deep_peer, n_deep)
    )

    def sum_start(k, stage, row):
        recv, peer, count = stages[stage]
        row_send[k, stage, 0:1, :] = row
        recv[k, count - 1 : count, :] = row
        for j in sorted(range(1, count), key=lambda j: -min(j, count - j)):
            pltpu.make_async_remote_copy(
                src_ref=row_send.at[k, stage, pl.ds(0, 1)],
                dst_ref=recv.at[k, pl.ds(j - 1, 1)],
                send_sem=sum_sems.at[k, stage, 0],
                recv_sem=sum_sems.at[k, stage, 1],
                device_id=peer(j),
                device_id_type=MESH,
            ).start()

    def drain(k, stage, which):
        recv, _, count = stages[stage]
        if count > 1:
            rows = recv.at[k, pl.ds(0, count - 1)]
            pltpu.make_async_copy(rows, rows, sum_sems.at[k, stage, which]).wait()

    def sum_done(k, stage):
        drain(k, stage, 1)
        return jnp.sum(stages[stage][0][k], axis=0, keepdims=True)

    def estimate(rough):
        load = face_load(rough)
        sum_start(0, 0, total_row([inner(rough, rough), energy(rough, load, solve(load))]))

    b = assemble(0, rhs_g, estimate)
    far_first.wait_recv()
    add_far(b, far_recv.at[0])

    load_b = face_load(b)
    inside_b = solve(load_b)
    g_b = contributions(b, inside_b)
    fill_near(1, g_b)
    start(1)
    keep(g_b)
    fill_far(1, g_b)
    sum_start(0, 1, sum_done(0, 0))
    w = assemble(1, g_b)

    def without_far(part, here):
        return jnp.where(jnp.logical_and(at_far, here), 0.0, part)

    apart = [
        [w[c][0], [without_far(w[c][1][0], core == 0), without_far(w[c][1][1], upper)], w[c][2]]
        for c in range(2)
    ]
    far_send[1, 8:16, :] = side_values(0, far_cells, face_load(apart))
    far_second.start()
    by_faces(0, b)
    sum_start(0, 2, sum_done(0, 1))
    far_terms.wait_recv()
    far_second.wait_recv()
    add_far(w, far_recv.at[1])

    far_w = far_send[1, 0:8, :] + far_recv[1, 0:8, :]
    far_trans = terms_recv[0:8, :]
    far_load = far_recv[1, 8:16, :] + far_trans * far_w
    load_0, load_1 = far_load[0:4], far_load[4:8]
    term_00, term_01, term_11 = (terms_recv[k : k + 4, :] for k in (8, 12, 16))
    far_next[0:4, :] = far_trans[0:4] * (far_w[0:4] - (term_00 * load_0 + term_01 * load_1))
    far_next[4:8, :] = far_trans[4:8] * (far_w[4:8] - (term_01 * load_0 + term_11 * load_1))

    load_w = face_load(w)
    inside_w = solve(load_w)
    g_w = contributions(w, inside_w)
    fill_near(2, g_w)
    start(2)
    keep(g_w)
    ww = assemble(2, g_w)
    add_far(ww, far_next)

    first = sum_done(0, 2)
    scale = pick(first, 0) / pick(first, 1)

    def blend(u, factor, v):
        return [
            [[u[c][d][s] - factor * v[c][d][s] for s in range(2)] for d in range(3)]
            for c in range(2)
        ]

    r = blend(b, scale, w)
    s = blend(w, scale, ww)
    load = face_load(s)
    parts = [inner(b, b), inner(b, r), inner(r, r), inner(r, s), inner(s, s)]
    sum_start(1, 0, total_row([*parts, energy(s, load, solve(load))]))
    load_ww = face_load(ww)
    inside_ww = solve(load_ww)
    g_ww = contributions(ww, inside_ww)
    by_faces(1, w)
    sum_start(1, 1, sum_done(1, 0))
    by_faces(2, ww)
    sum_start(1, 2, sum_done(1, 1))
    for step in range(ROUNDS):
        for copy in copies(step):
            copy.wait_send()
    for copy in (far_first, far_second, far_terms):
        copy.wait_send()
    for k, stage in ((0, 0), (0, 1), (0, 2), (1, 0), (1, 1)):
        drain(k, stage, 0)
    sums = sum_done(1, 2)
    bb, br, rr_, rs_, ss_, sas_ = (pick(sums, k) for k in range(6))

    norm_0 = bb
    near, away = bb / (bb - br), -br / (bb - br)
    tilt = away / scale
    alpha_0 = scale * near
    rr = near * (near * rr_ + away * br)
    bs, bw = (br - rr_) / scale, bb - 2.0 * br + rr_
    rs = near * (near * rs_ + tilt * (br - rr_)) + away * (near * bs + tilt * (bb - br))
    ss = near * near * ss_ + 2.0 * near * tilt * (bs - rs_) + tilt * tilt * bw
    sas = near * near * sas_ + 2.0 * near * tilt * ((bs - rs_) / scale - ss_)
    sas = sas + tilt * tilt * (bw / scale - (bs - rs_))

    beta_0 = rr / norm_0
    alpha_1 = rr / (rs - beta_0 * rr / alpha_0)
    ws = -(rr / alpha_0 + rs) / alpha_0
    norm_2 = -alpha_1 * (rs - alpha_1 * ss - alpha_1 * beta_0 * ws)
    beta_1 = norm_2 / rr
    ratio = alpha_1 * beta_0 / alpha_0
    along = ss - alpha_1 * sas - ratio * (ws - ss)
    energy_2 = -norm_2 / alpha_1 * (1.0 + ratio) - alpha_1 * along
    alpha_2 = norm_2 / (energy_2 - beta_1 * norm_2 / alpha_1)
    on_r = alpha_1 + alpha_2 * (1.0 + beta_1)
    on_s = -alpha_2 * alpha_1
    on_b = alpha_0 + alpha_1 * beta_0 + alpha_2 * beta_1 * beta_0 + on_r
    on_w = -alpha_2 * alpha_1 * beta_0 - alpha_0 * on_r + on_s
    on_ww = -alpha_0 * on_s

    for c in range(2):
        pressure_out[pl.ds(c, ROWS, stride=2), :] = base[c] + (
            on_b * inside_b[c] + on_w * inside_w[c] + on_ww * inside_ww[c]
        )
        for d in range(3):
            for k in range(2):
                flux = on_b * g_b[c][d][k] + on_w * g_w[c][d][k] + on_ww * g_ww[c][d][k]
                flux_out[pl.ds(32 * (2 * d + k) + c, ROWS, stride=2), :] = rhs_g[c][d][k] - flux
    by_face[0] = on_b * by_face[0] + on_w * by_face[1] + on_ww * by_face[2]
    for i in range(49):
        trace_out[:, LANES * i : LANES * (i + 1)] = by_face[0, 2 * i : 2 * i + 2, :]
    drain(1, 2, 0)


def solution(mesh):
    n_region, n_sub = mesh.shape["region"], mesh.shape["sub"]
    n_side = math.isqrt(n_sub // 4)
    n_flat, n_deep = 2 * n_side, 2 * n_region

    def local(conn_x, conn_y, conn_z, send_y, send_z, perm, storage, sigma, source):
        vmem = pl.BlockSpec(memory_space=pltpu.VMEM)
        dma = pltpu.SemaphoreType.DMA
        trace, pressure, flux = pl.pallas_call(
            functools.partial(kernel, n_region, n_sub),
            out_shape=(
                jax.ShapeDtypeStruct((2, NXF + 2 * E_DEV), F32),
                jax.ShapeDtypeStruct((2 * ROWS, LANES), F32),
                jax.ShapeDtypeStruct((12 * ROWS, LANES), F32),
            ),
            in_specs=[vmem] * 9,
            out_specs=(vmem,) * 3,
            scratch_shapes=[
                pltpu.VMEM((2 * ROWS, LANES), I32),
                pltpu.VMEM((2 * ROWS, LANES), I32),
                pltpu.VMEM((2 * ROWS, LANES), I32),
                pltpu.VMEM((6 * ROWS, LANES), F32),
                pltpu.VMEM((2 * ROWS, LANES), F32),
                pltpu.VMEM((2 * ROWS, LANES), F32),
                pltpu.VMEM((8, LANES), I32),
                pltpu.VMEM((6, 24, LANES), I32),
                pltpu.VMEM((12, ROWS, LANES), F32),
                pltpu.VMEM((11, 4 * ROWS, LANES), F32),
                pltpu.VMEM((3, 8, ROWS, LANES), F32),
                pltpu.VMEM((3, 104, LANES), F32),
                pltpu.VMEM((8, LANES), I32),
                pltpu.VMEM((8, LANES), I32),
                pltpu.VMEM((8, LANES), I32),
                pltpu.VMEM((ROUNDS, 8, LANES), F32),
                pltpu.VMEM((ROUNDS, 8, LANES), F32),
                pltpu.VMEM((ROUNDS, 2, 2, LANES), F32),
                pltpu.VMEM((ROUNDS, 2, 2, LANES), F32),
                pltpu.VMEM((2, 16, LANES), F32),
                pltpu.VMEM((2, 16, LANES), F32),
                pltpu.VMEM((24, LANES), F32),
                pltpu.VMEM((24, LANES), F32),
                pltpu.VMEM((8, LANES), F32),
                dma((ROUNDS, 2)),
                dma((ROUNDS, 2, 2)),
                dma((3, 2)),
                pltpu.VMEM((2, 3, 8, LANES), F32),
                pltpu.VMEM((2, n_flat, LANES), F32),
                pltpu.VMEM((2, n_side, LANES), F32),
                pltpu.VMEM((2, n_deep, LANES), F32),
                dma((2, 3, 2)),
            ],
            compiler_params=pltpu.CompilerParams(
                collective_id=0, has_side_effects=True, vmem_limit_bytes=32 * 1024 * 1024
            ),
        )(
            conn_x, conn_y, conn_z, send_y.reshape(4, LANES), send_z.reshape(1, 64),
            perm, storage, sigma.reshape(ROWS, LANES), source,
        )
        pressure = pressure.reshape(ROWS, 2, LANES).transpose(1, 0, 2).reshape(2, E_DEV)
        flux = flux.reshape(6, ROWS, 2, LANES).transpose(2, 0, 1, 3).reshape(2, 6, E_DEV)
        return trace, pressure, flux

    both = ("region", "sub")
    return jax.shard_map(
        local,
        mesh=mesh,
        in_specs=(
            P(None, both), P(None, both), P(None, both), P(both), P(both),
            P(None, None, both), P(None, both), P(both), P(None, both),
        ),
        out_specs=(P(None, both), P(None, both), P(None, None, both)),
        check_vma=False,
    )
```

```python
import functools

import jax
import jax.numpy as jnp
from jax import lax
from jax.experimental import pallas as pl
from jax.experimental.pallas import tpu as pltpu
from jax.sharding import PartitionSpec as P

MESH = pl.DeviceIdType.MESH
F32 = jnp.float32
I32 = jnp.int32
ROWS = 16
LANES = 128
E_DEV = ROWS * LANES
NXF = 2176
ROUNDS = 3


def iota(shape, dim):
    return lax.broadcasted_iota(I32, shape, dim)


def inverse(ref, side, more=()):
    def columns(face, number):
        spot = jnp.where(iota((LANES, LANES), 0) == (face & 127), 1.0, 0.0)
        hit = iota((24, LANES), 0) == (face >> 7)
        low = jnp.where(hit, iota((1, LANES), 1).astype(F32), 0.0)
        high = jnp.where(hit, (number + 1).astype(F32), 0.0)
        return jnp.concatenate([low, high], axis=0), spot

    def part(pairs):
        left = jnp.concatenate([pair[0] for pair in pairs], axis=1).astype(jnp.bfloat16)
        right = jnp.concatenate([pair[1] for pair in pairs], axis=1).astype(jnp.bfloat16)
        return lax.dot_general(left, right, (((1,), (1,)), ((), ())), preferred_element_type=F32)

    def step(i, total):
        rows = [4 * i + u for u in range(4)]
        return total + part([columns(ref[pl.ds(2 * r + side, 1), :], r) for r in rows])

    total = lax.fori_loop(0, ROWS // 4, step, jnp.zeros((48, LANES), F32))
    for other, count in more:
        total = total + part(
            [columns(other[h : h + 1, :], jnp.int32(ROWS + h)) for h in range(count)]
        )
    whole = total.astype(I32)
    return (whole[24:] - 1) * 128 + whole[:24]


def lane_gather(rows, lane):
    numbers = lax.GatherDimensionNumbers(
        offset_dims=(),
        collapsed_slice_dims=(1,),
        start_index_map=(1,),
        operand_batching_dims=(0,),
        start_indices_batching_dims=(0,),
    )
    return lax.gather(
        rows, lane[..., None], numbers, (1, 1), mode=lax.GatherScatterMode.PROMISE_IN_BOUNDS
    )


def lookup(rows, index, start=None):
    lane, high = index & 127, index >> 7
    out = start
    for number, row in rows:
        wide = jnp.broadcast_to(row, index.shape)
        found = lane_gather(wide, lane)
        out = jnp.where(high == number, found, jnp.zeros_like(found) if out is None else out)
    return out


def lookup_all(jobs, missing):
    lanes = [index & 127 for _, index in jobs]
    highs = [index >> 7 for _, index in jobs]

    def step(i, found):
        for u in range(4):
            row = 4 * i + u
            values = [
                lane_gather(jnp.broadcast_to(ref[pl.ds(row, 1), :], index.shape), lane)
                for (ref, index), lane in zip(jobs, lanes)
            ]
            found = [jnp.where(high == row, v, f) for high, v, f in zip(highs, values, found)]
        return found

    return lax.fori_loop(0, ROWS // 4, step, [jnp.full(i.shape, missing, r.dtype) for r, i in jobs])


def table(ref, count=ROWS, first=0):
    return [(first + h, ref[h : h + 1, :]) for h in range(count)]


def total_row(parts):
    lane = iota((1, LANES), 1)
    row = jnp.zeros((1, LANES), F32)
    for number, part in enumerate(parts):
        flat = jnp.sum(part, axis=0, keepdims=True)
        row = jnp.where(lane == number, jnp.sum(flat, axis=1, keepdims=True), row)
    return row


def pick(row, number):
    return jnp.sum(jnp.where(iota((1, LANES), 1) == number, row, 0.0), axis=1, keepdims=True)


def kernel(
    n_region, n_sub,
    conn_x_in, conn_y_in, conn_z_in, send_y, send_z, perm_in, storage_in, sigma_ref, source_in,
    trace_out, pressure_out, flux_out,
    conn_x, conn_y, conn_z, perm, storage, source,
    zlist, itable, tables, sides, vtables, by_face, near_cells, far_cells, z_cells,
    near_send, near_recv, z_send, z_recv, far_send, far_recv, terms_send, terms_recv, far_next,
    near_sems, z_sems, far_sems,
    row_send, flat_recv, deep_recv, sum_sems,
):
    region, sub = lax.axis_index("region"), lax.axis_index("sub")
    n_flat, n_deep = n_sub // 2, 2 * n_region
    core, deep = lax.rem(sub, 2), lax.rem(lax.div(sub, 2), 2)
    flat_me = lax.div(sub, 4) * 2 + core
    deep_me = deep * n_region + region
    upper = core == 1
    far_peer, near_peer = lax.rem(sub + n_sub + 2 * core - 1, n_sub), sub + 1 - 2 * core
    region_up, region_down = lax.rem(region + 1, n_region), lax.rem(region + n_region - 1, n_region)

    def flat_peer(offset):
        peer = lax.rem(flat_me + offset, n_flat)
        return (region, lax.div(peer, 2) * 4 + deep * 2 + lax.rem(peer, 2))

    def deep_peer(offset):
        peer = lax.rem(deep_me + offset, n_deep)
        return (lax.rem(peer, n_region), sub - deep * 2 + lax.div(peer, n_region) * 2)

    barrier = pltpu.get_barrier_semaphore()

    def greet(device):
        pl.semaphore_signal(barrier, inc=1, device_id=device, device_id_type=MESH)

    greet((region, far_peer))
    for peer, count in ((deep_peer, n_deep), (flat_peer, n_flat)):
        lax.fori_loop(1, count, lambda j, c, peer=peer: (greet(peer(j)), c)[1], 0)

    def lanes(i):
        return slice(LANES * i, LANES * (i + 1))

    for there, here in (
        (conn_y_in, conn_y), (conn_z_in, conn_z), (conn_x_in, conn_x),
        (storage_in, storage), (source_in, source),
    ):
        for i in range(ROWS):
            here[2 * i : 2 * i + 2, :] = there[:, lanes(i)]
    for c in range(2):
        for i in range(ROWS):
            perm[pl.ds(2 * i + c, 3, stride=32), :] = perm_in[c, :, lanes(i)]

    def pair(ref, first=0):
        return [ref[pl.ds(first + k, ROWS, stride=2), :] for k in range(2)]

    by_side = [pair(perm, 32 * d) for d in range(3)]
    trans = [[2.0 * by_side[d][c] for d in range(3)] for c in range(2)]
    store, origin, sigma = pair(storage), pair(source), sigma_ref[...]

    diag = [2.0 * (trans[c][0] + trans[c][1] + trans[c][2]) + store[c] + sigma for c in range(2)]
    determ = diag[0] * diag[1] - sigma * sigma
    solve_00, solve_01, solve_11 = diag[1] / determ, sigma / determ, diag[0] / determ

    def solve(load):
        return (solve_00 * load[0] + solve_01 * load[1], solve_01 * load[0] + solve_11 * load[1])

    def face_load(v):
        return [
            sum(trans[c][d] * (v[c][d][0] + v[c][d][1]) for d in range(3)) for c in range(2)
        ]

    def contributions(v, inner):
        return [
            [[trans[c][d] * (v[c][d][s] - inner[c]) for s in range(2)] for d in range(3)]
            for c in range(2)
        ]

    base = solve(origin)
    rhs_g = [[[trans[c][d] * base[c]] * 2 for d in range(3)] for c in range(2)]

    def at_face(which, face, count=ROWS):
        return lookup(table(itable.at[which], count), face, jnp.full(face.shape, -1, I32))

    zlist[0:1, :] = jnp.full((1, LANES), -1, I32)
    zlist[0:1, 0:64] = send_z[...]
    itable[2] = inverse(conn_y, 0, [(send_y, 4)])
    itable[3] = inverse(conn_y, 1)
    itable[4] = inverse(conn_z, 0, [(zlist, 1)])
    itable[5] = inverse(conn_z, 1)
    up_y_cells = at_face(3, send_y[...])
    down_y_cells = itable[2, ROWS : ROWS + 4, :]
    up_z_cells = at_face(5, zlist[0:1, :])
    down_z_cells = itable[4, ROWS : ROWS + 1, :]

    def by_core(if_upper, if_lower):
        return jnp.where(upper, if_upper, if_lower)

    for c in range(2):
        far_cells[4 * c : 4 * c + 4, :] = by_core(up_y_cells, down_y_cells)
        near_cells[4 * c : 4 * c + 4, :] = by_core(down_y_cells, up_y_cells)
        z_cells[c : c + 1, :] = up_z_cells
        z_cells[2 + c : 3 + c, :] = down_z_cells

    def remote(send, recv, sems, device):
        return pltpu.make_async_remote_copy(
            src_ref=send,
            dst_ref=recv,
            send_sem=sems.at[0],
            recv_sem=sems.at[1],
            device_id=device,
            device_id_type=MESH,
        )

    def copies(step):
        near, along = near_sems.at[step], z_sems.at[step]
        return [
            remote(near_send.at[step], near_recv.at[step], near, (region, near_peer)),
            remote(z_send.at[step, 0], z_recv.at[step, 0], along.at[0], (region_up, sub)),
            remote(z_send.at[step, 1], z_recv.at[step, 1], along.at[1], (region_down, sub)),
        ]

    far_first = remote(
        far_send.at[0, pl.ds(0, 8)], far_recv.at[0, pl.ds(0, 8)], far_sems.at[0], (region, far_peer)
    )
    far_second = remote(far_send.at[1], far_recv.at[1], far_sems.at[1], (region, far_peer))
    far_terms = remote(terms_send, terms_recv, far_sems.at[2], (region, far_peer))

    def side_values(at, cells, pair):
        for c in range(2):
            sides[at + c, 0:ROWS, :] = pair[c]
        second = iota((8, LANES), 0) >= 4
        rows = [
            (h, jnp.where(second, sides[at + 1, h : h + 1, :], sides[at, h : h + 1, :]))
            for h in range(ROWS)
        ]
        return lookup(rows, cells[...])

    def fill_far(step, g):
        pair = [by_core(g[c][1][1], g[c][1][0]) for c in range(2)]
        far_send[step, 0:8, :] = side_values(0, far_cells, pair)

    def fill_near(step, g):
        pair = [by_core(g[c][1][0], g[c][1][1]) for c in range(2)]
        near_send[step] = side_values(2, near_cells, pair)
        for s in range(2):
            for c in range(2):
                sides[4, pl.ds(2 - 2 * s + c, ROWS, stride=4), :] = g[c][2][s]
        rows = [(h, sides[4, 4 * h : 4 * h + 4, :]) for h in range(ROWS)]
        z_rows = lookup(rows, z_cells[0:4, :])
        z_send[step, 0] = z_rows[0:2]
        z_send[step, 1] = z_rows[2:4]

    def start(step):
        for copy in copies(step):
            copy.start()

    def keep(g):
        for d in (1, 2, 0):
            for c in range(2):
                for s in range(2):
                    tables[c * 6 + d * 2 + s] = g[c][d][s]

    greetings = 1 + (n_flat - 1) + (n_deep - 1)
    fill_far(0, rhs_g)
    fill_near(0, rhs_g)
    pl.semaphore_wait(barrier, greetings)
    far_first.start()
    start(0)
    keep(rhs_g)
    terms_send[0:8, :] = side_values(5, far_cells, [trans[c][1] for c in range(2)])
    terms_send[8:16, :] = side_values(7, far_cells, (solve_00, solve_01))
    terms_send[16:24, :] = side_values(9, far_cells, (solve_11, solve_11))
    far_terms.start()

    itable[0] = inverse(conn_x, 0)
    itable[1] = inverse(conn_x, 1)
    faces_x, faces_y, faces_z = pair(conn_x), pair(conn_y), pair(conn_z)
    asked = (faces_x[1], faces_y[1], faces_z[1], faces_x[0], faces_y[0], faces_z[0])
    found = lookup_all([(itable.at[k], face) for k, face in zip((0, 2, 4, 1, 3, 5), asked)], -1)
    up, down = list(found[:3]), list(found[3:])
    up[0] = lookup([(16, itable[0, 16:17, :])], asked[0], up[0])
    down[0] = lookup([(16, itable[1, 16:17, :])], asked[3], down[0])
    down[1] = jnp.where(asked[4] >= E_DEV, asked[4], down[1])
    down[2] = jnp.where(asked[5] >= E_DEV, asked[5], down[2])
    last_z = region == n_region - 1
    up[2] = jnp.where(jnp.logical_and(up[2] >= E_DEV, last_z), -1, up[2])
    first_y = jnp.logical_and(down[1] >= E_DEV, sub == 0)
    first_z = jnp.logical_and(down[2] >= E_DEV, region == 0)
    lone_x = down[0] < 0
    far_index = by_core(up[1], down[1]) - E_DEV
    near_index = by_core(down[1], up[1]) - E_DEV
    at_far = far_index >= 0
    far_index = jnp.where(sub == n_sub - 1, -1, far_index)

    def assemble(step, g, meanwhile=None):
        out = [[[None, None] for _ in range(3)] for _ in range(2)]
        across = lookup_all(
            [(tables.at[k], (up if k % 2 == 0 else down)[k % 6 // 2]) for k in range(12)], 0.0
        )
        for c in range(2):
            for d in range(3):
                at = c * 6 + d * 2
                out[c][d][1] = g[c][d][1] + across[at]
                out[c][d][0] = g[c][d][0] + across[at + 1]
        if meanwhile is not None:
            meanwhile(out)
        for copy in copies(step):
            copy.wait_recv()
        for c in range(2):
            near = lookup(table(near_recv.at[step, pl.ds(4 * c, 4)], 4), near_index)
            out[c][1][1] = out[c][1][1] + by_core(0.0, near)
            out[c][1][0] = out[c][1][0] + by_core(near, 0.0)
            from_below_z = table(z_recv.at[step, 0, pl.ds(c, 1)], 1, ROWS)
            from_above_z = table(z_recv.at[step, 1, pl.ds(c, 1)], 1, ROWS)
            out[c][2][1] = out[c][2][1] + lookup(from_above_z, up[2])
            out[c][2][0] = jnp.where(first_z, 0.0, out[c][2][0] + lookup(from_below_z, down[2]))
        return out

    def add_far(out, rows):
        for c in range(2):
            far = lookup(table(rows.at[pl.ds(4 * c, 4)], 4), far_index)
            out[c][1][1] = out[c][1][1] + by_core(far, 0.0)
            out[c][1][0] = jnp.where(first_y, 0.0, out[c][1][0] + by_core(0.0, far))

    def by_faces(number, v):
        jobs = []
        for c in range(2):
            parts = (v[c][0][0], v[c][0][1], v[c][1][1], v[c][2][1])
            for k, part in enumerate(parts):
                vtables[number, c * 4 + k] = part
                index = (itable[0], itable[1], itable[3, 0:ROWS, :], itable[5, 0:ROWS, :])[k]
                jobs.append((vtables.at[number, c * 4 + k], index))
        found = lookup_all(jobs, 0.0)
        for c in range(2):
            x_low, x_up, y_up, z_up = found[4 * c : 4 * c + 4]
            by_x = jnp.where(itable[1] < 0, x_low, x_up)
            by_face[number, pl.ds(c, 17, stride=2), :] = by_x[0:17]
            by_face[number, pl.ds(34 + c, ROWS, stride=2), :] = y_up
            by_face[number, pl.ds(66 + c, ROWS, stride=2), :] = z_up

    def inner(u, v):
        total = sum(u[c][d][1] * v[c][d][1] for c in range(2) for d in range(3))
        edge = sum(u[c][0][0] * v[c][0][0] for c in range(2))
        return total + jnp.where(lone_x, edge, 0.0)

    def energy(v, load, solved):
        total = sum(
            trans[c][d] * (v[c][d][0] * v[c][d][0] + v[c][d][1] * v[c][d][1])
            for c in range(2)
            for d in range(3)
        )
        return total - (load[0] * solved[0] + load[1] * solved[1])

    stages = ((flat_recv, flat_peer, n_flat), (deep_recv, deep_peer, n_deep))

    def sum_start(k, stage, row):
        recv, peer, count = stages[stage]
        row_send[k, stage, 0:1, :] = row
        recv[k, count - 1 : count, :] = row

        def one(j, carry):
            pltpu.make_async_remote_copy(
                src_ref=row_send.at[k, stage, pl.ds(0, 1)],
                dst_ref=recv.at[k, pl.ds(j - 1, 1)],
                send_sem=sum_sems.at[k, stage, 0],
                recv_sem=sum_sems.at[k, stage, 1],
                device_id=peer(j),
                device_id_type=MESH,
            ).start()
            return carry

        lax.fori_loop(1, count, one, 0)

    def drain(k, stage, which):
        recv, _, count = stages[stage]
        rows = recv.at[k, pl.ds(0, count - 1)]
        pltpu.make_async_copy(rows, rows, sum_sems.at[k, stage, which]).wait()

    def sum_done(k, stage):
        drain(k, stage, 1)
        return jnp.sum(stages[stage][0][k], axis=0, keepdims=True)

    def estimate(rough):
        load = face_load(rough)
        sum_start(0, 0, total_row([inner(rough, rough), energy(rough, load, solve(load))]))

    b = assemble(0, rhs_g, estimate)
    far_first.wait_recv()
    add_far(b, far_recv.at[0])

    load_b = face_load(b)
    inside_b = solve(load_b)
    g_b = contributions(b, inside_b)
    fill_near(1, g_b)
    start(1)
    keep(g_b)
    fill_far(1, g_b)
    sum_start(0, 1, sum_done(0, 0))
    w = assemble(1, g_b)

    def without_far(part, here):
        return jnp.where(jnp.logical_and(at_far, here), 0.0, part)

    apart = [
        [w[c][0], [without_far(w[c][1][0], core == 0), without_far(w[c][1][1], upper)], w[c][2]]
        for c in range(2)
    ]
    far_send[1, 8:16, :] = side_values(0, far_cells, face_load(apart))
    far_second.start()
    by_faces(0, b)
    far_terms.wait_recv()
    far_second.wait_recv()
    add_far(w, far_recv.at[1])

    far_w = far_send[1, 0:8, :] + far_recv[1, 0:8, :]
    far_trans = terms_recv[0:8, :]
    far_load = far_recv[1, 8:16, :] + far_trans * far_w
    load_0, load_1 = far_load[0:4], far_load[4:8]
    term_00, term_01, term_11 = (terms_recv[k : k + 4, :] for k in (8, 12, 16))
    far_next[0:4, :] = far_trans[0:4] * (far_w[0:4] - (term_00 * load_0 + term_01 * load_1))
    far_next[4:8, :] = far_trans[4:8] * (far_w[4:8] - (term_01 * load_0 + term_11 * load_1))

    load_w = face_load(w)
    inside_w = solve(load_w)
    g_w = contributions(w, inside_w)
    fill_near(2, g_w)
    start(2)
    keep(g_w)
    ww = assemble(2, g_w)
    add_far(ww, far_next)

    first = sum_done(0, 1)
    scale = pick(first, 0) / pick(first, 1)

    def blend(u, factor, v):
        return [
            [[u[c][d][s] - factor * v[c][d][s] for s in range(2)] for d in range(3)]
            for c in range(2)
        ]

    r = blend(b, scale, w)
    s = blend(w, scale, ww)
    load = face_load(s)
    parts = [inner(b, b), inner(b, r), inner(r, r), inner(r, s), inner(s, s)]
    sum_start(1, 0, total_row([*parts, energy(s, load, solve(load))]))
    load_ww = face_load(ww)
    inside_ww = solve(load_ww)
    g_ww = contributions(ww, inside_ww)
    by_faces(1, w)
    sum_start(1, 1, sum_done(1, 0))
    by_faces(2, ww)
    for step in range(ROUNDS):
        for copy in copies(step):
            copy.wait_send()
    for copy in (far_first, far_second, far_terms):
        copy.wait_send()
    for k, stage in ((0, 0), (0, 1), (1, 0)):
        drain(k, stage, 0)
    sums = sum_done(1, 1)
    bb, br, rr_, rs_, ss_, sas_ = (pick(sums, k) for k in range(6))

    norm_0 = bb
    near, away = bb / (bb - br), -br / (bb - br)
    tilt = away / scale
    alpha_0 = scale * near
    rr = near * (near * rr_ + away * br)
    bs, bw = (br - rr_) / scale, bb - 2.0 * br + rr_
    rs = near * (near * rs_ + tilt * (br - rr_)) + away * (near * bs + tilt * (bb - br))
    ss = near * near * ss_ + 2.0 * near * tilt * (bs - rs_) + tilt * tilt * bw
    sas = near * near * sas_ + 2.0 * near * tilt * ((bs - rs_) / scale - ss_)
    sas = sas + tilt * tilt * (bw / scale - (bs - rs_))

    beta_0 = rr / norm_0
    alpha_1 = rr / (rs - beta_0 * rr / alpha_0)
    ws = -(rr / alpha_0 + rs) / alpha_0
    norm_2 = -alpha_1 * (rs - alpha_1 * ss - alpha_1 * beta_0 * ws)
    beta_1 = norm_2 / rr
    ratio = alpha_1 * beta_0 / alpha_0
    along = ss - alpha_1 * sas - ratio * (ws - ss)
    energy_2 = -norm_2 / alpha_1 * (1.0 + ratio) - alpha_1 * along
    alpha_2 = norm_2 / (energy_2 - beta_1 * norm_2 / alpha_1)
    on_r = alpha_1 + alpha_2 * (1.0 + beta_1)
    on_s = -alpha_2 * alpha_1
    on_b = alpha_0 + alpha_1 * beta_0 + alpha_2 * beta_1 * beta_0 + on_r
    on_w = -alpha_2 * alpha_1 * beta_0 - alpha_0 * on_r + on_s
    on_ww = -alpha_0 * on_s

    for c in range(2):
        pressure_out[pl.ds(c, ROWS, stride=2), :] = base[c] + (
            on_b * inside_b[c] + on_w * inside_w[c] + on_ww * inside_ww[c]
        )
        for d in range(3):
            for k in range(2):
                flux = on_b * g_b[c][d][k] + on_w * g_w[c][d][k] + on_ww * g_ww[c][d][k]
                flux_out[pl.ds(32 * (2 * d + k) + c, ROWS, stride=2), :] = rhs_g[c][d][k] - flux
    by_face[0] = on_b * by_face[0] + on_w * by_face[1] + on_ww * by_face[2]
    for i in range(49):
        trace_out[:, LANES * i : LANES * (i + 1)] = by_face[0, 2 * i : 2 * i + 2, :]
    drain(1, 1, 0)


def hand_on(*refs):
    sems = refs[6]
    moves = [pltpu.make_async_copy(refs[k], refs[3 + k], sems.at[k]) for k in range(3)]
    for move in moves:
        move.start()
    for move in moves:
        move.wait()


def solution(mesh):
    n_region, n_sub = mesh.shape["region"], mesh.shape["sub"]
    n_flat, n_deep = n_sub // 2, 2 * n_region

    def local(conn_x, conn_y, conn_z, send_y, send_z, perm, storage, sigma, source):
        vmem = pl.BlockSpec(memory_space=pltpu.VMEM)
        dma = pltpu.SemaphoreType.DMA
        shapes = (
            jax.ShapeDtypeStruct((2, NXF + 2 * E_DEV), F32),
            jax.ShapeDtypeStruct((2 * ROWS, LANES), F32),
            jax.ShapeDtypeStruct((12 * ROWS, LANES), F32),
        )
        results = pl.pallas_call(
            functools.partial(kernel, n_region, n_sub),
            out_shape=shapes,
            in_specs=[vmem] * 9,
            out_specs=(vmem,) * 3,
            scratch_shapes=[
                pltpu.VMEM((2 * ROWS, LANES), I32),
                pltpu.VMEM((2 * ROWS, LANES), I32),
                pltpu.VMEM((2 * ROWS, LANES), I32),
                pltpu.VMEM((6 * ROWS, LANES), F32),
                pltpu.VMEM((2 * ROWS, LANES), F32),
                pltpu.VMEM((2 * ROWS, LANES), F32),
                pltpu.VMEM((8, LANES), I32),
                pltpu.VMEM((6, 24, LANES), I32),
                pltpu.VMEM((12, ROWS, LANES), F32),
                pltpu.VMEM((11, 4 * ROWS, LANES), F32),
                pltpu.VMEM((3, 8, ROWS, LANES), F32),
                pltpu.VMEM((3, 104, LANES), F32),
                pltpu.VMEM((8, LANES), I32),
                pltpu.VMEM((8, LANES), I32),
                pltpu.VMEM((8, LANES), I32),
                pltpu.VMEM((ROUNDS, 8, LANES), F32),
                pltpu.VMEM((ROUNDS, 8, LANES), F32),
                pltpu.VMEM((ROUNDS, 2, 2, LANES), F32),
                pltpu.VMEM((ROUNDS, 2, 2, LANES), F32),
                pltpu.VMEM((2, 16, LANES), F32),
                pltpu.VMEM((2, 16, LANES), F32),
                pltpu.VMEM((24, LANES), F32),
                pltpu.VMEM((24, LANES), F32),
                pltpu.VMEM((8, LANES), F32),
                dma((ROUNDS, 2)),
                dma((ROUNDS, 2, 2)),
                dma((3, 2)),
                pltpu.VMEM((2, 2, 8, LANES), F32),
                pltpu.VMEM((2, n_flat, LANES), F32),
                pltpu.VMEM((2, n_deep, LANES), F32),
                dma((2, 2, 2)),
            ],
            compiler_params=pltpu.CompilerParams(
                collective_id=0, has_side_effects=True, vmem_limit_bytes=32 * 1024 * 1024
            ),
        )(
            conn_x, conn_y, conn_z, send_y.reshape(4, LANES), send_z.reshape(1, 64),
            perm, storage, sigma.reshape(ROWS, LANES), source,
        )
        anywhere = pl.BlockSpec(memory_space=pl.ANY)
        trace, pressure, flux = pl.pallas_call(
            hand_on,
            out_shape=shapes,
            in_specs=[anywhere] * 3,
            out_specs=(anywhere,) * 3,
            scratch_shapes=[dma((3,))],
        )(*results)
        pressure = pressure.reshape(ROWS, 2, LANES).transpose(1, 0, 2).reshape(2, E_DEV)
        flux = flux.reshape(6, ROWS, 2, LANES).transpose(2, 0, 1, 3).reshape(2, 6, E_DEV)
        return trace, pressure, flux

    both = ("region", "sub")
    return jax.shard_map(
        local,
        mesh=mesh,
        in_specs=(
            P(None, both), P(None, both), P(None, both), P(both), P(both),
            P(None, None, both), P(None, both), P(both), P(None, both),
        ),
        out_specs=(P(None, both), P(None, both), P(None, None, both)),
        check_vma=False,
    )
```

```python
import functools

import jax
import jax.numpy as jnp
from jax import lax
from jax.experimental import pallas as pl
from jax.experimental.pallas import tpu as pltpu
from jax.sharding import PartitionSpec as P

MESH = pl.DeviceIdType.MESH
F32 = jnp.float32
I32 = jnp.int32
ROWS = 16
LANES = 128
E_DEV = ROWS * LANES
NXF = 2176
ROUNDS = 3


def iota(shape, dim):
    return lax.broadcasted_iota(I32, shape, dim)


def inverse(ref, side, more=()):
    def columns(face, number):
        spot = jnp.where(iota((LANES, LANES), 0) == (face & 127), 1.0, 0.0)
        hit = iota((24, LANES), 0) == (face >> 7)
        low = jnp.where(hit, iota((1, LANES), 1).astype(F32), 0.0)
        high = jnp.where(hit, (number + 1).astype(F32), 0.0)
        return jnp.concatenate([low, high], axis=0), spot

    def part(pairs):
        left = jnp.concatenate([pair[0] for pair in pairs], axis=1).astype(jnp.bfloat16)
        right = jnp.concatenate([pair[1] for pair in pairs], axis=1).astype(jnp.bfloat16)
        return lax.dot_general(left, right, (((1,), (1,)), ((), ())), preferred_element_type=F32)

    def step(i, total):
        rows = [4 * i + u for u in range(4)]
        return total + part([columns(ref[pl.ds(2 * r + side, 1), :], r) for r in rows])

    total = lax.fori_loop(0, ROWS // 4, step, jnp.zeros((48, LANES), F32))
    for other, count in more:
        total = total + part(
            [columns(other[h : h + 1, :], jnp.int32(ROWS + h)) for h in range(count)]
        )
    whole = total.astype(I32)
    return (whole[24:] - 1) * 128 + whole[:24]


def lane_gather(rows, lane):
    numbers = lax.GatherDimensionNumbers(
        offset_dims=(),
        collapsed_slice_dims=(1,),
        start_index_map=(1,),
        operand_batching_dims=(0,),
        start_indices_batching_dims=(0,),
    )
    return lax.gather(
        rows, lane[..., None], numbers, (1, 1), mode=lax.GatherScatterMode.PROMISE_IN_BOUNDS
    )


def lookup(rows, index, start=None):
    lane, high = index & 127, index >> 7
    out = start
    for number, row in rows:
        wide = jnp.broadcast_to(row, index.shape)
        found = lane_gather(wide, lane)
        out = jnp.where(high == number, found, jnp.zeros_like(found) if out is None else out)
    return out


def lookup_all(jobs, missing):
    lanes = [index & 127 for _, index in jobs]
    highs = [index >> 7 for _, index in jobs]

    def step(i, found):
        for u in range(4):
            row = 4 * i + u
            values = [
                lane_gather(jnp.broadcast_to(ref[pl.ds(row, 1), :], index.shape), lane)
                for (ref, index), lane in zip(jobs, lanes)
            ]
            found = [jnp.where(high == row, v, f) for high, v, f in zip(highs, values, found)]
        return found

    return lax.fori_loop(0, ROWS // 4, step, [jnp.full(i.shape, missing, r.dtype) for r, i in jobs])


def table(ref, count=ROWS, first=0):
    return [(first + h, ref[h : h + 1, :]) for h in range(count)]


def total_row(parts):
    lane = iota((1, LANES), 1)
    row = jnp.zeros((1, LANES), F32)
    for number, part in enumerate(parts):
        flat = jnp.sum(part, axis=0, keepdims=True)
        row = jnp.where(lane == number, jnp.sum(flat, axis=1, keepdims=True), row)
    return row


def pick(row, number):
    return jnp.sum(jnp.where(iota((1, LANES), 1) == number, row, 0.0), axis=1, keepdims=True)


def kernel(
    n_region, n_sub,
    conn_x_in, conn_y_in, conn_z_in, send_y, send_z, perm_in, storage_in, sigma_ref, source_in,
    trace_out, pressure_out, flux_out,
    conn_x, conn_y, conn_z, perm, storage, source,
    zlist, itable, tables, sides, vtables, by_face, near_cells, far_cells, z_cells,
    near_send, near_recv, z_send, z_recv, far_send, far_recv, terms_send, terms_recv, far_next,
    near_sems, z_sems, far_sems,
    row_send, flat_recv, deep_recv, sum_sems,
):
    region, sub = lax.axis_index("region"), lax.axis_index("sub")
    n_flat, n_deep = n_sub // 2, 2 * n_region
    core, deep = lax.rem(sub, 2), lax.rem(lax.div(sub, 2), 2)
    flat_me = lax.div(sub, 4) * 2 + core
    deep_me = deep * n_region + region
    upper = core == 1
    far_peer, near_peer = lax.rem(sub + n_sub + 2 * core - 1, n_sub), sub + 1 - 2 * core
    region_up, region_down = lax.rem(region + 1, n_region), lax.rem(region + n_region - 1, n_region)

    def flat_peer(offset):
        peer = lax.rem(flat_me + offset, n_flat)
        return (region, lax.div(peer, 2) * 4 + deep * 2 + lax.rem(peer, 2))

    def deep_peer(offset):
        peer = lax.rem(deep_me + offset, n_deep)
        return (lax.rem(peer, n_region), sub - deep * 2 + lax.div(peer, n_region) * 2)

    barrier = pltpu.get_barrier_semaphore()

    def greet(device):
        pl.semaphore_signal(barrier, inc=1, device_id=device, device_id_type=MESH)

    greet((region, far_peer))
    for peer, count in ((deep_peer, n_deep), (flat_peer, n_flat)):
        lax.fori_loop(1, count, lambda j, c, peer=peer: (greet(peer(j)), c)[1], 0)

    def lanes(i):
        return slice(LANES * i, LANES * (i + 1))

    for there, here in (
        (conn_y_in, conn_y), (conn_z_in, conn_z), (conn_x_in, conn_x),
        (storage_in, storage), (source_in, source),
    ):
        for i in range(ROWS):
            here[2 * i : 2 * i + 2, :] = there[:, lanes(i)]
    for c in range(2):
        for i in range(ROWS):
            perm[pl.ds(2 * i + c, 3, stride=32), :] = perm_in[c, :, lanes(i)]

    def pair(ref, first=0):
        return [ref[pl.ds(first + k, ROWS, stride=2), :] for k in range(2)]

    by_side = [pair(perm, 32 * d) for d in range(3)]
    trans = [[2.0 * by_side[d][c] for d in range(3)] for c in range(2)]
    store, origin, sigma = pair(storage), pair(source), sigma_ref[...]

    diag = [2.0 * (trans[c][0] + trans[c][1] + trans[c][2]) + store[c] + sigma for c in range(2)]
    determ = diag[0] * diag[1] - sigma * sigma
    solve_00, solve_01, solve_11 = diag[1] / determ, sigma / determ, diag[0] / determ

    def solve(load):
        return (solve_00 * load[0] + solve_01 * load[1], solve_01 * load[0] + solve_11 * load[1])

    def face_load(v):
        return [
            sum(trans[c][d] * (v[c][d][0] + v[c][d][1]) for d in range(3)) for c in range(2)
        ]

    def contributions(v, inner):
        return [
            [[trans[c][d] * (v[c][d][s] - inner[c]) for s in range(2)] for d in range(3)]
            for c in range(2)
        ]

    base = solve(origin)
    rhs_g = [[[trans[c][d] * base[c]] * 2 for d in range(3)] for c in range(2)]

    def at_face(which, face, count=ROWS):
        return lookup(table(itable.at[which], count), face, jnp.full(face.shape, -1, I32))

    zlist[0:1, :] = jnp.full((1, LANES), -1, I32)
    zlist[0:1, 0:64] = send_z[...]
    itable[2] = inverse(conn_y, 0, [(send_y, 4)])
    itable[3] = inverse(conn_y, 1)
    itable[4] = inverse(conn_z, 0, [(zlist, 1)])
    itable[5] = inverse(conn_z, 1)
    up_y_cells = at_face(3, send_y[...])
    down_y_cells = itable[2, ROWS : ROWS + 4, :]
    up_z_cells = at_face(5, zlist[0:1, :])
    down_z_cells = itable[4, ROWS : ROWS + 1, :]

    def by_core(if_upper, if_lower):
        return jnp.where(upper, if_upper, if_lower)

    for c in range(2):
        far_cells[4 * c : 4 * c + 4, :] = by_core(up_y_cells, down_y_cells)
        near_cells[4 * c : 4 * c + 4, :] = by_core(down_y_cells, up_y_cells)
        z_cells[c : c + 1, :] = up_z_cells
        z_cells[2 + c : 3 + c, :] = down_z_cells

    def remote(send, recv, sems, device):
        return pltpu.make_async_remote_copy(
            src_ref=send,
            dst_ref=recv,
            send_sem=sems.at[0],
            recv_sem=sems.at[1],
            device_id=device,
            device_id_type=MESH,
        )

    def copies(step):
        near, along = near_sems.at[step], z_sems.at[step]
        return [
            remote(near_send.at[step], near_recv.at[step], near, (region, near_peer)),
            remote(z_send.at[step, 0], z_recv.at[step, 0], along.at[0], (region_up, sub)),
            remote(z_send.at[step, 1], z_recv.at[step, 1], along.at[1], (region_down, sub)),
        ]

    far_first = remote(
        far_send.at[0, pl.ds(0, 8)], far_recv.at[0, pl.ds(0, 8)], far_sems.at[0], (region, far_peer)
    )
    far_second = remote(far_send.at[1], far_recv.at[1], far_sems.at[1], (region, far_peer))
    far_terms = remote(terms_send, terms_recv, far_sems.at[2], (region, far_peer))

    def side_values(at, cells, pair):
        for c in range(2):
            sides[at + c, 0:ROWS, :] = pair[c]
        second = iota((8, LANES), 0) >= 4
        rows = [
            (h, jnp.where(second, sides[at + 1, h : h + 1, :], sides[at, h : h + 1, :]))
            for h in range(ROWS)
        ]
        return lookup(rows, cells[...])

    def fill_far(step, g):
        pair = [by_core(g[c][1][1], g[c][1][0]) for c in range(2)]
        far_send[step, 0:8, :] = side_values(0, far_cells, pair)

    def fill_near(step, g):
        pair = [by_core(g[c][1][0], g[c][1][1]) for c in range(2)]
        near_send[step] = side_values(2, near_cells, pair)
        for s in range(2):
            for c in range(2):
                sides[4, pl.ds(2 - 2 * s + c, ROWS, stride=4), :] = g[c][2][s]
        rows = [(h, sides[4, 4 * h : 4 * h + 4, :]) for h in range(ROWS)]
        z_rows = lookup(rows, z_cells[0:4, :])
        z_send[step, 0] = z_rows[0:2]
        z_send[step, 1] = z_rows[2:4]

    def start(step):
        for copy in copies(step):
            copy.start()

    def keep(g):
        for d in (1, 2, 0):
            for c in range(2):
                for s in range(2):
                    tables[c * 6 + d * 2 + s] = g[c][d][s]

    greetings = 1 + (n_flat - 1) + (n_deep - 1)
    fill_far(0, rhs_g)
    fill_near(0, rhs_g)
    pl.semaphore_wait(barrier, greetings)
    far_first.start()
    start(0)
    keep(rhs_g)
    terms_send[0:8, :] = side_values(5, far_cells, [trans[c][1] for c in range(2)])
    terms_send[8:16, :] = side_values(7, far_cells, (solve_00, solve_01))
    terms_send[16:24, :] = side_values(9, far_cells, (solve_11, solve_11))
    far_terms.start()

    itable[0] = inverse(conn_x, 0)
    itable[1] = inverse(conn_x, 1)
    faces_x, faces_y, faces_z = pair(conn_x), pair(conn_y), pair(conn_z)
    asked = (faces_x[1], faces_y[1], faces_z[1], faces_x[0], faces_y[0], faces_z[0])
    found = lookup_all([(itable.at[k], face) for k, face in zip((0, 2, 4, 1, 3, 5), asked)], -1)
    up, down = list(found[:3]), list(found[3:])
    up[0] = lookup([(16, itable[0, 16:17, :])], asked[0], up[0])
    down[0] = lookup([(16, itable[1, 16:17, :])], asked[3], down[0])
    down[1] = jnp.where(asked[4] >= E_DEV, asked[4], down[1])
    down[2] = jnp.where(asked[5] >= E_DEV, asked[5], down[2])
    last_z = region == n_region - 1
    up[2] = jnp.where(jnp.logical_and(up[2] >= E_DEV, last_z), -1, up[2])
    first_y = jnp.logical_and(down[1] >= E_DEV, sub == 0)
    first_z = jnp.logical_and(down[2] >= E_DEV, region == 0)
    lone_x = down[0] < 0
    far_index = by_core(up[1], down[1]) - E_DEV
    near_index = by_core(down[1], up[1]) - E_DEV
    at_far = far_index >= 0
    far_index = jnp.where(sub == n_sub - 1, -1, far_index)

    def assemble(step, g, meanwhile=None):
        out = [[[None, None] for _ in range(3)] for _ in range(2)]
        across = lookup_all(
            [(tables.at[k], (up if k % 2 == 0 else down)[k % 6 // 2]) for k in range(12)], 0.0
        )
        for c in range(2):
            for d in range(3):
                at = c * 6 + d * 2
                out[c][d][1] = g[c][d][1] + across[at]
                out[c][d][0] = g[c][d][0] + across[at + 1]
        if meanwhile is not None:
            meanwhile(out)
        for copy in copies(step):
            copy.wait_recv()
        for c in range(2):
            near = lookup(table(near_recv.at[step, pl.ds(4 * c, 4)], 4), near_index)
            out[c][1][1] = out[c][1][1] + by_core(0.0, near)
            out[c][1][0] = out[c][1][0] + by_core(near, 0.0)
            from_below_z = table(z_recv.at[step, 0, pl.ds(c, 1)], 1, ROWS)
            from_above_z = table(z_recv.at[step, 1, pl.ds(c, 1)], 1, ROWS)
            out[c][2][1] = out[c][2][1] + lookup(from_above_z, up[2])
            out[c][2][0] = jnp.where(first_z, 0.0, out[c][2][0] + lookup(from_below_z, down[2]))
        return out

    def add_far(out, rows):
        for c in range(2):
            far = lookup(table(rows.at[pl.ds(4 * c, 4)], 4), far_index)
            out[c][1][1] = out[c][1][1] + by_core(far, 0.0)
            out[c][1][0] = jnp.where(first_y, 0.0, out[c][1][0] + by_core(0.0, far))

    def by_faces(number, v):
        jobs = []
        for c in range(2):
            parts = (v[c][0][0], v[c][0][1], v[c][1][1], v[c][2][1])
            for k, part in enumerate(parts):
                vtables[number, c * 4 + k] = part
                index = (itable[0], itable[1], itable[3, 0:ROWS, :], itable[5, 0:ROWS, :])[k]
                jobs.append((vtables.at[number, c * 4 + k], index))
        found = lookup_all(jobs, 0.0)
        for c in range(2):
            x_low, x_up, y_up, z_up = found[4 * c : 4 * c + 4]
            by_x = jnp.where(itable[1] < 0, x_low, x_up)
            by_face[number, pl.ds(c, 17, stride=2), :] = by_x[0:17]
            by_face[number, pl.ds(34 + c, ROWS, stride=2), :] = y_up
            by_face[number, pl.ds(66 + c, ROWS, stride=2), :] = z_up

    def inner(u, v):
        total = sum(u[c][d][1] * v[c][d][1] for c in range(2) for d in range(3))
        edge = sum(u[c][0][0] * v[c][0][0] for c in range(2))
        return total + jnp.where(lone_x, edge, 0.0)

    def energy(v, load, solved):
        total = sum(
            trans[c][d] * (v[c][d][0] * v[c][d][0] + v[c][d][1] * v[c][d][1])
            for c in range(2)
            for d in range(3)
        )
        return total - (load[0] * solved[0] + load[1] * solved[1])

    stages = ((flat_recv, flat_peer, n_flat), (deep_recv, deep_peer, n_deep))

    def sum_start(k, stage, row):
        recv, peer, count = stages[stage]
        row_send[k, stage, 0:1, :] = row
        recv[k, count - 1 : count, :] = row

        def one(j, carry):
            pltpu.make_async_remote_copy(
                src_ref=row_send.at[k, stage, pl.ds(0, 1)],
                dst_ref=recv.at[k, pl.ds(j - 1, 1)],
                send_sem=sum_sems.at[k, stage, 0],
                recv_sem=sum_sems.at[k, stage, 1],
                device_id=peer(j),
                device_id_type=MESH,
            ).start()
            return carry

        lax.fori_loop(1, count, one, 0)

    def drain(k, stage, which):
        recv, _, count = stages[stage]
        rows = recv.at[k, pl.ds(0, count - 1)]
        pltpu.make_async_copy(rows, rows, sum_sems.at[k, stage, which]).wait()

    def sum_done(k, stage):
        drain(k, stage, 1)
        return jnp.sum(stages[stage][0][k], axis=0, keepdims=True)

    def estimate(rough):
        load = face_load(rough)
        sum_start(0, 0, total_row([inner(rough, rough), energy(rough, load, solve(load))]))

    b = assemble(0, rhs_g, estimate)
    far_first.wait_recv()
    add_far(b, far_recv.at[0])

    load_b = face_load(b)
    inside_b = solve(load_b)
    g_b = contributions(b, inside_b)
    fill_near(1, g_b)
    start(1)
    keep(g_b)
    fill_far(1, g_b)
    sum_start(0, 1, sum_done(0, 0))
    w = assemble(1, g_b)

    def without_far(part, here):
        return jnp.where(jnp.logical_and(at_far, here), 0.0, part)

    apart = [
        [w[c][0], [without_far(w[c][1][0], core == 0), without_far(w[c][1][1], upper)], w[c][2]]
        for c in range(2)
    ]
    far_send[1, 8:16, :] = side_values(0, far_cells, face_load(apart))
    far_second.start()
    by_faces(0, b)
    far_terms.wait_recv()
    far_second.wait_recv()
    add_far(w, far_recv.at[1])

    far_w = far_send[1, 0:8, :] + far_recv[1, 0:8, :]
    far_trans = terms_recv[0:8, :]
    far_load = far_recv[1, 8:16, :] + far_trans * far_w
    load_0, load_1 = far_load[0:4], far_load[4:8]
    term_00, term_01, term_11 = (terms_recv[k : k + 4, :] for k in (8, 12, 16))
    far_next[0:4, :] = far_trans[0:4] * (far_w[0:4] - (term_00 * load_0 + term_01 * load_1))
    far_next[4:8, :] = far_trans[4:8] * (far_w[4:8] - (term_01 * load_0 + term_11 * load_1))

    load_w = face_load(w)
    inside_w = solve(load_w)
    g_w = contributions(w, inside_w)
    fill_near(2, g_w)
    start(2)
    keep(g_w)
    ww = assemble(2, g_w)
    add_far(ww, far_next)

    first = sum_done(0, 1)
    scale = pick(first, 0) / pick(first, 1)

    def blend(u, factor, v):
        return [
            [[u[c][d][s] - factor * v[c][d][s] for s in range(2)] for d in range(3)]
            for c in range(2)
        ]

    r = blend(b, scale, w)
    s = blend(w, scale, ww)
    load = face_load(s)
    parts = [inner(b, b), inner(b, r), inner(r, r), inner(r, s), inner(s, s)]
    sum_start(1, 0, total_row([*parts, energy(s, load, solve(load))]))
    load_ww = face_load(ww)
    inside_ww = solve(load_ww)
    g_ww = contributions(ww, inside_ww)
    sum_start(1, 1, sum_done(1, 0))
    by_faces(1, w)
    by_faces(2, ww)
    for step in range(ROUNDS):
        for copy in copies(step):
            copy.wait_send()
    for copy in (far_first, far_second, far_terms):
        copy.wait_send()
    for k, stage in ((0, 0), (0, 1), (1, 0)):
        drain(k, stage, 0)
    sums = sum_done(1, 1)
    bb, br, rr_, rs_, ss_, sas_ = (pick(sums, k) for k in range(6))

    norm_0 = bb
    near, away = bb / (bb - br), -br / (bb - br)
    tilt = away / scale
    alpha_0 = scale * near
    rr = near * (near * rr_ + away * br)
    bs, bw = (br - rr_) / scale, bb - 2.0 * br + rr_
    rs = near * (near * rs_ + tilt * (br - rr_)) + away * (near * bs + tilt * (bb - br))
    ss = near * near * ss_ + 2.0 * near * tilt * (bs - rs_) + tilt * tilt * bw
    sas = near * near * sas_ + 2.0 * near * tilt * ((bs - rs_) / scale - ss_)
    sas = sas + tilt * tilt * (bw / scale - (bs - rs_))

    beta_0 = rr / norm_0
    alpha_1 = rr / (rs - beta_0 * rr / alpha_0)
    ws = -(rr / alpha_0 + rs) / alpha_0
    norm_2 = -alpha_1 * (rs - alpha_1 * ss - alpha_1 * beta_0 * ws)
    beta_1 = norm_2 / rr
    ratio = alpha_1 * beta_0 / alpha_0
    along = ss - alpha_1 * sas - ratio * (ws - ss)
    energy_2 = -norm_2 / alpha_1 * (1.0 + ratio) - alpha_1 * along
    alpha_2 = norm_2 / (energy_2 - beta_1 * norm_2 / alpha_1)
    on_r = alpha_1 + alpha_2 * (1.0 + beta_1)
    on_s = -alpha_2 * alpha_1
    on_b = alpha_0 + alpha_1 * beta_0 + alpha_2 * beta_1 * beta_0 + on_r
    on_w = -alpha_2 * alpha_1 * beta_0 - alpha_0 * on_r + on_s
    on_ww = -alpha_0 * on_s

    for c in range(2):
        pressure_out[pl.ds(c, ROWS, stride=2), :] = base[c] + (
            on_b * inside_b[c] + on_w * inside_w[c] + on_ww * inside_ww[c]
        )
        for d in range(3):
            for k in range(2):
                flux = on_b * g_b[c][d][k] + on_w * g_w[c][d][k] + on_ww * g_ww[c][d][k]
                flux_out[pl.ds(32 * (2 * d + k) + c, ROWS, stride=2), :] = rhs_g[c][d][k] - flux
    by_face[0] = on_b * by_face[0] + on_w * by_face[1] + on_ww * by_face[2]
    for i in range(49):
        trace_out[:, LANES * i : LANES * (i + 1)] = by_face[0, 2 * i : 2 * i + 2, :]
    drain(1, 1, 0)


def solution(mesh):
    n_region, n_sub = mesh.shape["region"], mesh.shape["sub"]
    n_flat, n_deep = n_sub // 2, 2 * n_region

    def local(conn_x, conn_y, conn_z, send_y, send_z, perm, storage, sigma, source):
        vmem = pl.BlockSpec(memory_space=pltpu.VMEM)
        dma = pltpu.SemaphoreType.DMA
        shapes = (
            jax.ShapeDtypeStruct((2, NXF + 2 * E_DEV), F32),
            jax.ShapeDtypeStruct((2 * ROWS, LANES), F32),
            jax.ShapeDtypeStruct((12 * ROWS, LANES), F32),
        )
        trace, pressure, flux = pl.pallas_call(
            functools.partial(kernel, n_region, n_sub),
            out_shape=shapes,
            in_specs=[vmem] * 9,
            out_specs=(vmem,) * 3,
            scratch_shapes=[
                pltpu.VMEM((2 * ROWS, LANES), I32),
                pltpu.VMEM((2 * ROWS, LANES), I32),
                pltpu.VMEM((2 * ROWS, LANES), I32),
                pltpu.VMEM((6 * ROWS, LANES), F32),
                pltpu.VMEM((2 * ROWS, LANES), F32),
                pltpu.VMEM((2 * ROWS, LANES), F32),
                pltpu.VMEM((8, LANES), I32),
                pltpu.VMEM((6, 24, LANES), I32),
                pltpu.VMEM((12, ROWS, LANES), F32),
                pltpu.VMEM((11, 4 * ROWS, LANES), F32),
                pltpu.VMEM((3, 8, ROWS, LANES), F32),
                pltpu.VMEM((3, 104, LANES), F32),
                pltpu.VMEM((8, LANES), I32),
                pltpu.VMEM((8, LANES), I32),
                pltpu.VMEM((8, LANES), I32),
                pltpu.VMEM((ROUNDS, 8, LANES), F32),
                pltpu.VMEM((ROUNDS, 8, LANES), F32),
                pltpu.VMEM((ROUNDS, 2, 2, LANES), F32),
                pltpu.VMEM((ROUNDS, 2, 2, LANES), F32),
                pltpu.VMEM((2, 16, LANES), F32),
                pltpu.VMEM((2, 16, LANES), F32),
                pltpu.VMEM((24, LANES), F32),
                pltpu.VMEM((24, LANES), F32),
                pltpu.VMEM((8, LANES), F32),
                dma((ROUNDS, 2)),
                dma((ROUNDS, 2, 2)),
                dma((3, 2)),
                pltpu.VMEM((2, 2, 8, LANES), F32),
                pltpu.VMEM((2, n_flat, LANES), F32),
                pltpu.VMEM((2, n_deep, LANES), F32),
                dma((2, 2, 2)),
            ],
            compiler_params=pltpu.CompilerParams(
                collective_id=0, has_side_effects=True, vmem_limit_bytes=32 * 1024 * 1024
            ),
        )(
            conn_x, conn_y, conn_z, send_y.reshape(4, LANES), send_z.reshape(1, 64),
            perm, storage, sigma.reshape(ROWS, LANES), source,
        )
        pressure = pressure.reshape(ROWS, 2, LANES).transpose(1, 0, 2).reshape(2, E_DEV)
        flux = flux.reshape(6, ROWS, 2, LANES).transpose(2, 0, 1, 3).reshape(2, 6, E_DEV)
        return trace, pressure, flux

    both = ("region", "sub")
    return jax.shard_map(
        local,
        mesh=mesh,
        in_specs=(
            P(None, both), P(None, both), P(None, both), P(both), P(both),
            P(None, None, both), P(None, both), P(both), P(None, both),
        ),
        out_specs=(P(None, both), P(None, both), P(None, None, both)),
        check_vma=False,
    )
```
